128 devices in a mesh: dp: 64 (over z, x, y_lo, core), mp: 2 (over y_hi).
Axes of the slice: x: 4, y: 4 (y_hi: 2, y_lo: 2; y = y_hi * 2 + y_lo), z: 4, core: 2. Of those that a mesh axis runs over, the one named last changes fastest.
Arguments:
- code_tokens: int32 [32768], P('dp'), may hold values from 0 to 2047
- segments: int32 [32768], P('dp'), may hold values from 0 to 4, as said below
- layout: int32 [8, 8], replicated, may hold values from 0 to 1, as said below
- durations: int32 [256], P('dp'), may hold values from 2048 to 49149
- overflow: int32 [64], P('dp'), may hold values from 0 to 1, as said below
- upper_context: bfloat16 [32768, 1024], P('dp', 'mp'), may hold values from -6 to 6
- embed_table: bfloat16 [2048, 1024], P(None, 'mp'), may hold values from -6 to 6
- condition_weight: bfloat16 [1024, 1024], P(None, 'mp'), may hold values from -0.1875 to 0.1875
- attention_weight: bfloat16 [4, 1024, 1024], P(None, None, 'mp')
- feedforward_weight: bfloat16 [2, 1024, 4096], P(None, None, 'mp'), may hold values from -0.1875 to 0.1875
- output_table: bfloat16 [1024, 2048], P(None, 'mp')
- norm_gains: float32 [6, 1024], replicated
- embed_master: float32 [2048, 1024], P('dp', 'mp'), may hold values from -6 to 6
- condition_master: float32 [1024, 1024], P('dp', 'mp'), may hold values from -0.1875 to 0.1875
- attention_master: float32 [4, 1024, 1024], P(None, 'dp', 'mp'), may hold values from -0.1875 to 0.1875
- feedforward_master: float32 [2, 1024, 4096], P(None, 'dp', 'mp'), may hold values from -0.1875 to 0.1875
- output_master: float32 [1024, 2048], P('dp', 'mp'), may hold values from -0.1875 to 0.1875
- norms_master: float32 [6, 1024], P(None, 'dp')
- embed_first: float32 [2048, 1024], P('dp', 'mp'), may hold values from -2.2888184e-05 to 2.2888184e-05
- condition_first: float32 [1024, 1024], P('dp', 'mp'), may hold values from -0.00036621094 to 0.00036621094
- attention_first: float32 [4, 1024, 1024], P(None, 'dp', 'mp'), may hold values from -0.00036621094 to 0.00036621094
- feedforward_first: float32 [2, 1024, 4096], P(None, 'dp', 'mp'), may hold values from -0.00036621094 to 0.00036621094
- output_first: float32 [1024, 2048], P('dp', 'mp'), may hold values from -0.00036621094 to 0.00036621094
- norms_first: float32 [6, 1024], P(None, 'dp'), may hold values from -0.0014648438 to 0.0014648438
- embed_second: float32 [2048, 1024], P('dp', 'mp'), may hold values from 4.598491e-11 to 1.8506123e-10
- condition_second: float32 [1024, 1024], P('dp', 'mp'), may hold values from 2.9497638e-09 to 1.1804663e-08
- attention_second: float32 [4, 1024, 1024], P(None, 'dp', 'mp'), may hold values from 2.9497638e-09 to 1.1804663e-08
- feedforward_second: float32 [2, 1024, 4096], P(None, 'dp', 'mp'), may hold values from 2.9497638e-09 to 1.1804663e-08
- output_second: float32 [1024, 2048], P('dp', 'mp'), may hold values from 2.9497638e-09 to 1.1804663e-08
- norms_second: float32 [6, 1024], P(None, 'dp'), may hold values from 4.7106496e-08 to 1.8898677e-07
Outputs:
- loss_sum: float32 [], replicated
- clip_seconds: float32 [], replicated
- gradient_norm: float32 [], replicated
- embed_moment: float32 [2048, 1024], P('dp', 'mp')
- embed_variance: float32 [2048, 1024], P('dp', 'mp')
- embed_updated: float32 [2048, 1024], P('dp', 'mp')
- condition_moment: float32 [1024, 1024], P('dp', 'mp')
- condition_variance: float32 [1024, 1024], P('dp', 'mp')
- condition_updated: float32 [1024, 1024], P('dp', 'mp')
- attention_moment: float32 [4, 1024, 1024], P(None, 'dp', 'mp')
- attention_variance: float32 [4, 1024, 1024], P(None, 'dp', 'mp')
- attention_updated: float32 [4, 1024, 1024], P(None, 'dp', 'mp')
- feedforward_moment: float32 [2, 1024, 4096], P(None, 'dp', 'mp')
- feedforward_variance: float32 [2, 1024, 4096], P(None, 'dp', 'mp')
- feedforward_updated: float32 [2, 1024, 4096], P(None, 'dp', 'mp')
- output_moment: float32 [1024, 2048], P('dp', 'mp')
- output_variance: float32 [1024, 2048], P('dp', 'mp')
- output_updated: float32 [1024, 2048], P('dp', 'mp')
- norms_moment: float32 [6, 1024], P(None, 'dp')
- norms_variance: float32 [6, 1024], P(None, 'dp')
- norms_updated: float32 [6, 1024], P(None, 'dp')
The draws below stay inside these ranges and needn't reach their ends.
Inputs may be any that keep to these rules, and one draw needn't show every extreme that they name: `segments`: within each window the clip numbers never fall, run through 0 to 3 with every clip present, and may be followed by padding marked 4; at least 8 tokens of each window are no padding. `layout`: the diagonal is 1 and entries above it are 0. `overflow`: at least one window is kept (flag 0).
All inputs are finite; a program needn't handle non-finite values.
Results may differ from the reference program's by a relative error of at most 0.015.
Values sent between devices are 32-bit elements; how exact they have to be, the bound alone decides.
No kernel may reach another device: no remote copies, remote signals or barrier semaphores. Data moves between devices by JAX's collectives and lax.ppermute only.
A program may use at most 192 MiB of HBM per device.

```python
import math
import jax
import jax.numpy as jnp
import numpy as np
from jax import lax

D = 1024
HEADS = 16
HEAD_DIM = 64
FF = 4096
VOCAB = 2048
TOK_DEV = 512
BLK = 64
CLIPS_DEV = 4
STEP = 10
TOKENS = 32768
CLIPS = 256
NPARAM = 17831936
N_DP = 64


def norm_table(key):
    ramp = 0.6 + 1.2 * jnp.arange(D, dtype=jnp.float32) / (D - 1)
    noise_draw = jax.random.normal(key, (6, D), jnp.float32)
    gain_rows = jnp.arange(6)[:, None] % 2 == 0
    return jnp.where(gain_rows, ramp[None, :] * (1.0 + 0.1 * noise_draw), 0.2 * noise_draw)


def draw_segments(key, part):
    key = jax.random.fold_in(key, 11)
    devices = TOKENS // TOK_DEV
    spread_count = max(devices - 1, 1)
    device_ids = jnp.arange(devices, dtype=jnp.int32)
    lowest = TOK_DEV // 3
    live_rows = lowest + (TOK_DEV - lowest) * device_ids // spread_count
    key_jitter, key_shift = jax.random.split(key)
    jitter = jax.random.randint(key_jitter, (devices,), 0, TOK_DEV // 8 + 1)
    live_rows = jnp.maximum(live_rows - jitter, 2 * CLIPS_DEV)
    offsets = jax.random.randint(key_shift, (devices,), 0, live_rows)
    position = jnp.arange(TOK_DEV, dtype=jnp.int32)[None, :]
    clip_ids = jnp.minimum((position * CLIPS_DEV + offsets[:, None]) // live_rows[:, None], CLIPS_DEV - 1)
    return jnp.where(position < live_rows[:, None], clip_ids, CLIPS_DEV).reshape(TOKENS).astype(jnp.int32)


def draw_durations(key, part):
    key = jax.random.fold_in(key, 12)
    devices = CLIPS // CLIPS_DEV
    spread_count = max(devices - 1, 1)
    device_ids = jnp.arange(CLIPS, dtype=jnp.int32) // CLIPS_DEV
    base_draw = jax.random.randint(key, (CLIPS,), 2048, 16384)
    return (base_draw * (spread_count + 2 * device_ids) // spread_count).astype(jnp.int32)


def draw_overflow(key, part):
    key = jax.random.fold_in(key, 18)
    devices = CLIPS // CLIPS_DEV
    key_bits, key_order = jax.random.split(key)
    flags = (jax.random.randint(key_bits, (devices,), 0, 8) == 0).astype(jnp.int32)
    order = jax.random.permutation(key_order, devices)
    slots = jnp.arange(devices, dtype=jnp.int32)
    flags = jnp.where(slots == order[0], 0, flags)
    flags = jnp.where(slots == order[1], 1, flags)
    return flags.astype(jnp.int32)


def draw_layout(key, part):
    key = jax.random.fold_in(key, 13)
    blocks = TOK_DEV // BLK
    random_bits = jax.random.randint(key, (blocks, blocks), 0, 2)
    rows_index = jnp.arange(blocks)[:, None]
    cols_index = jnp.arange(blocks)[None, :]
    return jnp.where(rows_index == cols_index, 1, jnp.where(cols_index < rows_index, random_bits, 0)).astype(jnp.int32)


def draw_output_table(key, part):
    key = jax.random.fold_in(key, 14)
    rise_span = 2.0
    noise_draw = jax.random.normal(key, (D, VOCAB), jnp.float32)
    column_scale = 1.0 + rise_span * jnp.arange(VOCAB, dtype=jnp.float32) / (VOCAB - 1)
    return (noise_draw * column_scale[None, :] * D ** (-0.5)).astype(jnp.bfloat16)


def draw_attention_weight(key, part):
    key = jax.random.fold_in(key, 17)
    noise_draw = jax.random.normal(key, (4, D, D), jnp.float32)
    slot_scale = jnp.where(jnp.arange(4) == 3, 4.0, 1.0) * D ** (-0.5)
    return (noise_draw * slot_scale[:, None, None]).astype(jnp.bfloat16)


def draw_norm_gains(key, part):
    key = jax.random.fold_in(key, 15)
    return norm_table(key)


def draw_norms_master(key, part):
    key = jax.random.fold_in(key, 16)
    return norm_table(key)


def touch_ends(entries, own_key, low, largest):
    index_at = [jax.random.randint(jax.random.fold_in(own_key, axis), (), 0, length) for axis, length in enumerate(entries.shape)]
    longest = entries.shape.index(max(entries.shape))
    next_to = index_at[:longest] + [(index_at[longest] + 1) % entries.shape[longest]] + index_at[longest + 1:]
    return entries.at[tuple(index_at)].set(low).at[tuple(next_to)].set(largest)


def levels(rng, extent, cuts, least, high):
    def one(dim, parts):
        draws = jax.random.uniform(jax.random.fold_in(jax.random.fold_in(rng, 6), dim), (parts,), jnp.float32, least / len(cuts), high / len(cuts))
        return jnp.repeat(jnp.exp(draws), extent[dim] // parts).reshape((-1,) + (1,) * (len(extent) - dim - 1))

    factor_of = one(*cuts[0])
    for cut in cuts[1:]:
        factor_of = factor_of * one(*cut)
    return factor_of


def rank_bounds(amount, slope):
    loads = [(1 << 20) // math.isqrt(rank ** slope) + 1 for rank in range(1, amount + 1)]
    spread = 1 + sum(loads) // (1 << 30)
    return np.cumsum(np.array([max(1, weight // spread) for weight in loads]))


def ranked_ids(stream_key, shape, count, skew):
    listing = rank_bounds(count, skew)
    lot = jax.random.randint(jax.random.fold_in(stream_key, 1), shape, 0, int(listing[count - 1]))
    standing = jnp.searchsorted(jnp.asarray(listing, jnp.int32), lot, side="right")
    return jax.random.permutation(jax.random.fold_in(stream_key, 2), count)[standing].astype(jnp.int32)


def bell_draw(rng, extent, scale, most, cuts=(), held_as=jnp.bfloat16):
    factor_of = levels(rng, extent, cuts, -0.22, 0.18) if cuts else 1.0
    entries = jax.random.normal(rng, extent, jnp.float32) * scale * factor_of
    return jnp.minimum(jnp.maximum(entries, -most), most).astype(held_as)


def setup_inputs(seed: int = 0) -> dict:
    key_of = jax.random.split(jax.random.key(seed), 31)
    code_tokens = touch_ends(ranked_ids(key_of[0], (TOKENS,), VOCAB, 1), jax.random.fold_in(key_of[0], 3), 0, VOCAB - 1).astype(jnp.int32)
    segments = draw_segments(jax.random.fold_in(key_of[30], 71), 0)
    layout = draw_layout(jax.random.fold_in(key_of[30], 71), 0)
    durations = draw_durations(jax.random.fold_in(key_of[30], 71), 0)
    overflow = draw_overflow(jax.random.fold_in(key_of[30], 71), 0)
    upper_context = bell_draw(key_of[5], (TOKENS, D), 1.0, 6.0, ((0, 64), (1, 2)))
    embed_table = bell_draw(key_of[6], (VOCAB, D), 1.0, 6.0, ((1, 2),))
    condition_weight = bell_draw(key_of[7], (D, D), D ** -0.5, 0.1875, ((1, 2),))
    attention_weight = draw_attention_weight(jax.random.fold_in(key_of[30], 71), 0)
    feedforward_weight = bell_draw(key_of[9], (2, D, FF), D ** -0.5, 0.1875, ((2, 2),))
    output_table = draw_output_table(jax.random.fold_in(key_of[30], 71), 0)
    norm_gains = draw_norm_gains(jax.random.fold_in(key_of[30], 71), 0)
    embed_master = bell_draw(key_of[12], (VOCAB, D), 1.0, 6.0, ((0, 64), (1, 2)), jnp.float32)
    condition_master = bell_draw(key_of[13], (D, D), D ** -0.5, 0.1875, ((0, 64), (1, 2)), jnp.float32)
    attention_master = bell_draw(key_of[14], (4, D, D), D ** -0.5, 0.1875, ((1, 64), (2, 2)), jnp.float32)
    feedforward_master = bell_draw(key_of[15], (2, D, FF), D ** -0.5, 0.1875, ((1, 64), (2, 2)), jnp.float32)
    output_master = bell_draw(key_of[16], (D, VOCAB), D ** -0.5, 0.1875, ((0, 64), (1, 2)), jnp.float32)
    norms_master = draw_norms_master(jax.random.fold_in(key_of[30], 71), 0)
    embed_first = bell_draw(key_of[18], (VOCAB, D), (0.0069 / NPARAM ** 0.5), 2.288818359375e-05, ((0, 64), (1, 2)), jnp.float32)
    condition_first = bell_draw(key_of[19], (D, D), (0.111 / NPARAM ** 0.5), 0.00036621094, ((0, 64), (1, 2)), jnp.float32)
    attention_first = bell_draw(key_of[20], (4, D, D), (0.111 / NPARAM ** 0.5), 0.00036621094, ((1, 64), (2, 2)), jnp.float32)
    feedforward_first = bell_draw(key_of[21], (2, D, FF), (0.111 / NPARAM ** 0.5), 0.00036621094, ((1, 64), (2, 2)), jnp.float32)
    output_first = bell_draw(key_of[22], (D, VOCAB), (0.111 / NPARAM ** 0.5), 0.00036621094, ((0, 64), (1, 2)), jnp.float32)
    norms_first = bell_draw(key_of[23], (6, D), (0.444 / NPARAM ** 0.5), 0.0014648438, ((1, 64),), jnp.float32)
    embed_second = jnp.clip(jnp.exp(math.log(1.850612302289889e-10) - 1.3923734 * jax.random.uniform(key_of[24], (VOCAB, D), jnp.float32) ** levels(key_of[24], (VOCAB, D), ((0, 64), (1, 2)), -0.2, 0.2)), 4.598491032403729e-11, 1.850612302289889e-10)
    condition_second = jnp.clip(jnp.exp(math.log(1.1804663024861384e-08) - 1.3867695 * jax.random.uniform(key_of[25], (D, D), jnp.float32) ** levels(key_of[25], (D, D), ((0, 64), (1, 2)), -0.2, 0.2)), 2.9497637665798493e-09, 1.1804663024861384e-08)
    attention_second = jnp.clip(jnp.exp(math.log(1.1804663024861384e-08) - 1.3867695 * jax.random.uniform(key_of[26], (4, D, D), jnp.float32) ** levels(key_of[26], (4, D, D), ((1, 64), (2, 2)), -0.2, 0.2)), 2.9497637665798493e-09, 1.1804663024861384e-08)
    feedforward_second = jnp.clip(jnp.exp(math.log(1.1804663024861384e-08) - 1.3867695 * jax.random.uniform(key_of[27], (2, D, FF), jnp.float32) ** levels(key_of[27], (2, D, FF), ((1, 64), (2, 2)), -0.2, 0.2)), 2.9497637665798493e-09, 1.1804663024861384e-08)
    output_second = jnp.clip(jnp.exp(math.log(1.1804663024861384e-08) - 1.3867695 * jax.random.uniform(key_of[28], (D, VOCAB), jnp.float32) ** levels(key_of[28], (D, VOCAB), ((0, 64), (1, 2)), -0.2, 0.2)), 2.9497637665798493e-09, 1.1804663024861384e-08)
    norms_second = jnp.clip(jnp.exp(math.log(1.8898677467404923e-07) - 1.3892661 * jax.random.uniform(key_of[29], (6, D), jnp.float32) ** levels(key_of[29], (6, D), ((1, 64),), -0.2, 0.2)), 4.710649648131948e-08, 1.8898677467404923e-07)
    return {"code_tokens": code_tokens, "segments": segments, "layout": layout, "durations": durations, "overflow": overflow, "upper_context": upper_context, "embed_table": embed_table, "condition_weight": condition_weight, "attention_weight": attention_weight, "feedforward_weight": feedforward_weight, "output_table": output_table, "norm_gains": norm_gains, "embed_master": embed_master, "condition_master": condition_master, "attention_master": attention_master, "feedforward_master": feedforward_master, "output_master": output_master, "norms_master": norms_master, "embed_first": embed_first, "condition_first": condition_first, "attention_first": attention_first, "feedforward_first": feedforward_first, "output_first": output_first, "norms_first": norms_first, "embed_second": embed_second, "condition_second": condition_second, "attention_second": attention_second, "feedforward_second": feedforward_second, "output_second": output_second, "norms_second": norms_second}


@jax.custom_vjp
def low(v):
    return lax.optimization_barrier(v.astype(jnp.bfloat16)).astype(jnp.float32)

@jax.custom_vjp
def low_back(v):
    return v

def low_keep(v):
    return (low(v), None)

def low_pass(kept, grad):
    return (grad,)

def back_keep(v):
    return (v, None)

def back_low(kept, grad):
    return (low(grad),)
low.defvjp(low_keep, low_pass)
low_back.defvjp(back_keep, back_low)
LAYER_EPS = 1e-05
SAMPLE_RATE = 44100.0
LOG_TWO_NATS = 0.6931471805599453
CLIP_NORM = 1.0
BETA_FIRST = 0.9
BETA_SECOND = 0.95
ADAM_EPSILON = 1e-08
WEIGHT_DECAY = 0.01
RATE_MATRIX = 0.1
RATE_TABLE = 1.0
RATE_NORMS = 1.0
HIGHEST = lax.Precision.HIGHEST

def matmul(left_side, right_side):
    return jnp.dot(left_side, right_side, precision=HIGHEST)

def norm_rows(values, gain_row, shift_row):
    average = lax.optimization_barrier(jnp.mean(values, axis=-1, keepdims=True))
    centred = values - average
    variance = lax.optimization_barrier(jnp.mean(centred * centred, axis=-1, keepdims=True))
    return centred * lax.rsqrt(variance + LAYER_EPS) * gain_row + shift_row

def allowed_mask(segments, layout):
    length = segments.shape[0]
    position = jnp.arange(length)
    blocks = layout.shape[0]
    block_open = jnp.broadcast_to(layout[:, None, :, None], (blocks, BLK, blocks, BLK)).reshape(length, length) > 0
    causal = position[None, :] <= position[:, None]
    return causal & (segments[:, None] == segments[None, :]) & block_open

def window_loss(params, code_tokens, segments, layout, context, keep_flag):
    embed_table, condition_weight, attention_weight, feedforward_weight, output_table, norm_gains = params
    length = code_tokens.shape[0]
    condition_branch = low_back(matmul(context, condition_weight.T))
    residual = embed_table[code_tokens] + condition_branch
    normed_one = low(norm_rows(residual, norm_gains[0], norm_gains[1]))
    projected = [low_back(low(matmul(normed_one, attention_weight[index_slot]))).reshape(length, HEADS, HEAD_DIM) for index_slot in range(3)]
    scores = low_back(jnp.einsum('qhd,khd->hqk', projected[0], projected[1], precision=HIGHEST) * HEAD_DIM ** (-0.5))
    masked = jnp.where(allowed_mask(segments, layout)[None], scores, -1e+30)
    row_top = lax.optimization_barrier(jnp.max(masked, axis=-1, keepdims=True))
    exponents = jnp.exp(masked - row_top)
    attend = low(exponents / lax.optimization_barrier(jnp.sum(exponents, axis=-1, keepdims=True)))
    mixed = jnp.einsum('hqk,khd->qhd', attend, projected[2], precision=HIGHEST).reshape(length, D)
    mixed = low_back(low(mixed))
    residual = residual + low_back(matmul(mixed, attention_weight[3].T))
    normed_two = low(norm_rows(residual, norm_gains[2], norm_gains[3]))
    pre_act = low_back(matmul(normed_two, feedforward_weight[0]))
    activated = low(jax.nn.gelu(pre_act))
    residual = residual + low_back(matmul(activated, feedforward_weight[1].T))
    normed_three = low(norm_rows(residual, norm_gains[4], norm_gains[5]))
    logits = low_back(matmul(normed_three, output_table))
    logit_top = lax.optimization_barrier(jnp.max(logits, axis=1, keepdims=True))
    log_norm = logit_top[:, 0] + jnp.log(lax.optimization_barrier(jnp.sum(jnp.exp(logits - logit_top), axis=1)))
    targets = jnp.concatenate([code_tokens[1:], code_tokens[-1:]])
    picked = jnp.take_along_axis(logits, targets[:, None], axis=1)[:, 0]
    next_segment = jnp.concatenate([segments[1:], jnp.full((1,), -1, jnp.int32)])
    counted = ((segments == next_segment) & (segments < CLIPS_DEV)).astype(jnp.float32) * keep_flag
    return jnp.sum(counted * (log_norm - picked)) / LOG_TWO_NATS

def adam_step(gradient, master, first_old, second_old, step_rate, decay_rate):
    moment = BETA_FIRST * first_old + (1.0 - BETA_FIRST) * gradient
    variance = BETA_SECOND * second_old + (1.0 - BETA_SECOND) * gradient * gradient
    moment_hat = moment / (1.0 - BETA_FIRST ** STEP)
    variance_hat = variance / (1.0 - BETA_SECOND ** STEP)
    updated = master - step_rate * (moment_hat / (jnp.sqrt(variance_hat) + ADAM_EPSILON) + decay_rate * master)
    return (moment, variance, updated)

def reference(code_tokens, segments, layout, durations, overflow, upper_context, embed_table, condition_weight, attention_weight, feedforward_weight, output_table, norm_gains, embed_master, condition_master, attention_master, feedforward_master, output_master, norms_master, embed_first, condition_first, attention_first, feedforward_first, output_first, norms_first, embed_second, condition_second, attention_second, feedforward_second, output_second, norms_second):
    weights = (embed_table, condition_weight, attention_weight, feedforward_weight, output_table, norm_gains)
    params = tuple((weight.astype(jnp.float32) for weight in weights))
    keep_all = 1.0 - overflow.astype(jnp.float32)
    windows = (code_tokens.reshape(N_DP, TOK_DEV), segments.reshape(N_DP, TOK_DEV), upper_context.astype(jnp.float32).reshape(N_DP, TOK_DEV, D), keep_all)

    def window_step(running, inputs):
        codes_here, segments_here, context_here, keep_here = inputs

        def loss_of(params_here):
            return window_loss(params_here, codes_here, segments_here, layout, context_here, keep_here)
        loss_here, pullback = jax.vjp(loss_of, params)
        gradients = pullback(jnp.ones((), jnp.float32))[0]
        summed = jax.tree.map(jnp.add, running[0], gradients)
        return ((summed, running[1] + loss_here), None)
    zero_grads = jax.tree.map(jnp.zeros_like, params)
    (grad_sums, loss_sum), _ = lax.scan(window_step, (zero_grads, jnp.zeros((), jnp.float32)), windows)
    clip_seconds = jnp.sum(durations.astype(jnp.float32) * jnp.repeat(keep_all, CLIPS_DEV)) / SAMPLE_RATE
    scaled = tuple((gradient / clip_seconds for gradient in grad_sums))
    gradient_norm = jnp.sqrt(sum((jnp.sum(gradient * gradient) for gradient in scaled)))
    clip_factor = CLIP_NORM / jnp.maximum(gradient_norm, CLIP_NORM)
    masters = (embed_master, condition_master, attention_master, feedforward_master, output_master, norms_master)
    firsts = (embed_first, condition_first, attention_first, feedforward_first, output_first, norms_first)
    seconds_old = (embed_second, condition_second, attention_second, feedforward_second, output_second, norms_second)
    rates = (RATE_TABLE, RATE_MATRIX, RATE_MATRIX, RATE_MATRIX, RATE_MATRIX, RATE_NORMS)
    decays = (WEIGHT_DECAY, WEIGHT_DECAY, WEIGHT_DECAY, WEIGHT_DECAY, WEIGHT_DECAY, 0.0)
    updates = [adam_step(scaled[index_slot] * clip_factor, masters[index_slot], firsts[index_slot], seconds_old[index_slot], rates[index_slot], decays[index_slot]) for index_slot in range(6)]
    return (loss_sum, clip_seconds, gradient_norm, updates[0][0], updates[0][1], updates[0][2], updates[1][0], updates[1][1], updates[1][2], updates[2][0], updates[2][1], updates[2][2], updates[3][0], updates[3][1], updates[3][2], updates[4][0], updates[4][1], updates[4][2], updates[5][0], updates[5][1], updates[5][2])
```

```python
import functools

import jax
import jax.numpy as jnp
import numpy as np
from jax import lax
from jax.experimental import pallas as pl
from jax.experimental.pallas import tpu as pltpu
from jax.sharding import Mesh
from jax.sharding import PartitionSpec as P

HEAD_DIM = 64
BLK = 64
CLIPS_DEV = 4
STEP = 10


LAYER_EPS = 1e-05
SAMPLE_RATE = 44100.0
LOG_TWO_NATS = 0.6931471805599453
CLIP_NORM = 1.0
BETA_FIRST = 0.9
BETA_SECOND = 0.95
ADAM_EPSILON = 1e-08
WEIGHT_DECAY = 0.01
RATE_MATRIX = 0.1
RATE_TABLE = 1.0
RATE_NORMS = 1.0
SQUARE_SCALE = 2.0**-9

AXES = ("z", "x", "yl", "c", "yh")
SIZES = (4, 4, 2, 2, 2)
DP = ("z", "x", "yl", "c")
VMEM_LIMIT = 48 * 1024 * 1024
BF16 = jnp.bfloat16
F32 = jnp.float32


def send(value, move):
    pairs = []
    for index in range(int(np.prod(SIZES))):
        z, x, yl, c, yh = (int(i) for i in np.unravel_index(index, SIZES))
        z, x, y, c = move(z, x, yh * 2 + yl, c)
        y %= 4
        pairs.append((index, int(np.ravel_multi_index((z % 4, x % 4, y % 2, c, y // 2), SIZES))))
    return lax.ppermute(value, AXES, pairs)


def swap_core(value):
    return send(value, lambda z, x, y, c: (z, x, y, 1 - c))


def pair_sum(value):
    return value + swap_core(value)


def ring(axis):
    def move(z, x, y, c):
        step = 1 - 2 * c
        return {"z": (z + step, x, y, c), "x": (z, x + step, y, c), "y": (z, x, y + step, c)}[axis]

    return move


def by(axis, count):
    def move(z, x, y, c):
        return {"z": (z + count, x, y, c), "x": (z, x + count, y, c), "y": (z, x, y + count, c)}[axis]

    return move


def flipped(axis, bit):
    def move(z, x, y, c):
        return {"z": (z ^ bit, x, y, c), "x": (z, x ^ bit, y, c), "y": (z, x, y ^ bit, c)}[axis]

    return move


def place_kernel(outer_stride, inner_stride, s_ref, native_ref, b0, b1, b2, b3, out_ref):
    width = native_ref.shape[-1]
    out_ref[0, :, :width] = native_ref[0]
    outer, inner, sign = s_ref[0], s_ref[1], s_ref[2]
    for j, buf in enumerate((b0, b1, b2, b3)):
        outer_at = lax.rem(outer - sign * j + 8, 4)
        for i in range(4):
            inner_at = lax.rem(inner - sign * i + 8, 4)
            row = pl.multiple_of(outer_at * outer_stride + inner_at * inner_stride, 64)
            out_ref[0, pl.ds(row, 64), width:] = buf[i, 0].astype(BF16)


def place(native, first_slot, slots, buffers, scalars, outer_stride, inner_stride):
    rows, width = native.shape[1], native.shape[2] // 2
    block = pl.BlockSpec((4, 1, 64, width), lambda k, s: (0, k, 0, 0))
    return pl.pallas_call(
        functools.partial(place_kernel, outer_stride, inner_stride),
        grid_spec=pltpu.PrefetchScalarGridSpec(
            num_scalar_prefetch=1,
            grid=(slots,),
            in_specs=[pl.BlockSpec((1, rows, width), lambda k, s: (first_slot + k, 0, s[3]))]
            + [block] * 4,
            out_specs=pl.BlockSpec((1, rows, 2 * width), lambda k, s: (k, 0, 0)),
        ),
        out_shape=jax.ShapeDtypeStruct((slots, rows, 2 * width), BF16),
        compiler_params=pltpu.CompilerParams(vmem_limit_bytes=VMEM_LIMIT),
        cost_estimate=pl.CostEstimate(
            flops=0, bytes_accessed=slots * rows * width * 10, transcendentals=0
        ),
    )(scalars, native, *buffers)


def place_halves_kernel(s_ref, native_ref, near_ref, far_ref, out_ref):
    half, width = near_ref.shape
    out_ref[:, :width] = native_ref[...]
    near = s_ref[4]
    out_ref[pl.ds(pl.multiple_of(near * half, 64), half), width:] = near_ref[...].astype(BF16)
    out_ref[pl.ds(pl.multiple_of((1 - near) * half, 64), half), width:] = far_ref[...].astype(BF16)


def place_halves(native, near, far, scalars):
    rows, width = native.shape[0], native.shape[1] // 2
    whole = pl.BlockSpec((rows // 2, width), lambda k, s: (0, 0))
    return pl.pallas_call(
        place_halves_kernel,
        grid_spec=pltpu.PrefetchScalarGridSpec(
            num_scalar_prefetch=1,
            grid=(1,),
            in_specs=[pl.BlockSpec((rows, width), lambda k, s: (0, s[3])), whole, whole],
            out_specs=pl.BlockSpec((rows, 2 * width), lambda k, s: (0, 0)),
        ),
        out_shape=jax.ShapeDtypeStruct((rows, 2 * width), BF16),
        compiler_params=pltpu.CompilerParams(vmem_limit_bytes=VMEM_LIMIT),
        cost_estimate=pl.CostEstimate(
            flops=0, bytes_accessed=rows * width * 10, transcendentals=0
        ),
    )(scalars, native, near, far)


def own_quarter(half, core):
    width = half.shape[-1] // 2
    return jnp.where(core == 0, half[..., :width], half[..., width:])


def row_block(native, core, block):
    slots, rows, width = native.shape
    view = native.reshape(slots, rows // 64, 64, width)
    rows_here = lax.dynamic_slice_in_dim(view, block, 1, 1)[:, 0]
    return own_quarter(rows_here, core).astype(F32)


def gathered(piece, first_axis, second_axis):
    pieces = [piece]
    for _ in range(3):
        pieces.append(send(pieces[-1], ring(first_axis)))
    buffers = [jnp.stack(pieces)]
    for _ in range(3):
        buffers.append(send(buffers[-1], ring(second_axis)))
    return buffers


def chunk_kernel(mode, has_recv, s_ref, lhs_ref, rhs_ref, *rest):
    out_ref = rest[-1]
    rhs = rhs_ref[...].reshape(rhs_ref.shape[-2:])
    rows, width = out_ref.shape[-2:]
    if mode == "hot":
        row_id = lax.broadcasted_iota(jnp.int32, (rows, rhs.shape[0]), 0)
        code = ((row_id // 128) * 4 + s_ref[0]) * 128 + lax.rem(row_id, 128)
        lhs = (code == lhs_ref[...]).astype(F32).astype(BF16)
        high = rhs.astype(BF16)
        low = (rhs - high.astype(F32)).astype(BF16)
        total = jnp.dot(lhs, high, preferred_element_type=F32)
        total += jnp.dot(lhs, low, preferred_element_type=F32)
    else:
        lhs = lhs_ref[...].reshape(rows, lhs_ref.shape[-1])
        total = jnp.dot(lhs, rhs, preferred_element_type=F32)
    total = total.reshape(out_ref.shape)
    if has_recv:
        total += rest[0][...]
    out_ref[...] = total


def chunk_product(order, lhs, rhs, rhs_spec, rows, width, tile, scalars, recv, hot=False):
    tokens = 512
    steps = width // tile
    if hot:
        lhs_spec = pl.BlockSpec((1, tokens), lambda *g: (0, 0))
    elif order == "x":
        lhs = lhs.reshape(4, 4, 64, tokens)
        lhs_spec = pl.BlockSpec((4, 1, 64, tokens), lambda *g: (0, g[-1][0], 0, 0))
    elif order == "z":
        lhs = lhs.reshape(4, 256, tokens)
        lhs_spec = pl.BlockSpec((1, 256, tokens), lambda *g: (g[-1][0], 0, 0))
    else:
        lhs = lhs.reshape(16, 2, 32, tokens)
        lhs_spec = pl.BlockSpec((16, 1, 32, tokens), lambda *g: (0, g[-1][0], 0, 0))
    if order == "y":
        grid = (steps,)
        out_spec = pl.BlockSpec((rows, tile), lambda j, s: (0, j))
        out_shape = jax.ShapeDtypeStruct((rows, width), F32)
        halves = 1
    else:
        grid = (2, steps)
        out_spec = pl.BlockSpec((1, rows, tile), lambda h, j, s: (h, 0, j))
        out_shape = jax.ShapeDtypeStruct((2, rows, width), F32)
        halves = 2
    operands = [lhs, rhs] + ([] if recv is None else [recv])
    in_specs = [lhs_spec, rhs_spec] + ([] if recv is None else [out_spec])
    moved = halves * rows * width * 4
    return pl.pallas_call(
        functools.partial(chunk_kernel, "hot" if hot else "plain", recv is not None),
        grid_spec=pltpu.PrefetchScalarGridSpec(
            num_scalar_prefetch=1, grid=grid, in_specs=in_specs, out_specs=out_spec
        ),
        out_shape=out_shape,
        compiler_params=pltpu.CompilerParams(vmem_limit_bytes=VMEM_LIMIT),
        cost_estimate=pl.CostEstimate(
            flops=2 * tokens * halves * rows * width,
            bytes_accessed=moved * (1 if recv is None else 2),
            transcendentals=0,
        ),
    )(scalars, *operands)


def ring_scatter(axis, place_at, sign, make):
    total = make(lax.rem(place_at - sign + 8, 4), None)
    for k in range(2, 5):
        total = make(lax.rem(place_at - k * sign + 8, 4), send(total, ring(axis)))
    return total


def added(part, arrived):
    return part if arrived is None else part + arrived


class Spot:
    def __init__(self):
        self.z, self.x, self.yl, self.c, self.yh = (lax.axis_index(a) for a in AXES)
        self.y = self.yh * 2 + self.yl
        self.sign = 1 - 2 * self.c


def reduce_rows(order, spot, lhs, rhs, block, rhs_at, width, tile, per_device=16, hot=False):
    pair = 2 * per_device

    def product(chunk, half, arrived):
        scalars = jnp.stack([chunk, half, spot.c, spot.yh]).astype(jnp.int32)
        rows = pair * (16 if order == "y" else 8)
        if order == "y":
            spec = pl.BlockSpec(block, lambda j, s: rhs_at(s[1], j, s))
        else:
            spec = pl.BlockSpec(block, lambda h, j, s: rhs_at(h, j, s))
        return chunk_product(order, lhs, rhs, spec, rows, width, tile, scalars, arrived, hot)

    def half_of(y):
        return lax.rem(y // 2 + spot.yh, 2)

    if order == "x":
        first = ring_scatter("x", spot.x, spot.sign, lambda k, a: product(k, spot.c, a))
        first = first.reshape(2, 4, 2, pair, width)
        second = ring_scatter(
            "y",
            spot.y,
            spot.sign,
            lambda k, a: added(
                lax.dynamic_slice(
                    first, (half_of(k), 0, lax.rem(k, 2), 0, 0), (1, 4, 1, pair, width)
                ).reshape(4, pair, width),
                a,
            ),
        )
        third = ring_scatter(
            "z", spot.z, spot.sign, lambda k, a: added(lax.dynamic_index_in_dim(second, k, 0, False), a)
        )
    elif order == "z":
        first = ring_scatter("z", spot.z, spot.sign, lambda k, a: product(k, spot.c, a))
        first = first.reshape(2, 4, 2, pair, width)
        second = ring_scatter(
            "x", spot.x, spot.sign, lambda k, a: added(lax.dynamic_index_in_dim(first, k, 1, False), a)
        )
        third = ring_scatter(
            "y",
            spot.y,
            spot.sign,
            lambda k, a: added(
                lax.dynamic_slice(
                    second, (half_of(k), lax.rem(k, 2), 0, 0), (1, 1, pair, width)
                ).reshape(pair, width),
                a,
            ),
        )
    else:
        first = ring_scatter(
            "y", spot.y, spot.sign, lambda k, a: product(lax.rem(k, 2), half_of(k), a)
        )
        first = first.reshape(4, 4, pair, width)
        second = ring_scatter(
            "z", spot.z, spot.sign, lambda k, a: added(lax.dynamic_index_in_dim(first, k, 0, False), a)
        )
        third = ring_scatter(
            "x", spot.x, spot.sign, lambda k, a: added(lax.dynamic_index_in_dim(second, k, 0, False), a)
        )
    return third


def sum_of_four(value, axis, place_at):
    pieces = [value] + [send(value, by(axis, k)) for k in (1, 2, 3)]
    total = None
    for at in range(4):
        back = lax.rem(place_at - at + 4, 4)
        part = pieces[3]
        for k in (2, 1, 0):
            part = jnp.where(back == k, pieces[k], part)
        total = part if total is None else total + part
    return total


def contract(left_side, right_side, left_dim, right_dim):
    return lax.dot_general(
        left_side,
        right_side,
        (((left_dim,), (right_dim,)), ((), ())),
        preferred_element_type=jnp.float32,
    )


def norm_rows(values, gain_row, shift_row):
    average = jnp.mean(values, axis=-1, keepdims=True)
    centred = values - average
    variance = jnp.mean(centred * centred, axis=-1, keepdims=True)
    return centred * lax.rsqrt(variance + LAYER_EPS) * gain_row + shift_row


def allowed_mask(segments, layout):
    length = segments.shape[0]
    position = jnp.arange(length)
    blocks = layout.shape[0]
    block_open = (
        jnp.broadcast_to(layout[:, None, :, None], (blocks, BLK, blocks, BLK)).reshape(
            length, length
        )
        > 0
    )
    causal = position[None, :] <= position[:, None]
    return causal & (segments[:, None] == segments[None, :]) & block_open


def masked_scores(queries, keys_low, allowed):
    scores = jnp.einsum(
        "qhd,khd->hqk", queries, keys_low, preferred_element_type=jnp.float32
    ) * HEAD_DIM ** (-0.5)
    return jnp.where(allowed[None], scores, -1e30)


def layer_forward(residual, project_weight, mix_weight, up_weight, down_weight, norm_gains, allowed):
    length = residual.shape[0]
    heads_local = project_weight.shape[2] // HEAD_DIM
    normed_one = norm_rows(residual, norm_gains[0], norm_gains[1]).astype(jnp.bfloat16)
    projected = jnp.einsum(
        "td,sde->ste", normed_one, project_weight, preferred_element_type=jnp.float32
    ).astype(jnp.bfloat16)
    heads_view = projected.reshape(3, length, heads_local, HEAD_DIM)
    masked = masked_scores(heads_view[0], heads_view[1], allowed)
    row_top = jnp.max(masked, axis=-1, keepdims=True)
    exponents = jnp.exp(masked - row_top)
    row_sums = jnp.sum(exponents, axis=-1, keepdims=True)
    attend_low = (exponents / row_sums).astype(jnp.bfloat16)
    log_total = row_top + jnp.log(row_sums)
    mixed_low = (
        jnp.einsum("hqk,khd->qhd", attend_low, heads_view[2], preferred_element_type=jnp.float32)
        .astype(jnp.bfloat16)
        .reshape(length, -1)
    )
    after_attention = residual + pair_sum(contract(mixed_low, mix_weight, 1, 1))
    normed_two = norm_rows(after_attention, norm_gains[2], norm_gains[3]).astype(jnp.bfloat16)
    pre_act = jnp.dot(normed_two, up_weight, preferred_element_type=jnp.float32)
    activated = jax.nn.gelu(pre_act).astype(jnp.bfloat16)
    after_block = after_attention + pair_sum(contract(activated, down_weight, 1, 1))
    saved_state = (
        residual,
        normed_one,
        heads_view,
        log_total,
        mixed_low,
        after_attention,
        normed_two,
        pre_act,
        activated,
    )
    return (after_block, saved_state)


def head_loss(after_block, output_table, norm_gains, code_tokens, segments, keep_flag, spot):
    normed_three = norm_rows(after_block, norm_gains[4], norm_gains[5]).astype(jnp.bfloat16)
    logits = jnp.dot(normed_three, output_table, preferred_element_type=jnp.float32)
    width = output_table.shape[1]
    quarter = width // 2
    targets = jnp.concatenate([code_tokens[1:], code_tokens[-1:]])
    column = jnp.arange(width)
    code = jnp.where(
        column < quarter,
        spot.yh * width + spot.c * quarter + column,
        (1 - spot.yh) * width + spot.c * quarter + column - quarter,
    )
    target_hit = code[None, :] == targets[:, None]
    row_top = jnp.max(logits, axis=1)
    row_sums = jnp.sum(jnp.exp(logits - row_top[:, None]), axis=1)
    picked = jnp.sum(jnp.where(target_hit, logits, 0.0), axis=1)
    other = swap_core(jnp.stack([row_top, row_sums, picked]))
    both_top = jnp.maximum(row_top, other[0])
    both_sums = row_sums * jnp.exp(row_top - both_top) + other[1] * jnp.exp(other[0] - both_top)
    log_norm = both_top + jnp.log(both_sums)
    next_segment = jnp.concatenate([segments[1:], jnp.full((1,), -1, jnp.int32)])
    counted = ((segments == next_segment) & (segments < CLIPS_DEV)).astype(jnp.float32) * keep_flag
    loss_local = jnp.sum(counted * (log_norm - (picked + other[2]))) / LOG_TWO_NATS
    grad_logits = (counted / LOG_TWO_NATS)[:, None] * (
        jnp.exp(logits - log_norm[:, None]) - target_hit.astype(jnp.float32)
    )
    grad_low = grad_logits.astype(jnp.bfloat16)
    grad_normed = pair_sum(contract(grad_low, output_table, 1, 1))
    _, pullback = jax.vjp(norm_rows, after_block, norm_gains[4], norm_gains[5])
    grad_input, grad_gain, grad_shift = pullback(grad_normed)
    return (loss_local, grad_input, normed_three, grad_low, (grad_gain, grad_shift))


def feedforward_backward(grad_block, saved_state, up_weight, down_weight, norm_gains):
    after_attention, normed_two, pre_act, activated = saved_state[5:]
    branch_low = grad_block.astype(jnp.bfloat16)
    grad_activated = jnp.dot(branch_low, down_weight, preferred_element_type=jnp.float32)
    _, gelu_pull = jax.vjp(jax.nn.gelu, pre_act)
    grad_pre = gelu_pull(grad_activated)[0].astype(jnp.bfloat16)
    grad_normed = pair_sum(contract(grad_pre, up_weight, 1, 1))
    _, pullback = jax.vjp(norm_rows, after_attention, norm_gains[2], norm_gains[3])
    grad_input, grad_gain, grad_shift = pullback(grad_normed)
    return (grad_block + grad_input, branch_low, grad_pre, (grad_gain, grad_shift))


def attention_backward(grad_attention, saved_state, project_weight, mix_weight, norm_gains, allowed):
    residual, normed_one, heads_view, log_total, mixed_low = saved_state[:5]
    length = residual.shape[0]
    heads_local = heads_view.shape[2]
    branch_low = grad_attention.astype(jnp.bfloat16)
    grad_mixed = (
        jnp.dot(branch_low, mix_weight, preferred_element_type=jnp.float32)
        .astype(jnp.bfloat16)
        .reshape(length, heads_local, HEAD_DIM)
    )
    masked = masked_scores(heads_view[0], heads_view[1], allowed)
    attend_full = jnp.exp(masked - log_total)
    attend_low = attend_full.astype(jnp.bfloat16)
    grad_values = jnp.einsum(
        "hqk,qhd->khd", attend_low, grad_mixed, preferred_element_type=jnp.float32
    )
    grad_attend = jnp.einsum(
        "qhd,khd->hqk", grad_mixed, heads_view[2], preferred_element_type=jnp.float32
    )
    grad_scores = (
        attend_full * (grad_attend - jnp.sum(attend_full * grad_attend, axis=-1, keepdims=True))
    ).astype(jnp.bfloat16)
    score_scale = HEAD_DIM ** (-0.5)
    grad_queries = (
        jnp.einsum("hqk,khd->qhd", grad_scores, heads_view[1], preferred_element_type=jnp.float32)
        * score_scale
    )
    grad_keys = (
        jnp.einsum("hqk,qhd->khd", grad_scores, heads_view[0], preferred_element_type=jnp.float32)
        * score_scale
    )
    grad_projected = (
        jnp.stack([grad_queries, grad_keys, grad_values])
        .astype(jnp.bfloat16)
        .reshape(3, length, -1)
    )
    grad_normed = pair_sum(
        jnp.einsum(
            "ste,sde->td", grad_projected, project_weight, preferred_element_type=jnp.float32
        )
    )
    _, pullback = jax.vjp(norm_rows, residual, norm_gains[0], norm_gains[1])
    grad_input, grad_gain, grad_shift = pullback(grad_normed)
    return (grad_attention + grad_input, branch_low, grad_projected, (grad_gain, grad_shift))


def adam_step(gradient, master, first_old, second_old, step_rate, decay_rate):
    moment = BETA_FIRST * first_old + (1.0 - BETA_FIRST) * gradient
    variance = BETA_SECOND * second_old + (1.0 - BETA_SECOND) * gradient * gradient
    moment_hat = moment / (1.0 - BETA_FIRST**STEP)
    variance_hat = variance / (1.0 - BETA_SECOND**STEP)
    updated = master - step_rate * (
        moment_hat / (jnp.sqrt(variance_hat) + ADAM_EPSILON) + decay_rate * master
    )
    return (moment, variance, updated)


def local(
    code_tokens,
    segments,
    layout,
    durations,
    overflow,
    upper_context,
    embed_table,
    condition_weight,
    attention_weight,
    feedforward_weight,
    output_table,
    norm_gains,
    embed_master,
    condition_master,
    attention_master,
    feedforward_master,
    output_master,
    norms_master,
    embed_first,
    condition_first,
    attention_first,
    feedforward_first,
    output_first,
    norms_first,
    embed_second,
    condition_second,
    attention_second,
    feedforward_second,
    output_second,
    norms_second,
):
    spot = Spot()
    core, yh = spot.c, spot.yh
    settled = core == yh
    length = code_tokens.shape[0]

    keep_native = 1.0 - overflow[0].astype(jnp.float32)
    local_seconds = keep_native * jnp.sum(durations.astype(jnp.float32)) / SAMPLE_RATE
    native_ints = jnp.concatenate([code_tokens, segments, jnp.broadcast_to(overflow, (128,))])
    window_ints = jnp.where(settled, native_ints, swap_core(native_ints))
    window_tokens = window_ints[:length]
    window_segments = window_ints[length : 2 * length]
    keep_flag = 1.0 - window_ints[2 * length].astype(jnp.float32)

    embedded = jnp.take(embed_table, code_tokens, axis=0)
    width = embed_table.shape[1] // 2
    own_part = jnp.concatenate(
        [own_quarter(upper_context, core), own_quarter(embedded, core)], axis=1
    ).astype(F32)
    sibling_part = jnp.concatenate(
        [own_quarter(upper_context, 1 - core), own_quarter(embedded, 1 - core)], axis=1
    ).astype(F32)
    arrived_part = lax.optimization_barrier(swap_core(sibling_part))
    near_part = jnp.where(settled, own_part, arrived_part)
    far_part = lax.optimization_barrier(
        send(jnp.where(settled, arrived_part, own_part), by("y", 2))
    )
    context = jnp.concatenate([near_part[:, :width], far_part[:, :width]], axis=1).astype(BF16)

    block = spot.z * 4 + spot.x

    def crossed(value):
        return send(value, lambda z, x, y, c: (z, x, 3 - y, c))

    condition_three = condition_weight[None]
    piece_small = jnp.concatenate(
        [
            row_block(condition_three, core, block),
            row_block(attention_weight, core, block)[3:],
        ]
    )
    piece_project = row_block(attention_weight, core, block)[:3]
    piece_up = row_block(feedforward_weight, core, block)[:1]
    piece_down = row_block(feedforward_weight, core, block)[1:]
    buffers_small = gathered(crossed(piece_small), "z", "x")
    buffers_project = gathered(crossed(piece_project), "x", "z")
    buffers_up = gathered(crossed(piece_up), "x", "z")
    buffers_down = gathered(crossed(piece_down), "z", "x")
    scalars_xz = jnp.stack([spot.z, spot.x, spot.sign, core, spot.yl]).astype(jnp.int32)
    scalars_zx = jnp.stack([spot.x, spot.z, spot.sign, core, spot.yl]).astype(jnp.int32)
    condition_full = place(
        condition_three, 0, 1, [b[:, :1] for b in buffers_small], scalars_zx, 64, 256
    )[0]
    mix_full = place(attention_weight, 3, 1, [b[:, 1:] for b in buffers_small], scalars_zx, 64, 256)[0]
    project_full = place(attention_weight, 0, 3, buffers_project, scalars_xz, 256, 64)
    up_full = place(feedforward_weight, 0, 1, buffers_up, scalars_xz, 256, 64)[0]
    down_full = place(feedforward_weight, 1, 1, buffers_down, scalars_zx, 64, 256)[0]
    table_halves = own_quarter(output_table, core).reshape(2, output_table.shape[0] // 2, -1)
    near_half = crossed(lax.dynamic_index_in_dim(table_halves, 1 - spot.yl, 0, False).astype(F32))
    far_half = send(near_half, flipped("y", 1))
    output_full = place_halves(output_table, near_half, far_half, scalars_xz)

    allowed = allowed_mask(window_segments, layout)
    near_slot, far_slot = yh * 2 + core, (1 - yh) * 2 + core
    embed_part = contract(context, condition_full, 1, 1)
    columns = []
    for slot in range(4):
        columns.append(
            embed_part[:, slot * width : (slot + 1) * width]
            + jnp.where(
                near_slot == slot,
                near_part[:, width:],
                jnp.where(far_slot == slot, far_part[:, width:], 0.0),
            )
        )
    residual = pair_sum(jnp.concatenate(columns, axis=1))

    after_block, saved_state = layer_forward(
        residual, project_full, mix_full, up_full, down_full, norm_gains, allowed
    )
    loss_local, grad_block, normed_three, grad_logits, norm_three = head_loss(
        after_block, output_full, norm_gains, window_tokens, window_segments, keep_flag, spot
    )
    output_sum = reduce_rows(
        "y", spot, normed_three.T, grad_logits, (length, 512), lambda h, j, s: (0, h), 512, 512
    )
    grad_attention, down_left, grad_pre, norm_two = feedforward_backward(
        grad_block, saved_state, up_full, down_full, norm_gains
    )
    down_sum = reduce_rows(
        "z", spot, down_left.T, saved_state[8], (length, 512), lambda h, j, s: (0, h * 2 + j), 1024, 512
    )
    up_sum = reduce_rows(
        "x", spot, saved_state[6].T, grad_pre, (length, 512), lambda h, j, s: (0, h * 2 + j), 1024, 512
    )
    grad_residual, mix_left, grad_projected, norm_one = attention_backward(
        grad_attention, saved_state, project_full, mix_full, norm_gains, allowed
    )
    mix_sum = reduce_rows(
        "z", spot, mix_left.T, saved_state[4], (length, 256), lambda h, j, s: (0, h), 256, 256
    )
    project_sum = reduce_rows(
        "y", spot, saved_state[1].T, grad_projected, (1, length, 256), lambda h, j, s: (j, 0, h), 768, 256
    )
    condition_sum = reduce_rows(
        "z", spot, grad_residual.astype(BF16).T, context, (length, 256), lambda h, j, s: (0, h), 256, 256
    )
    embed_sum = reduce_rows(
        "x",
        spot,
        window_tokens[None],
        grad_residual,
        (length, 256),
        lambda h, j, s: (0, lax.rem(s[3] + h, 2) * 2 + s[2]),
        256,
        256,
        per_device=32,
        hot=True,
    )
    norms_grad = jnp.stack(
        [norm_one[0], norm_one[1], norm_two[0], norm_two[1], norm_three[0], norm_three[1]]
    )
    for axis in ("x", "y", "z"):
        for bit in (1, 2):
            norms_grad = norms_grad + send(norms_grad, flipped(axis, bit))
    dp_rank = ((spot.z * 4 + spot.x) * 2 + spot.yl) * 2 + core
    norms_share = lax.dynamic_slice_in_dim(norms_grad, dp_rank * 16, 16, 1)

    sums = [output_sum, down_sum, up_sum, mix_sum, project_sum, condition_sum, embed_sum]
    squares = 0.5 * jnp.sum((norms_share * SQUARE_SCALE) ** 2)
    for piece in sums:
        squares = squares + jnp.sum((piece * SQUARE_SCALE) ** 2)
    scalars = jnp.stack([0.5 * loss_local, squares, 0.5 * local_seconds])
    scalars = pair_sum(jnp.broadcast_to(scalars[:, None], (3, 128)))
    for axis, at in (("x", spot.x), ("z", spot.z), ("y", spot.y)):
        scalars = sum_of_four(scalars, axis, at)
    loss_total, seconds_total = scalars[0, 0], scalars[2, 0]
    inverse = 1.0 / seconds_total
    gradient_norm = jnp.sqrt(scalars[1, 0]) * (inverse / SQUARE_SCALE)
    clip_factor = CLIP_NORM / jnp.maximum(gradient_norm, CLIP_NORM)

    flat = [piece.reshape(2, 16, -1) for piece in sums[:-1]] + [sums[-1].reshape(2, 16, 512)]
    flat = jnp.concatenate(flat, axis=2)
    mine = lax.dynamic_index_in_dim(flat, core, 0, False)
    theirs = swap_core(lax.dynamic_index_in_dim(flat, 1 - core, 0, False))
    low_side = jnp.where(core == 0, mine, theirs)
    high_side = jnp.where(core == 0, theirs, mine)

    def share(start, stop):
        return low_side[:, start:stop], high_side[:, start:stop]

    output_share = jnp.concatenate(share(0, 512), axis=1)
    feedforward_share = jnp.stack(
        [jnp.concatenate(share(1536, 2560), axis=1), jnp.concatenate(share(512, 1536), axis=1)]
    )
    mix_low, mix_high = share(2560, 2816)
    project_low, project_high = share(2816, 3584)
    attention_share = jnp.stack(
        [
            jnp.concatenate(
                [project_low[:, 256 * k : 256 * k + 256], project_high[:, 256 * k : 256 * k + 256]],
                axis=1,
            )
            for k in range(3)
        ]
        + [jnp.concatenate([mix_low, mix_high], axis=1)]
    )
    condition_share = jnp.concatenate(share(3584, 3840), axis=1)
    embed_share = jnp.concatenate([part.reshape(32, 256) for part in share(3840, 4352)], axis=1)

    shares = (
        embed_share,
        condition_share,
        attention_share,
        feedforward_share,
        output_share,
        norms_share,
    )
    masters = (
        embed_master,
        condition_master,
        attention_master,
        feedforward_master,
        output_master,
        norms_master,
    )
    firsts = (
        embed_first,
        condition_first,
        attention_first,
        feedforward_first,
        output_first,
        norms_first,
    )
    seconds_old = (
        embed_second,
        condition_second,
        attention_second,
        feedforward_second,
        output_second,
        norms_second,
    )
    rates = (RATE_TABLE, RATE_MATRIX, RATE_MATRIX, RATE_MATRIX, RATE_MATRIX, RATE_NORMS)
    decays = (WEIGHT_DECAY, WEIGHT_DECAY, WEIGHT_DECAY, WEIGHT_DECAY, WEIGHT_DECAY, 0.0)
    outputs = [loss_total, seconds_total, gradient_norm]
    for slot in range(6):
        outputs += adam_step(
            shares[slot] * inverse * clip_factor,
            masters[slot],
            firsts[slot],
            seconds_old[slot],
            rates[slot],
            decays[slot],
        )
    return tuple(outputs)


def solution(mesh):
    torus = Mesh(mesh.devices.reshape(SIZES), AXES)
    table, slotted = P(DP, "yh"), P(None, DP, "yh")
    state = (table, table, slotted, slotted, table, P(None, DP))
    results = tuple(spec for spec in state for _ in range(3))
    return jax.shard_map(
        local,
        mesh=torus,
        in_specs=(
            P(DP),
            P(DP),
            P(),
            P(DP),
            P(DP),
            table,
            P(None, "yh"),
            P(None, "yh"),
            P(None, None, "yh"),
            P(None, None, "yh"),
            P(None, "yh"),
            P(),
        )
        + state * 3,
        out_specs=(P(), P(), P()) + results,
        check_vma=False,
    )
```

```python
import functools

import jax
import jax.numpy as jnp
import numpy as np
from jax import lax
from jax.experimental import pallas as pl
from jax.experimental.pallas import tpu as pltpu
from jax.sharding import Mesh
from jax.sharding import PartitionSpec as P

HEAD_DIM = 64
BLK = 64
CLIPS_DEV = 4
STEP = 10


LAYER_EPS = 1e-05
SAMPLE_RATE = 44100.0
LOG_TWO_NATS = 0.6931471805599453
CLIP_NORM = 1.0
BETA_FIRST = 0.9
BETA_SECOND = 0.95
ADAM_EPSILON = 1e-08
WEIGHT_DECAY = 0.01
RATE_MATRIX = 0.1
RATE_TABLE = 1.0
RATE_NORMS = 1.0
SQUARE_SCALE = 2.0**-9

AXES = ("z", "x", "yl", "c", "yh")
SIZES = (4, 4, 2, 2, 2)
DP = ("z", "x", "yl", "c")
VMEM_LIMIT = 40 * 1024 * 1024
QUERY_ROWS = 256
BF16 = jnp.bfloat16
F32 = jnp.float32


def send(value, move):
    pairs = []
    for index in range(int(np.prod(SIZES))):
        z, x, yl, c, yh = (int(i) for i in np.unravel_index(index, SIZES))
        target = move(z, x, yh * 2 + yl, c)
        if target is not None:
            z, x, y, c = target
            y %= 4
            at = (z % 4, x % 4, y % 2, c, y // 2)
            pairs.append((index, int(np.ravel_multi_index(at, SIZES))))
    return lax.ppermute(value, AXES, pairs)


def swap_core(value):
    return send(value, lambda z, x, y, c: (z, x, y, 1 - c))


def pair_sum(value):
    return value + swap_core(value)


def ring(axis):
    def move(z, x, y, c):
        step = 1 - 2 * c
        return {"z": (z + step, x, y, c), "x": (z, x + step, y, c), "y": (z, x, y + step, c)}[axis]

    return move


def by(axis, count):
    def move(z, x, y, c):
        return {"z": (z + count, x, y, c), "x": (z, x + count, y, c), "y": (z, x, y + count, c)}[axis]

    return move


def flipped(axis, bit):
    def move(z, x, y, c):
        return {"z": (z ^ bit, x, y, c), "x": (z, x ^ bit, y, c), "y": (z, x, y ^ bit, c)}[axis]

    return move


def after(value, *earlier):
    return lax.optimization_barrier((value, *earlier))[0]


def own_quarter(half, core):
    width = half.shape[-1] // 2
    return jnp.where(core == 0, half[..., :width], half[..., width:])


def row_block(native, core, block):
    slots, rows, width = native.shape
    view = native.reshape(slots, rows // 64, 64, width)
    rows_here = lax.dynamic_slice_in_dim(view, block, 1, 1)[:, 0]
    return own_quarter(rows_here, core).astype(F32)


def place_kernel(rings, s_ref, native_ref, *rest):
    out_ref = rest[-1]
    width = native_ref.shape[-1]
    part = width // len(rings)
    out_ref[0, :, :width] = native_ref[0]
    z, x, sign = s_ref[0], s_ref[1], s_ref[2]
    for r, axis in enumerate(rings):
        lanes = slice(width + r * part, width + (r + 1) * part)
        for j in range(4):
            for i in range(4):
                z_at = lax.rem(z - sign * (j if axis == "z" else i) + 8, 4)
                x_at = lax.rem(x - sign * (j if axis == "x" else i) + 8, 4)
                rows = pl.ds(pl.multiple_of(z_at * 256 + x_at * 64, 64), 64)
                out_ref[0, rows, lanes] = rest[4 * r + j][i].astype(BF16)


def place(native, first_slot, slots, rings, buffers, scalars):
    rows, width = native.shape[1], native.shape[2] // 2
    block = pl.BlockSpec((4, 64, width // len(rings)), lambda k, s: (0, 0, k))
    return pl.pallas_call(
        functools.partial(place_kernel, rings),
        grid_spec=pltpu.PrefetchScalarGridSpec(
            num_scalar_prefetch=1,
            grid=(slots,),
            in_specs=[pl.BlockSpec((1, rows, width), lambda k, s: (first_slot + k, 0, s[3]))]
            + [block] * len(buffers),
            out_specs=pl.BlockSpec((1, rows, 2 * width), lambda k, s: (k, 0, 0)),
        ),
        out_shape=jax.ShapeDtypeStruct((slots, rows, 2 * width), BF16),
        compiler_params=pltpu.CompilerParams(vmem_limit_bytes=VMEM_LIMIT),
        cost_estimate=estimate(1, 1),
    )(scalars, native, *buffers)


def place_halves_kernel(s_ref, native_ref, near_ref, far_ref, out_ref):
    half, width = near_ref.shape
    out_ref[:, :width] = native_ref[...]
    near = s_ref[4]
    out_ref[pl.ds(pl.multiple_of(near * half, 64), half), width:] = near_ref[...].astype(BF16)
    out_ref[pl.ds(pl.multiple_of((1 - near) * half, 64), half), width:] = far_ref[...].astype(BF16)


def place_halves(native, near, far, scalars):
    rows, width = native.shape[0], native.shape[1] // 2
    whole = pl.BlockSpec((rows // 2, width), lambda k, s: (0, 0))
    return pl.pallas_call(
        place_halves_kernel,
        grid_spec=pltpu.PrefetchScalarGridSpec(
            num_scalar_prefetch=1,
            grid=(1,),
            in_specs=[pl.BlockSpec((rows, width), lambda k, s: (0, s[3])), whole, whole],
            out_specs=pl.BlockSpec((rows, 2 * width), lambda k, s: (0, 0)),
        ),
        out_shape=jax.ShapeDtypeStruct((rows, 2 * width), BF16),
        compiler_params=pltpu.CompilerParams(vmem_limit_bytes=VMEM_LIMIT),
        cost_estimate=pl.CostEstimate(
            flops=0, bytes_accessed=rows * width * 10, transcendentals=0
        ),
    )(scalars, native, near, far)


def direct(value, axis):
    return jnp.stack([value] + [send(value, by(axis, k)) for k in (1, 2, 3)])


def around(buffer, axis):
    buffers = [buffer]
    for _ in range(3):
        buffers.append(send(buffers[-1], ring(axis)))
    return buffers


class Ring:
    def __init__(self, axis, place_at, sign, part):
        self.axis, self.place_at, self.sign, self.part = axis, place_at, sign, part
        self.step = 1
        self.total = part(lax.rem(place_at - sign + 8, 4))

    def arrive(self):
        return send(self.total, ring(self.axis))

    def add(self, arrived):
        self.step += 1
        own = lax.rem(self.place_at - self.step * self.sign + 8, 4)
        self.total = self.part(own, arrived)


def rows_of(grad, outer):
    view = grad.reshape(outer, 4, -1, grad.shape[1])

    def part(k, arrived=None):
        own = lax.dynamic_index_in_dim(view, k, 1, False).reshape(-1, grad.shape[1])
        return added(own, arrived)

    return part


def added(product, arrived):
    return product if arrived is None else product + arrived


def ring_x(spot, left, right):
    def part(k, arrived=None):
        rows = lax.dynamic_index_in_dim(left, k, 1, False).reshape(-1, left.shape[-1])
        return added(jnp.dot(rows, right, preferred_element_type=F32), arrived)

    return Ring("x", spot.x, spot.sign, part)


def ring_y(spot, left, right_own, right_other):
    def part(k, arrived=None):
        rows = lax.dynamic_index_in_dim(left, lax.rem(k, 2), 1, False).reshape(-1, left.shape[-1])
        right = jnp.where(lax.div(k, 2) == spot.yh, right_own, right_other)
        return added(jnp.dot(rows, right, preferred_element_type=F32), arrived)

    return Ring("y", spot.y, spot.sign, part)


def scatter_z(grad):
    return lax.psum_scatter(grad, "z", scatter_dimension=0, tiled=True)


def direct_y(spot, grad, rows):
    width = grad.shape[1] // 2
    view = grad.reshape(-1, 2, rows, 2 * width)
    same = lax.dynamic_index_in_dim(view, spot.yl, 1, False)
    other = lax.dynamic_index_in_dim(view, 1 - spot.yl, 1, False)
    near = send(other[..., :width], flipped("y", 1))
    far = send(other[..., width:], flipped("y", 3))
    across = send(same[..., width:], flipped("y", 2))
    return ((same[..., :width] + near) + (far + across)).reshape(-1, width)


def direct_sum(axis, place_at, grad, outer=1):
    view = grad.reshape(outer, 4, grad.shape[0] // (4 * outer), grad.shape[1])
    parts = [
        send(lax.dynamic_index_in_dim(view, lax.rem(place_at + k, 4), 1, False), by(axis, k))
        for k in (1, 2, 3)
    ]
    own = lax.dynamic_index_in_dim(view, place_at, 1, False)
    return ((own + parts[0]) + (parts[1] + parts[2])).reshape(-1, grad.shape[1])


def turned(value):
    return lax.optimization_barrier(value.T)


class Spot:
    def __init__(self):
        self.z, self.x, self.yl, self.c, self.yh = (lax.axis_index(a) for a in AXES)
        self.y = self.yh * 2 + self.yl
        self.sign = 1 - 2 * self.c


def sum_of_four(value, axis, place_at):
    pieces = [value] + [send(value, by(axis, k)) for k in (1, 2, 3)]
    total = None
    for at in range(4):
        back = lax.rem(place_at - at + 4, 4)
        part = pieces[3]
        for k in (2, 1, 0):
            part = jnp.where(back == k, pieces[k], part)
        total = part if total is None else total + part
    return total


def contract(left_side, right_side, left_dim, right_dim):
    return lax.dot_general(
        left_side,
        right_side,
        (((left_dim,), (right_dim,)), ((), ())),
        preferred_element_type=jnp.float32,
    )


def attention_forward_kernel(heads_ref, mask_ref, out_ref, total_ref):
    length = heads_ref.shape[1]
    for half in range(2):
        lanes = slice(half * HEAD_DIM, (half + 1) * HEAD_DIM)
        keys, values = heads_ref[1, :, lanes], heads_ref[2, :, lanes]
        scaled = heads_ref[0, :, lanes] * jnp.asarray(HEAD_DIM ** (-0.5), BF16)
        for start in range(0, length, QUERY_ROWS):
            stop = start + QUERY_ROWS
            scores = contract(scaled[start:stop], keys[:stop], 1, 1)
            scores = jnp.where(mask_ref[start:stop, :stop] > 0, scores, -1e30)
            top = jnp.max(scores, axis=-1, keepdims=True)
            weights = jnp.exp(scores - top)
            sums = jnp.sum(weights, axis=-1, keepdims=True)
            weights = (weights * (1.0 / sums)).astype(BF16)
            out_ref[start:stop, lanes] = contract(weights, values[:stop], 1, 0).astype(BF16)
            total_ref[0, start:stop, half : half + 1] = top + jnp.log(sums)


def attention_backward_kernel(heads_ref, mask_ref, total_ref, grad_ref, out_ref, keys_acc, values_acc):
    length = heads_ref.shape[1]
    for half in range(2):
        lanes = slice(half * HEAD_DIM, (half + 1) * HEAD_DIM)
        keys, values = heads_ref[1, :, lanes], heads_ref[2, :, lanes]
        scaled = heads_ref[0, :, lanes] * jnp.asarray(HEAD_DIM ** (-0.5), BF16)
        for start in range(length - QUERY_ROWS, -1, -QUERY_ROWS):
            stop = start + QUERY_ROWS
            queries, grad = scaled[start:stop], grad_ref[start:stop, lanes]
            scores = contract(queries, keys[:stop], 1, 1)
            scores = jnp.where(mask_ref[start:stop, :stop] > 0, scores, -1e30)
            weights = jnp.exp(scores - total_ref[0, start:stop, half : half + 1])
            grad_values = contract(weights.astype(BF16), grad, 0, 0)
            grad_weights = contract(grad, values[:stop], 1, 1)
            total = jnp.sum(weights * grad_weights, axis=-1, keepdims=True)
            grad_scores = (weights * (grad_weights - total)).astype(BF16)
            grad_queries = contract(grad_scores, keys[:stop], 1, 0) * HEAD_DIM ** (-0.5)
            out_ref[0, start:stop, lanes] = grad_queries.astype(BF16)
            grad_keys = contract(grad_scores, queries, 0, 0)
            if stop == length:
                keys_acc[...] = grad_keys
                values_acc[...] = grad_values
            else:
                keys_acc[:stop] += grad_keys
                values_acc[:stop] += grad_values
        out_ref[1, :, lanes] = keys_acc[...].astype(BF16)
        out_ref[2, :, lanes] = values_acc[...].astype(BF16)


def estimate(flops, moved):
    return pl.CostEstimate(flops=flops, bytes_accessed=moved, transcendentals=0)


def attention_forward(heads, mask):
    length, width = heads.shape[1:]
    return pl.pallas_call(
        attention_forward_kernel,
        grid=(width // 128,),
        in_specs=[
            pl.BlockSpec((3, length, 128), lambda g: (0, 0, g)),
            pl.BlockSpec((length, length), lambda g: (0, 0)),
        ],
        out_specs=[
            pl.BlockSpec((length, 128), lambda g: (0, g)),
            pl.BlockSpec((1, length, 2), lambda g: (g, 0, 0)),
        ],
        out_shape=[
            jax.ShapeDtypeStruct((length, width), BF16),
            jax.ShapeDtypeStruct((width // 128, length, 2), F32),
        ],
        compiler_params=pltpu.CompilerParams(vmem_limit_bytes=VMEM_LIMIT),
        cost_estimate=estimate(1, 1),
    )(heads, mask)


def attention_backward(heads, mask, totals, grad_mixed):
    length, width = heads.shape[1:]
    return pl.pallas_call(
        attention_backward_kernel,
        grid=(width // 128,),
        in_specs=[
            pl.BlockSpec((3, length, 128), lambda g: (0, 0, g)),
            pl.BlockSpec((length, length), lambda g: (0, 0)),
            pl.BlockSpec((1, length, 2), lambda g: (g, 0, 0)),
            pl.BlockSpec((length, 128), lambda g: (0, g)),
        ],
        out_specs=pl.BlockSpec((3, length, 128), lambda g: (0, 0, g)),
        out_shape=jax.ShapeDtypeStruct((3, length, width), BF16),
        scratch_shapes=[pltpu.VMEM((length, HEAD_DIM), F32), pltpu.VMEM((length, HEAD_DIM), F32)],
        compiler_params=pltpu.CompilerParams(vmem_limit_bytes=VMEM_LIMIT),
        cost_estimate=estimate(1, 1),
    )(heads, mask, totals, grad_mixed)


def feedforward_backward_kernel(block_ref, down_ref, pre_ref, up_ref, grad_pre_ref, normed_ref):
    grad_activated = jnp.dot(block_ref[...], down_ref[...], preferred_element_type=F32)
    pre = pre_ref[...]
    slope = 0.7978845608028654
    bent = jnp.tanh(slope * (pre + 0.044715 * pre * pre * pre))
    inner = slope * (1.0 + 3.0 * 0.044715 * pre * pre)
    factor = 0.5 * (1.0 + bent) + 0.5 * pre * (1.0 - bent * bent) * inner
    grad_pre = (grad_activated * factor).astype(BF16)
    grad_pre_ref[...] = grad_pre
    part = contract(grad_pre, up_ref[...], 1, 1)

    @pl.when(pl.program_id(0) == 0)
    def _():
        normed_ref[...] = part

    @pl.when(pl.program_id(0) > 0)
    def _():
        normed_ref[...] += part


def feedforward_backward(block_low, down_full, pre_act, up_full):
    length, hidden = pre_act.shape
    width, tile = block_low.shape[1], 512
    return pl.pallas_call(
        feedforward_backward_kernel,
        grid=(hidden // tile,),
        in_specs=[
            pl.BlockSpec((length, width), lambda g: (0, 0)),
            pl.BlockSpec((width, tile), lambda g: (0, g)),
            pl.BlockSpec((length, tile), lambda g: (0, g)),
            pl.BlockSpec((width, tile), lambda g: (0, g)),
        ],
        out_specs=[
            pl.BlockSpec((length, tile), lambda g: (0, g)),
            pl.BlockSpec((length, width), lambda g: (0, 0)),
        ],
        out_shape=[
            jax.ShapeDtypeStruct((length, hidden), BF16),
            jax.ShapeDtypeStruct((length, width), F32),
        ],
        compiler_params=pltpu.CompilerParams(vmem_limit_bytes=VMEM_LIMIT),
        cost_estimate=estimate(1, 1),
    )(block_low, down_full, pre_act, up_full)


def norm_rows(values, gain_row, shift_row):
    average = jnp.mean(values, axis=-1, keepdims=True)
    centred = values - average
    variance = jnp.mean(centred * centred, axis=-1, keepdims=True)
    return centred * lax.rsqrt(variance + LAYER_EPS) * gain_row + shift_row


def allowed_mask(segments, layout):
    length = segments.shape[0]
    position = jnp.arange(length)
    blocks = layout.shape[0]
    block_open = (
        jnp.broadcast_to(layout[:, None, :, None], (blocks, BLK, blocks, BLK)).reshape(
            length, length
        )
        > 0
    )
    causal = position[None, :] <= position[:, None]
    return causal & (segments[:, None] == segments[None, :]) & block_open


def layer_forward(residual, project_weight, mix_weight, up_weight, down_weight, norm_gains, mask, early):
    normed_one = norm_rows(residual, norm_gains[0], norm_gains[1]).astype(jnp.bfloat16)
    heads = jnp.einsum(
        "td,sde->ste", normed_one, project_weight, preferred_element_type=jnp.float32
    ).astype(jnp.bfloat16)
    heads = after(heads, *early[0])
    mixed_low, totals = attention_forward(heads, mask)
    mixed_low = after(mixed_low, *early[1])
    after_attention = residual + pair_sum(contract(mixed_low, mix_weight, 1, 1))
    normed_two = norm_rows(after_attention, norm_gains[2], norm_gains[3]).astype(jnp.bfloat16)
    normed_two = after(normed_two, *early[2])
    pre_act = jnp.dot(normed_two, up_weight, preferred_element_type=jnp.float32)
    activated = jax.nn.gelu(pre_act).astype(jnp.bfloat16)
    activated = after(activated, *early[3])
    after_block = after_attention + pair_sum(contract(activated, down_weight, 1, 1))
    saved_state = (
        residual,
        normed_one,
        heads,
        totals,
        mixed_low,
        after_attention,
        normed_two,
        pre_act,
        activated,
    )
    return (after_block, saved_state)


def head_loss(after_block, output_table, norm_gains, code_tokens, segments, keep_flag, spot):
    normed_three = norm_rows(after_block, norm_gains[4], norm_gains[5]).astype(jnp.bfloat16)
    logits = jnp.dot(normed_three, output_table, preferred_element_type=jnp.float32)
    width = output_table.shape[1]
    quarter = width // 2
    targets = jnp.concatenate([code_tokens[1:], code_tokens[-1:]])
    column = jnp.arange(width)
    code = jnp.where(
        column < quarter,
        spot.yh * width + spot.c * quarter + column,
        (1 - spot.yh) * width + spot.c * quarter + column - quarter,
    )
    target_hit = code[None, :] == targets[:, None]
    row_top = jnp.max(logits, axis=1)
    row_sums = jnp.sum(jnp.exp(logits - row_top[:, None]), axis=1)
    picked = jnp.sum(jnp.where(target_hit, logits, 0.0), axis=1)
    other = swap_core(jnp.stack([row_top, row_sums, picked]))
    both_top = jnp.maximum(row_top, other[0])
    both_sums = row_sums * jnp.exp(row_top - both_top) + other[1] * jnp.exp(other[0] - both_top)
    log_norm = both_top + jnp.log(both_sums)
    next_segment = jnp.concatenate([segments[1:], jnp.full((1,), -1, jnp.int32)])
    counted = ((segments == next_segment) & (segments < CLIPS_DEV)).astype(jnp.float32) * keep_flag
    loss_local = jnp.sum(counted * (log_norm - (picked + other[2]))) / LOG_TWO_NATS
    grad_logits = (counted / LOG_TWO_NATS)[:, None] * (
        jnp.exp(logits - log_norm[:, None]) - target_hit.astype(jnp.float32)
    )
    grad_low = grad_logits.astype(jnp.bfloat16)
    return (loss_local, normed_three, grad_low)


def norm_backward(values, gain_row, shift_row, grad_normed):
    _, pullback = jax.vjp(norm_rows, values, gain_row, shift_row)
    return pullback(grad_normed)


def adam_step(gradient, master, first_old, second_old, step_rate, decay_rate):
    moment = BETA_FIRST * first_old + (1.0 - BETA_FIRST) * gradient
    variance = BETA_SECOND * second_old + (1.0 - BETA_SECOND) * gradient * gradient
    moment_hat = moment / (1.0 - BETA_FIRST**STEP)
    variance_hat = variance / (1.0 - BETA_SECOND**STEP)
    updated = master - step_rate * (
        moment_hat / (jnp.sqrt(variance_hat) + ADAM_EPSILON) + decay_rate * master
    )
    return (moment, variance, updated)


def local(
    code_tokens,
    segments,
    layout,
    durations,
    overflow,
    upper_context,
    embed_table,
    condition_weight,
    attention_weight,
    feedforward_weight,
    output_table,
    norm_gains,
    embed_master,
    condition_master,
    attention_master,
    feedforward_master,
    output_master,
    norms_master,
    embed_first,
    condition_first,
    attention_first,
    feedforward_first,
    output_first,
    norms_first,
    embed_second,
    condition_second,
    attention_second,
    feedforward_second,
    output_second,
    norms_second,
):
    spot = Spot()
    core, yh = spot.c, spot.yh
    settled = core == yh
    length = code_tokens.shape[0]

    keep_native = 1.0 - overflow[0].astype(jnp.float32)
    local_seconds = keep_native * jnp.sum(durations.astype(jnp.float32)) / SAMPLE_RATE
    native_ints = jnp.concatenate([code_tokens, segments, jnp.broadcast_to(overflow, (128,))])
    window_ints = jnp.where(settled, native_ints, swap_core(native_ints))
    window_tokens = window_ints[:length]
    window_segments = window_ints[length : 2 * length]
    keep_flag = 1.0 - window_ints[2 * length].astype(jnp.float32)

    def crossed(value):
        return send(value, lambda z, x, y, c: (z, x, 3 - y, c))

    block = spot.z * 4 + spot.x
    barrier = lax.optimization_barrier
    project_rows = row_block(attention_weight, core, block)[:3]
    feedforward_rows = row_block(feedforward_weight, core, block)
    pieces = crossed(
        jnp.concatenate([*project_rows, feedforward_rows[1], feedforward_rows[0]], axis=1)
    )
    quarter = project_rows.shape[2]

    embedded = jnp.take(embed_table, code_tokens, axis=0).astype(F32)
    half_width = embed_table.shape[1]
    embed_part = contract(upper_context, condition_weight, 1, 1)
    embed_part = jnp.concatenate(
        [
            embed_part[:, :half_width] + jnp.where(yh == 0, embedded, 0.0),
            embed_part[:, half_width:] + jnp.where(yh == 1, embedded, 0.0),
        ],
        axis=1,
    )
    embed_part, pieces = barrier((embed_part, pieces))
    from_other = send(
        embed_part,
        lambda z, x, y, c: (z, x, y ^ 2, c) if c != y // 2 else None,
    )
    first, second = [pieces[:, : 5 * quarter]], [pieces[:, 5 * quarter :]]
    for _ in range(3):
        arrived = barrier((send(first[-1], ring("x")), send(second[-1], ring("z"))))
        first.append(arrived[0])
        second.append(arrived[1])
    first, second = jnp.stack(first), jnp.stack(second)
    first, second, from_other = barrier((first, second, from_other))
    window_sum = embed_part + from_other
    residual = jnp.where(settled, window_sum, swap_core(window_sum))

    def half_rows(native):
        halves = own_quarter(native, core).reshape(2, native.shape[0] // 2, -1)
        return lax.dynamic_index_in_dim(halves, 1 - spot.yl, 0, False).astype(F32)

    mix_half, output_half, residual = barrier(
        (half_rows(attention_weight[3]), half_rows(output_table), residual)
    )
    project_buffers = [first[:, :, : 3 * quarter]]
    up_buffers = [second[:, :, 2 * quarter :]]
    on_y = [mix_half]
    for move in (lambda z, x, y, c: (z, x, 3 - y, c), flipped("y", 1), lambda z, x, y, c: (z, x, 3 - y, c)):
        value = output_half if len(on_y) == 3 else on_y[-1]
        arrived = barrier(
            (send(project_buffers[-1], ring("z")), send(up_buffers[-1], ring("x")), send(value, move))
        )
        for buffers, value in zip((project_buffers, up_buffers, on_y), arrived, strict=True):
            buffers.append(value)
    mix_near, mix_far, output_near = on_y[1:]
    down_low, down_high = [first[:, :, 3 * quarter :]], [second[:, :, : 2 * quarter]]
    down_low[0], down_high[0], *_ = barrier((down_low[0], down_high[0], output_near))
    for k in range(3):
        arrived = [send(down_low[-1], ring("z")), send(down_high[-1], ring("x"))]
        if k == 0:
            arrived.append(send(output_near, flipped("y", 1)))
        arrived = barrier(tuple(arrived))
        down_low.append(arrived[0])
        down_high.append(arrived[1])
        if k == 0:
            output_far = arrived[2]

    scalars = jnp.stack([spot.z, spot.x, spot.sign, core, spot.yl]).astype(jnp.int32)
    project_full = place(attention_weight, 0, 3, ("z",), project_buffers, scalars)
    mix_full = place_halves(attention_weight[3], mix_near, mix_far, scalars)
    up_full = place(feedforward_weight, 0, 1, ("x",), up_buffers, scalars)[0]
    down_full = place(feedforward_weight, 1, 1, ("z", "x"), down_low + down_high, scalars)[0]
    output_full = place_halves(output_table, output_near, output_far, scalars)

    width = half_width // 2
    context_own = own_quarter(upper_context, core).astype(F32)
    context_sibling = own_quarter(upper_context, 1 - core).astype(F32)
    context_arrived = swap_core(context_sibling)
    context_near = jnp.where(settled, context_own, context_arrived)
    context_far = send(
        after(jnp.where(settled, context_arrived, context_own), output_far), by("y", 2)
    )

    allowed = allowed_mask(window_segments, layout).astype(F32)
    after_block, saved_state = layer_forward(
        residual,
        project_full,
        mix_full,
        up_full,
        down_full,
        norm_gains,
        allowed,
        (
            (mix_full, up_full, down_low[1]),
            (down_low[2], output_far),
            (down_low[3],),
            (context_far,),
        ),
    )
    residual, normed_one, heads, totals, mixed_low = saved_state[:5]
    after_attention, normed_two, pre_act, activated = saved_state[5:]
    loss_local, normed_three, grad_logits = head_loss(
        after_block, output_full, norm_gains, window_tokens, window_segments, keep_flag, spot
    )
    left_three = turned(normed_three).reshape(16, 2, 32, length)
    left_two = turned(normed_two).reshape(4, 4, 64, length)
    left_one = turned(normed_one).reshape(16, 2, 32, length)

    grad_normed = pair_sum(contract(grad_logits, output_full, 1, 1))
    output_ring = ring_y(spot, left_three, grad_logits[:, :512], grad_logits[:, 512:])
    grad_normed = after(grad_normed, output_ring.total)
    grad_block, *norm_three = norm_backward(after_block, norm_gains[4], norm_gains[5], grad_normed)
    block_low = grad_block.astype(BF16)
    down_grad = contract(block_low, activated, 0, 0)
    down_z = scatter_z(down_grad)
    block_low = after(block_low, down_grad)

    grad_pre, normed_part = feedforward_backward(block_low, down_full, pre_act, up_full)
    output_one = output_ring.arrive()
    normed_part = after(normed_part, output_one)
    grad_normed = pair_sum(normed_part)
    up_ring = ring_x(spot, left_two, grad_pre)
    output_ring.add(output_one)
    grad_normed = after(grad_normed, up_ring.total, output_ring.total)
    grad_input, *norm_two = norm_backward(
        after_attention, norm_gains[2], norm_gains[3], grad_normed
    )
    grad_attention = grad_block + grad_input
    attention_low = grad_attention.astype(BF16)
    grad_mixed = jnp.dot(attention_low, mix_full, preferred_element_type=F32).astype(BF16)
    grad_projected = attention_backward(heads, allowed, totals, grad_mixed)
    grad_projected, up_one, output_two = barrier(
        (grad_projected, up_ring.arrive(), output_ring.arrive())
    )
    up_ring.add(up_one)
    output_ring.add(output_two)
    grad_projected = after(grad_projected, up_ring.total, output_ring.total)
    quarter = grad_projected.shape[2] // 2
    project_ring = ring_y(
        spot,
        left_one,
        jnp.concatenate([grad_projected[k, :, :quarter] for k in range(3)], axis=1),
        jnp.concatenate([grad_projected[k, :, quarter:] for k in range(3)], axis=1),
    )
    normed_part = jnp.einsum(
        "ste,sde->td", grad_projected, project_full, preferred_element_type=F32
    )
    grad_normed = pair_sum(after(normed_part, project_ring.total))
    grad_input, *norm_one = norm_backward(residual, norm_gains[0], norm_gains[1], grad_normed)
    grad_residual = grad_attention + grad_input

    context_far = context_far + 0.0 * local_seconds
    context = jnp.concatenate([context_near, context_far], axis=1).astype(BF16)

    def columns_of(half):
        side = jnp.where(half == 0, grad_residual[:, : 2 * width], grad_residual[:, 2 * width :])
        return own_quarter(side, core)

    own_grad = jnp.concatenate([columns_of(yh), columns_of(1 - yh)], axis=1)
    own_high = own_grad.astype(BF16)
    own_low = (own_grad - own_high.astype(F32)).astype(BF16)
    hot = (jnp.arange(embed_table.shape[0])[:, None] == window_tokens[None, :]).astype(BF16)
    embed_grad = jnp.dot(hot, own_high, preferred_element_type=F32) + jnp.dot(
        hot, own_low, preferred_element_type=F32
    )
    embed_z = scatter_z(embed_grad)
    small_left = barrier(
        (attention_low.T.reshape(4, 4, 64, length), grad_residual.astype(BF16).T.reshape(4, 4, 64, length))
    )

    def small_part(k, arrived=None):
        parts = [
            jnp.dot(
                lax.dynamic_index_in_dim(left, k, 1, False).reshape(-1, length),
                right,
                preferred_element_type=F32,
            )
            for left, right in zip(small_left, (mixed_low, context), strict=True)
        ]
        return added(jnp.concatenate(parts, axis=1), arrived)

    small_ring = Ring("x", spot.x, spot.sign, small_part)
    norms_grad = jnp.stack([*norm_one, *norm_two, *norm_three])

    up_two, output_three, project_one, first_small = barrier(
        (up_ring.arrive(), output_ring.arrive(), project_ring.arrive(), small_ring.total)
    )
    up_ring.add(up_two)
    project_ring.add(project_one)
    output_ring.add(output_three)
    small_ring.total = first_small
    output_y = output_ring.total
    up_three, project_two, small_one, down_z = barrier(
        (up_ring.arrive(), project_ring.arrive(), small_ring.arrive(), down_z)
    )
    up_ring.add(up_three)
    project_ring.add(project_two)
    small_ring.add(small_one)
    up_x = up_ring.total
    down_ring = Ring("x", spot.x, spot.sign, rows_of(down_z, 1))
    out_ring = Ring("z", spot.z, spot.sign, rows_of(output_y, 1))
    up_zring = Ring("z", spot.z, spot.sign, rows_of(up_x, 1))
    norms = norms_grad
    norms_at = [("x", 1), ("x", 2), ("y", 1), ("y", 2), ("z", 1), ("z", 2)]

    def one_round(rings):
        nonlocal norms
        axis, bit = norms_at.pop(0)
        arrived = barrier((*[r.arrive() for r in rings], send(norms, flipped(axis, bit))))
        for r, value in zip(rings, arrived, strict=False):
            r.add(value)
        norms = norms + arrived[-1]

    one_round([project_ring, small_ring, down_ring, up_zring])
    project_zring = Ring("z", spot.z, spot.sign, rows_of(project_ring.total, 1))
    one_round([small_ring, down_ring, up_zring, project_zring])
    small_zring = Ring("z", spot.z, spot.sign, rows_of(small_ring.total, 1))
    embed_ring = Ring("x", spot.x, spot.sign, rows_of(embed_z, 1))
    one_round([down_ring, up_zring, project_zring, embed_ring])
    one_round([project_zring, small_zring, embed_ring, out_ring])
    one_round([small_zring, embed_ring, out_ring])
    one_round([small_zring, out_ring])
    norms_grad = norms
    up_z, small_z = up_zring.total, small_zring.total
    last = direct_y(
        spot,
        jnp.concatenate(
            [
                up_z[:, :1024],
                down_ring.total[:, :1024],
                small_z[:, :256],
                small_z[:, 512:768],
                up_z[:, 1024:],
                down_ring.total[:, 1024:],
                small_z[:, 256:512],
                small_z[:, 768:],
            ],
            axis=1,
        ),
        32,
    )
    embed_sum = direct_y(spot, embed_ring.total, 64)
    last_y = direct_sum(
        "x", spot.x, jnp.concatenate([out_ring.total, project_zring.total], axis=1)
    )
    output_sum, project_sum = last_y[:, :512], last_y[:, 512:]
    up_sum, down_sum = last[:, :1024], last[:, 1024:2048]
    mix_sum, condition_sum = last[:, 2048:2304], last[:, 2304:]
    dp_rank = ((spot.z * 4 + spot.x) * 2 + spot.yl) * 2 + core
    norms_share = lax.dynamic_slice_in_dim(norms_grad, dp_rank * 16, 16, 1)

    sums = [output_sum, down_sum, up_sum, mix_sum, project_sum, condition_sum, embed_sum]
    squares = 0.5 * jnp.sum((norms_share * SQUARE_SCALE) ** 2)
    for piece in sums:
        squares = squares + jnp.sum((piece * SQUARE_SCALE) ** 2)
    scalars = jnp.stack([0.5 * loss_local, squares, 0.5 * local_seconds])
    scalars = pair_sum(jnp.broadcast_to(scalars[:, None], (3, 128)))
    for axis, at in (("x", spot.x), ("z", spot.z), ("y", spot.y)):
        scalars = sum_of_four(scalars, axis, at)
    loss_total, seconds_total = scalars[0, 0], scalars[2, 0]
    inverse = 1.0 / seconds_total
    gradient_norm = jnp.sqrt(scalars[1, 0]) * (inverse / SQUARE_SCALE)
    clip_factor = CLIP_NORM / jnp.maximum(gradient_norm, CLIP_NORM)

    flat = [piece.reshape(2, 16, -1) for piece in sums[:-1]] + [sums[-1].reshape(2, 16, 512)]
    flat = jnp.concatenate(flat, axis=2)
    mine = lax.dynamic_index_in_dim(flat, core, 0, False)
    theirs = swap_core(lax.dynamic_index_in_dim(flat, 1 - core, 0, False))
    low_side = jnp.where(core == 0, mine, theirs)
    high_side = jnp.where(core == 0, theirs, mine)

    def share(start, stop):
        return low_side[:, start:stop], high_side[:, start:stop]

    output_share = jnp.concatenate(share(0, 512), axis=1)
    feedforward_share = jnp.stack(
        [jnp.concatenate(share(1536, 2560), axis=1), jnp.concatenate(share(512, 1536), axis=1)]
    )
    mix_low, mix_high = share(2560, 2816)
    project_low, project_high = share(2816, 3584)
    attention_share = jnp.stack(
        [
            jnp.concatenate(
                [project_low[:, 256 * k : 256 * k + 256], project_high[:, 256 * k : 256 * k + 256]],
                axis=1,
            )
            for k in range(3)
        ]
        + [jnp.concatenate([mix_low, mix_high], axis=1)]
    )
    condition_share = jnp.concatenate(share(3584, 3840), axis=1)
    embed_share = jnp.concatenate([part.reshape(32, 256) for part in share(3840, 4352)], axis=1)

    shares = (
        embed_share,
        condition_share,
        attention_share,
        feedforward_share,
        output_share,
        norms_share,
    )
    masters = (
        embed_master,
        condition_master,
        attention_master,
        feedforward_master,
        output_master,
        norms_master,
    )
    firsts = (
        embed_first,
        condition_first,
        attention_first,
        feedforward_first,
        output_first,
        norms_first,
    )
    seconds_old = (
        embed_second,
        condition_second,
        attention_second,
        feedforward_second,
        output_second,
        norms_second,
    )
    rates = (RATE_TABLE, RATE_MATRIX, RATE_MATRIX, RATE_MATRIX, RATE_MATRIX, RATE_NORMS)
    decays = (WEIGHT_DECAY, WEIGHT_DECAY, WEIGHT_DECAY, WEIGHT_DECAY, WEIGHT_DECAY, 0.0)
    outputs = [loss_total, seconds_total, gradient_norm]
    for slot in range(6):
        outputs += adam_step(
            shares[slot] * inverse * clip_factor,
            masters[slot],
            firsts[slot],
            seconds_old[slot],
            rates[slot],
            decays[slot],
        )
    return tuple(outputs)


def solution(mesh):
    torus = Mesh(mesh.devices.reshape(SIZES), AXES)
    table, slotted = P(DP, "yh"), P(None, DP, "yh")
    state = (table, table, slotted, slotted, table, P(None, DP))
    results = tuple(spec for spec in state for _ in range(3))
    return jax.shard_map(
        local,
        mesh=torus,
        in_specs=(
            P(DP),
            P(DP),
            P(),
            P(DP),
            P(DP),
            table,
            P(None, "yh"),
            P(None, "yh"),
            P(None, None, "yh"),
            P(None, None, "yh"),
            P(None, "yh"),
            P(),
        )
        + state * 3,
        out_specs=(P(), P(), P()) + results,
        check_vma=False,
    )
```

```python
import functools

import jax
import jax.numpy as jnp
import numpy as np
from jax import lax
from jax.experimental import pallas as pl
from jax.experimental.pallas import tpu as pltpu
from jax.sharding import Mesh
from jax.sharding import PartitionSpec as P

HEAD_DIM = 64
BLK = 64
CLIPS_DEV = 4
STEP = 10


LAYER_EPS = 1e-05
SAMPLE_RATE = 44100.0
LOG_TWO_NATS = 0.6931471805599453
CLIP_NORM = 1.0
BETA_FIRST = 0.9
BETA_SECOND = 0.95
ADAM_EPSILON = 1e-08
WEIGHT_DECAY = 0.01
RATE_MATRIX = 0.1
RATE_TABLE = 1.0
RATE_NORMS = 1.0
SQUARE_SCALE = 2.0**-9

AXES = ("z", "x", "yl", "c", "yh")
SIZES = (4, 4, 2, 2, 2)
DP = ("z", "x", "yl", "c")
MIB = 1024 * 1024
QUERY_ROWS = 256
BF16 = jnp.bfloat16
F32 = jnp.float32


def send(value, move):
    pairs = []
    for index in range(int(np.prod(SIZES))):
        z, x, yl, c, yh = (int(i) for i in np.unravel_index(index, SIZES))
        target = move(z, x, yh * 2 + yl, c)
        if target is not None:
            z, x, y, c = target
            y %= 4
            at = (z % 4, x % 4, y % 2, c, y // 2)
            pairs.append((index, int(np.ravel_multi_index(at, SIZES))))
    return lax.ppermute(value, AXES, pairs)


def swap_core(value):
    return send(value, lambda z, x, y, c: (z, x, y, 1 - c))


def pair_sum(value):
    return value + swap_core(value)


def ring(axis):
    def move(z, x, y, c):
        step = 1 - 2 * c
        return {"z": (z + step, x, y, c), "x": (z, x + step, y, c), "y": (z, x, y + step, c)}[axis]

    return move


def by(axis, count):
    def move(z, x, y, c):
        return {"z": (z + count, x, y, c), "x": (z, x + count, y, c), "y": (z, x, y + count, c)}[axis]

    return move


def flipped(axis, bit):
    def move(z, x, y, c):
        return {"z": (z ^ bit, x, y, c), "x": (z, x ^ bit, y, c), "y": (z, x, y ^ bit, c)}[axis]

    return move


def after(value, *earlier):
    return lax.optimization_barrier((value, *earlier))[0]


def pieces_kernel(s_ref, *refs):
    width = 0
    for ref in refs[:-1]:
        refs[-1][:, width : width + ref.shape[-1]] = ref[0].astype(F32)
        width += ref.shape[-1]


def pieces_of(attention_weight, feedforward_weight, index):
    narrow, wide = attention_weight.shape[2] // 2, feedforward_weight.shape[2] // 2
    specs = [pl.BlockSpec((1, 64, narrow), lambda g, s, k=k: (k, s[0], s[1])) for k in range(3)]
    specs += [pl.BlockSpec((1, 64, wide), lambda g, s, k=k: (k, s[0], s[1])) for k in (1, 0)]
    width = 3 * narrow + 2 * wide
    return pl.pallas_call(
        pieces_kernel,
        grid_spec=pltpu.PrefetchScalarGridSpec(
            num_scalar_prefetch=1,
            grid=(1,),
            in_specs=specs,
            out_specs=pl.BlockSpec((64, width), lambda g, s: (0, 0)),
        ),
        out_shape=jax.ShapeDtypeStruct((64, width), F32),
        compiler_params=pltpu.CompilerParams(vmem_limit_bytes=8 * MIB),
        cost_estimate=estimate(1, 1),
    )(index, *in_hbm(*[attention_weight] * 3, *[feedforward_weight] * 2))


def own_quarter(half, core):
    width = half.shape[-1] // 2
    return jnp.where(core == 0, half[..., :width], half[..., width:])


def place_kernel(rings, s_ref, native_ref, *rest):
    out_ref = rest[-1]
    width = native_ref.shape[-1]
    part = width // len(rings)
    out_ref[0, :, :width] = native_ref[0]
    z, x, sign = s_ref[0], s_ref[1], s_ref[2]
    for r, axis in enumerate(rings):
        lanes = slice(width + r * part, width + (r + 1) * part)
        for j in range(4):
            for i in range(4):
                z_at = lax.rem(z - sign * (j if axis == "z" else i) + 8, 4)
                x_at = lax.rem(x - sign * (j if axis == "x" else i) + 8, 4)
                rows = pl.ds(pl.multiple_of(z_at * 256 + x_at * 64, 64), 64)
                out_ref[0, rows, lanes] = rest[4 * r + j][i].astype(BF16)


def place(native, first_slot, slots, rings, buffers, scalars):
    rows, width = native.shape[1], native.shape[2] // 2
    block = pl.BlockSpec((4, 64, width // len(rings)), lambda k, s: (0, 0, k))
    return pl.pallas_call(
        functools.partial(place_kernel, rings),
        grid_spec=pltpu.PrefetchScalarGridSpec(
            num_scalar_prefetch=1,
            grid=(slots,),
            in_specs=[pl.BlockSpec((1, rows, width), lambda k, s: (first_slot + k, 0, s[3]))]
            + [block] * len(buffers),
            out_specs=pl.BlockSpec((1, rows, 2 * width), lambda k, s: (k, 0, 0)),
        ),
        out_shape=jax.ShapeDtypeStruct((slots, rows, 2 * width), BF16),
        compiler_params=pltpu.CompilerParams(vmem_limit_bytes=24 * MIB),
        cost_estimate=estimate(1, 1),
    )(scalars, *in_hbm(native), *buffers)


def place_halves_kernel(s_ref, native_ref, near_ref, far_ref, out_ref):
    half, width = near_ref.shape
    out_ref[:, :width] = native_ref[...]
    near = s_ref[4]
    out_ref[pl.ds(pl.multiple_of(near * half, 64), half), width:] = near_ref[...].astype(BF16)
    out_ref[pl.ds(pl.multiple_of((1 - near) * half, 64), half), width:] = far_ref[...].astype(BF16)


def place_halves(native, near, far, scalars):
    rows, width = native.shape[0], native.shape[1] // 2
    whole = pl.BlockSpec((rows // 2, width), lambda k, s: (0, 0))
    return pl.pallas_call(
        place_halves_kernel,
        grid_spec=pltpu.PrefetchScalarGridSpec(
            num_scalar_prefetch=1,
            grid=(1,),
            in_specs=[pl.BlockSpec((rows, width), lambda k, s: (0, s[3])), whole, whole],
            out_specs=pl.BlockSpec((rows, 2 * width), lambda k, s: (0, 0)),
        ),
        out_shape=jax.ShapeDtypeStruct((rows, 2 * width), BF16),
        compiler_params=pltpu.CompilerParams(vmem_limit_bytes=12 * MIB),
        cost_estimate=pl.CostEstimate(
            flops=0, bytes_accessed=rows * width * 10, transcendentals=0
        ),
    )(scalars, *in_hbm(native), near, far)


def direct(value, axis):
    return jnp.stack([value] + [send(value, by(axis, k)) for k in (1, 2, 3)])


def around(buffer, axis):
    buffers = [buffer]
    for _ in range(3):
        buffers.append(send(buffers[-1], ring(axis)))
    return buffers


class Ring:
    def __init__(self, axis, place_at, sign, part):
        self.axis, self.place_at, self.sign, self.part = axis, place_at, sign, part
        self.step = 1
        self.total = part(lax.rem(place_at - sign + 8, 4))

    def arrive(self):
        return send(self.total, ring(self.axis))

    def add(self, arrived):
        self.step += 1
        own = lax.rem(self.place_at - self.step * self.sign + 8, 4)
        self.total = self.part(own, arrived)


def ring_of(spot, axis, grad):
    view = grad.reshape(1, 4, -1, grad.shape[1])

    def part(k, arrived=None):
        return chunk_added(view, k.astype(jnp.int32)[None], arrived)

    return Ring(axis, spot.z if axis == "z" else spot.x, spot.sign, part)


def added(product, arrived):
    return product if arrived is None else product + arrived


def ring_x(spot, left, right, tile):
    left = left.reshape(4, 4, -1, left.shape[-1])
    segment = (left, right, (right.shape[0], tile), lambda j, s: (0, j), right.shape[1] // tile)

    def part(k, arrived=None):
        index = k.astype(jnp.int32)[None]
        return chunk_product([segment], (4, 1, *left.shape[2:]), tile, index, arrived)

    return Ring("x", spot.x, spot.sign, part)


def ring_y(spot, tile, *segments):
    tokens = segments[0][0].shape[-1]
    rest = segments[0][0].shape[0] // 32

    def part(k, arrived=None):
        half = jnp.where(lax.div(k, 2) == spot.yh, 0, 1)
        index = jnp.stack([lax.rem(k, 2), half]).astype(jnp.int32)
        turned = [
            (left.reshape(16, 2, rest, tokens), right, block, lambda j, s, at=at: at(j, s[1]), tiles)
            for left, right, block, at, tiles in segments
        ]
        return chunk_product(turned, (16, 1, rest, tokens), tile, index, arrived)

    return Ring("y", spot.y, spot.sign, part)


def scatter_z(grad):
    return lax.psum_scatter(grad, "z", scatter_dimension=0, tiled=True)


def direct_y(spot, grad, rows):
    width = grad.shape[1] // 2
    view = grad.reshape(-1, 2, rows, 2 * width)
    same = lax.dynamic_index_in_dim(view, spot.yl, 1, False)
    other = lax.dynamic_index_in_dim(view, 1 - spot.yl, 1, False)
    near = send(other[..., :width], flipped("y", 1))
    far = send(other[..., width:], flipped("y", 3))
    across = send(same[..., width:], flipped("y", 2))
    return ((same[..., :width] + near) + (far + across)).reshape(-1, width)


def direct_sum(axis, place_at, grad, outer=1):
    view = grad.reshape(outer, 4, grad.shape[0] // (4 * outer), grad.shape[1])
    parts = [
        send(lax.dynamic_index_in_dim(view, lax.rem(place_at + k, 4), 1, False), by(axis, k))
        for k in (1, 2, 3)
    ]
    own = lax.dynamic_index_in_dim(view, place_at, 1, False)
    return ((own + parts[0]) + (parts[1] + parts[2])).reshape(-1, grad.shape[1])


def turned(value):
    return lax.optimization_barrier(value.T)


class Spot:
    def __init__(self):
        self.z, self.x, self.yl, self.c, self.yh = (lax.axis_index(a) for a in AXES)
        self.y = self.yh * 2 + self.yl
        self.sign = 1 - 2 * self.c


def sum_of_four(value, axis, place_at):
    pieces = [value] + [send(value, by(axis, k)) for k in (1, 2, 3)]
    total = None
    for at in range(4):
        back = lax.rem(place_at - at + 4, 4)
        part = pieces[3]
        for k in (2, 1, 0):
            part = jnp.where(back == k, pieces[k], part)
        total = part if total is None else total + part
    return total


def contract(left_side, right_side, left_dim, right_dim):
    return lax.dot_general(
        left_side,
        right_side,
        (((left_dim,), (right_dim,)), ((), ())),
        preferred_element_type=jnp.float32,
    )


def attention_forward_kernel(heads_ref, mask_ref, out_ref, total_ref):
    length = heads_ref.shape[1]
    for half in range(2):
        lanes = slice(half * HEAD_DIM, (half + 1) * HEAD_DIM)
        keys, values = heads_ref[1, :, lanes], heads_ref[2, :, lanes]
        scaled = heads_ref[0, :, lanes] * jnp.asarray(HEAD_DIM ** (-0.5), BF16)
        for start in range(0, length, QUERY_ROWS):
            stop = start + QUERY_ROWS
            scores = contract(scaled[start:stop], keys[:stop], 1, 1)
            scores = jnp.where(mask_ref[start:stop, :stop] > 0, scores, -1e30)
            top = jnp.max(scores, axis=-1, keepdims=True)
            weights = jnp.exp(scores - top)
            sums = jnp.sum(weights, axis=-1, keepdims=True)
            weights = (weights * (1.0 / sums)).astype(BF16)
            out_ref[start:stop, lanes] = contract(weights, values[:stop], 1, 0).astype(BF16)
            total_ref[0, start:stop, half : half + 1] = top + jnp.log(sums)


def attention_backward_kernel(heads_ref, mask_ref, total_ref, grad_ref, out_ref, keys_acc, values_acc):
    length = heads_ref.shape[1]
    for half in range(2):
        lanes = slice(half * HEAD_DIM, (half + 1) * HEAD_DIM)
        keys, values = heads_ref[1, :, lanes], heads_ref[2, :, lanes]
        scaled = heads_ref[0, :, lanes] * jnp.asarray(HEAD_DIM ** (-0.5), BF16)
        for start in range(length - QUERY_ROWS, -1, -QUERY_ROWS):
            stop = start + QUERY_ROWS
            queries, grad = scaled[start:stop], grad_ref[start:stop, lanes]
            scores = contract(queries, keys[:stop], 1, 1)
            scores = jnp.where(mask_ref[start:stop, :stop] > 0, scores, -1e30)
            weights = jnp.exp(scores - total_ref[0, start:stop, half : half + 1])
            grad_values = contract(weights.astype(BF16), grad, 0, 0)
            grad_weights = contract(grad, values[:stop], 1, 1)
            total = jnp.sum(weights * grad_weights, axis=-1, keepdims=True)
            grad_scores = (weights * (grad_weights - total)).astype(BF16)
            grad_queries = contract(grad_scores, keys[:stop], 1, 0) * HEAD_DIM ** (-0.5)
            out_ref[0, start:stop, lanes] = grad_queries.astype(BF16)
            grad_keys = contract(grad_scores, queries, 0, 0)
            if stop == length:
                keys_acc[...] = grad_keys
                values_acc[...] = grad_values
            else:
                keys_acc[:stop] += grad_keys
                values_acc[:stop] += grad_values
        out_ref[1, :, lanes] = keys_acc[...].astype(BF16)
        out_ref[2, :, lanes] = values_acc[...].astype(BF16)


def estimate(flops, moved):
    return pl.CostEstimate(flops=flops, bytes_accessed=moved, transcendentals=0)


def in_hbm(*values):
    return [pltpu.with_memory_space_constraint(value, pltpu.HBM) for value in values]


def norm_forward_kernel(row, parts, base_ref, *rest):
    ins, outs = rest[: parts + 1], rest[parts + 1 :]
    gains_ref = ins[-1]
    values = base_ref[...]
    if parts:
        values = values + (ins[0][...] + ins[1][...])
        outs[2][...] = values
    centred = values - jnp.mean(values, axis=-1, keepdims=True)
    variance = jnp.mean(centred * centred, axis=-1, keepdims=True)
    normed = centred * lax.rsqrt(variance + LAYER_EPS) * gains_ref[row : row + 1] + gains_ref[row + 1 : row + 2]
    outs[0][...] = normed.astype(BF16)
    outs[1][...] = normed.T.astype(BF16)


def norm_forward(row, gains, base, parts=()):
    length, width = base.shape
    rows = 128
    block = pl.BlockSpec((rows, width), lambda g: (g, 0))
    turned = pl.BlockSpec((width, rows), lambda g: (0, g))
    shapes = [jax.ShapeDtypeStruct((length, width), BF16), jax.ShapeDtypeStruct((width, length), BF16)]
    if parts:
        shapes.append(jax.ShapeDtypeStruct((length, width), F32))
    return pl.pallas_call(
        functools.partial(norm_forward_kernel, row, len(parts)),
        grid=(length // rows,),
        in_specs=[block] * (1 + len(parts)) + [pl.BlockSpec(gains.shape, lambda g: (0, 0))],
        out_specs=[block, turned, block][: len(shapes)],
        out_shape=shapes,
        compiler_params=pltpu.CompilerParams(vmem_limit_bytes=14 * MIB),
        cost_estimate=estimate(1, 1),
    )(base, *parts, gains)


def norm_backward_kernel(row, has_base, values_ref, part_ref, other_ref, gains_ref, *rest):
    if has_base:
        base_ref, rest = rest[0], rest[1:]
    out_ref, low_ref, turned_ref, sums_ref = rest
    values = values_ref[...]
    grad = part_ref[...] + other_ref[...]
    centred = values - jnp.mean(values, axis=-1, keepdims=True)
    scale = lax.rsqrt(jnp.mean(centred * centred, axis=-1, keepdims=True) + LAYER_EPS)
    normed = centred * scale
    gained = grad * gains_ref[row : row + 1]
    inner = gained - jnp.mean(gained, axis=-1, keepdims=True)
    inner = scale * (inner - normed * jnp.mean(gained * normed, axis=-1, keepdims=True))
    if has_base:
        inner = base_ref[...] + inner
    out_ref[...] = inner
    low_ref[...] = inner.astype(BF16)
    turned_ref[...] = inner.T.astype(BF16)
    sums = jnp.concatenate(
        [jnp.sum(grad * normed, axis=0, keepdims=True), jnp.sum(grad, axis=0, keepdims=True)], axis=0
    )

    @pl.when(pl.program_id(0) == 0)
    def _():
        sums_ref[...] = sums

    @pl.when(pl.program_id(0) > 0)
    def _():
        sums_ref[...] += sums


def norm_backward(row, gains, values, part, other, base=None):
    length, width = values.shape
    rows = 128
    block = pl.BlockSpec((rows, width), lambda g: (g, 0))
    operands = [values, part, other, gains] + ([] if base is None else [base])
    specs = [block] * 3 + [pl.BlockSpec(gains.shape, lambda g: (0, 0))] + ([] if base is None else [block])
    return pl.pallas_call(
        functools.partial(norm_backward_kernel, row, base is not None),
        grid=(length // rows,),
        in_specs=specs,
        out_specs=[
            block,
            block,
            pl.BlockSpec((width, rows), lambda g: (0, g)),
            pl.BlockSpec((2, width), lambda g: (0, 0)),
        ],
        out_shape=[
            jax.ShapeDtypeStruct((length, width), F32),
            jax.ShapeDtypeStruct((length, width), BF16),
            jax.ShapeDtypeStruct((width, length), BF16),
            jax.ShapeDtypeStruct((2, width), F32),
        ],
        compiler_params=pltpu.CompilerParams(vmem_limit_bytes=16 * MIB),
        cost_estimate=estimate(1, 1),
    )(*operands)


def chunk_kernel(bounds, has_recv, s_ref, *rest):
    out_ref = rest[-1]
    for n, (start, stop) in enumerate(bounds):
        left_ref, right_ref = rest[2 * n], rest[2 * n + 1]

        @pl.when((pl.program_id(0) >= start) & (pl.program_id(0) < stop))
        def _(left_ref=left_ref, right_ref=right_ref):
            left = left_ref[...].reshape(out_ref.shape[0], left_ref.shape[-1])
            right = right_ref[...].reshape(right_ref.shape[-2:])
            total = jnp.dot(left, right, preferred_element_type=F32)
            if has_recv:
                total += rest[2 * len(bounds)][...]
            out_ref[...] = total


def chunk_product(segments, left_block, tile, index, arrived, place_for=jax.ShapeDtypeStruct):
    rows = int(np.prod(left_block[:-1]))
    out_spec = pl.BlockSpec((rows, tile), lambda j, s: (0, j))
    operands, specs, bounds, start = [], [], [], 0
    for left, right, right_block, right_at, tiles in segments:

        def at(j, s, start=start, tiles=tiles, right_at=right_at):
            return right_at(jnp.clip(j - start, 0, tiles - 1), s)

        operands += [left, right]
        specs += [
            pl.BlockSpec(left_block, lambda j, s: (0, s[0], 0, 0)),
            pl.BlockSpec(right_block, at),
        ]
        bounds.append((start, start + tiles))
        start += tiles
    extra = [] if arrived is None else [arrived]
    return pl.pallas_call(
        functools.partial(chunk_kernel, tuple(bounds), arrived is not None),
        grid_spec=pltpu.PrefetchScalarGridSpec(
            num_scalar_prefetch=1,
            grid=(start,),
            in_specs=specs + [out_spec] * len(extra),
            out_specs=out_spec,
        ),
        out_shape=place_for((rows, tile * start), F32),
        compiler_params=pltpu.CompilerParams(vmem_limit_bytes=16 * MIB),
        cost_estimate=estimate(1, 1),
    )(index, *operands, *extra)


def add_kernel(s_ref, own_ref, *rest):
    out_ref = rest[-1]
    total = own_ref[0, 0]
    for arrived_ref in rest[:-1]:
        total = total + arrived_ref[...]
    out_ref[...] = total


def chunk_added(view, index, arrived):
    rows, width = view.shape[2:]
    tile = width // 2
    out_spec = pl.BlockSpec((rows, tile), lambda j, s: (0, j))
    extra = [] if arrived is None else [arrived]
    return pl.pallas_call(
        add_kernel,
        grid_spec=pltpu.PrefetchScalarGridSpec(
            num_scalar_prefetch=1,
            grid=(2,),
            in_specs=[pl.BlockSpec((1, 1, rows, tile), lambda j, s: (0, s[0], 0, j))]
            + [out_spec] * len(extra),
            out_specs=out_spec,
        ),
        out_shape=jax.ShapeDtypeStruct((rows, width), F32),
        compiler_params=pltpu.CompilerParams(vmem_limit_bytes=8 * MIB),
        cost_estimate=estimate(1, 1),
    )(index, view, *extra)


def attention_forward(heads, mask):
    length, width = heads.shape[1:]
    return pl.pallas_call(
        attention_forward_kernel,
        grid=(width // 128,),
        in_specs=[
            pl.BlockSpec((3, length, 128), lambda g: (0, 0, g)),
            pl.BlockSpec((length, length), lambda g: (0, 0)),
        ],
        out_specs=[
            pl.BlockSpec((length, 128), lambda g: (0, g)),
            pl.BlockSpec((1, length, 2), lambda g: (g, 0, 0)),
        ],
        out_shape=[
            jax.ShapeDtypeStruct((length, width), BF16),
            jax.ShapeDtypeStruct((width // 128, length, 2), F32),
        ],
        compiler_params=pltpu.CompilerParams(vmem_limit_bytes=16 * MIB),
        cost_estimate=estimate(1, 1),
    )(heads, mask)


def attention_backward(heads, mask, totals, grad_mixed):
    length, width = heads.shape[1:]
    return pl.pallas_call(
        attention_backward_kernel,
        grid=(width // 128,),
        in_specs=[
            pl.BlockSpec((3, length, 128), lambda g: (0, 0, g)),
            pl.BlockSpec((length, length), lambda g: (0, 0)),
            pl.BlockSpec((1, length, 2), lambda g: (g, 0, 0)),
            pl.BlockSpec((length, 128), lambda g: (0, g)),
        ],
        out_specs=pl.BlockSpec((3, length, 128), lambda g: (0, 0, g)),
        out_shape=jax.ShapeDtypeStruct((3, length, width), BF16),
        scratch_shapes=[pltpu.VMEM((length, HEAD_DIM), F32), pltpu.VMEM((length, HEAD_DIM), F32)],
        compiler_params=pltpu.CompilerParams(vmem_limit_bytes=16 * MIB),
        cost_estimate=estimate(1, 1),
    )(heads, mask, totals, grad_mixed)


def feedforward_backward_kernel(block_ref, down_ref, pre_ref, up_ref, grad_pre_ref, normed_ref):
    grad_activated = jnp.dot(block_ref[...], down_ref[...], preferred_element_type=F32)
    pre = pre_ref[...]
    slope = 0.7978845608028654
    bent = jnp.tanh(slope * (pre + 0.044715 * pre * pre * pre))
    inner = slope * (1.0 + 3.0 * 0.044715 * pre * pre)
    factor = 0.5 * (1.0 + bent) + 0.5 * pre * (1.0 - bent * bent) * inner
    grad_pre = (grad_activated * factor).astype(BF16)
    grad_pre_ref[...] = grad_pre
    part = contract(grad_pre, up_ref[...], 1, 1)

    @pl.when(pl.program_id(0) == 0)
    def _():
        normed_ref[...] = part

    @pl.when(pl.program_id(0) > 0)
    def _():
        normed_ref[...] += part


def feedforward_backward(block_low, down_full, pre_act, up_full):
    length, hidden = pre_act.shape
    width, tile = block_low.shape[1], 512
    return pl.pallas_call(
        feedforward_backward_kernel,
        grid=(hidden // tile,),
        in_specs=[
            pl.BlockSpec((length, width), lambda g: (0, 0)),
            pl.BlockSpec((width, tile), lambda g: (0, g)),
            pl.BlockSpec((length, tile), lambda g: (0, g)),
            pl.BlockSpec((width, tile), lambda g: (0, g)),
        ],
        out_specs=[
            pl.BlockSpec((length, tile), lambda g: (0, g)),
            pl.BlockSpec((length, width), lambda g: (0, 0)),
        ],
        out_shape=[
            jax.ShapeDtypeStruct((length, hidden), BF16),
            jax.ShapeDtypeStruct((length, width), F32),
        ],
        compiler_params=pltpu.CompilerParams(vmem_limit_bytes=22 * MIB),
        cost_estimate=estimate(1, 1),
    )(*in_hbm(block_low, down_full, pre_act, up_full))


def allowed_mask(segments, layout):
    length = segments.shape[0]
    position = jnp.arange(length)
    blocks = layout.shape[0]
    block_open = (
        jnp.broadcast_to(layout[:, None, :, None], (blocks, BLK, blocks, BLK)).reshape(
            length, length
        )
        > 0
    )
    causal = position[None, :] <= position[:, None]
    return causal & (segments[:, None] == segments[None, :]) & block_open


def layer_forward(residual, project_weight, mix_weight, up_weight, down_weight, norm_gains, mask, early):
    normed_one, left_one = norm_forward(0, norm_gains, residual)
    heads = jnp.einsum(
        "td,sde->ste", normed_one, project_weight, preferred_element_type=jnp.float32
    ).astype(jnp.bfloat16)
    heads = after(heads, *early[0])
    mixed_low, totals = attention_forward(heads, mask)
    mixed_low = after(mixed_low, *early[1])
    part = contract(mixed_low, mix_weight, 1, 1)
    other = after(swap_core(part), *early[2])
    normed_two, left_two, after_attention = norm_forward(2, norm_gains, residual, (part, other))
    pre_act = jnp.dot(normed_two, up_weight, preferred_element_type=jnp.float32)
    activated = jax.nn.gelu(pre_act).astype(jnp.bfloat16)
    activated = after(activated, *early[3])
    down_full = down_weight(activated)
    part = contract(activated, down_full, 1, 1)
    normed_three, left_three, after_block = norm_forward(
        4, norm_gains, after_attention, (part, swap_core(part))
    )
    saved_state = (heads, totals, mixed_low, after_attention, pre_act, activated, down_full)
    return (after_block, normed_three, (left_one, left_two, left_three), saved_state)


def head_loss(normed_three, output_table, code_tokens, segments, keep_flag, spot):
    logits = jnp.dot(normed_three, output_table, preferred_element_type=jnp.float32)
    width = output_table.shape[1]
    quarter = width // 2
    targets = jnp.concatenate([code_tokens[1:], code_tokens[-1:]])
    column = jnp.arange(width)
    code = jnp.where(
        column < quarter,
        spot.yh * width + spot.c * quarter + column,
        (1 - spot.yh) * width + spot.c * quarter + column - quarter,
    )
    target_hit = code[None, :] == targets[:, None]
    row_top = jnp.max(logits, axis=1)
    row_sums = jnp.sum(jnp.exp(logits - row_top[:, None]), axis=1)
    picked = jnp.sum(jnp.where(target_hit, logits, 0.0), axis=1)
    other = swap_core(jnp.stack([row_top, row_sums, picked]))
    both_top = jnp.maximum(row_top, other[0])
    both_sums = row_sums * jnp.exp(row_top - both_top) + other[1] * jnp.exp(other[0] - both_top)
    log_norm = both_top + jnp.log(both_sums)
    next_segment = jnp.concatenate([segments[1:], jnp.full((1,), -1, jnp.int32)])
    counted = ((segments == next_segment) & (segments < CLIPS_DEV)).astype(jnp.float32) * keep_flag
    loss_local = jnp.sum(counted * (log_norm - (picked + other[2]))) / LOG_TWO_NATS
    grad_logits = (counted / LOG_TWO_NATS)[:, None] * (
        jnp.exp(logits - log_norm[:, None]) - target_hit.astype(jnp.float32)
    )
    grad_low = grad_logits.astype(jnp.bfloat16)
    return (loss_local, grad_low)


def adam_step(gradient, master, first_old, second_old, step_rate, decay_rate):
    moment = BETA_FIRST * first_old + (1.0 - BETA_FIRST) * gradient
    variance = BETA_SECOND * second_old + (1.0 - BETA_SECOND) * gradient * gradient
    moment_hat = moment / (1.0 - BETA_FIRST**STEP)
    variance_hat = variance / (1.0 - BETA_SECOND**STEP)
    updated = master - step_rate * (
        moment_hat / (jnp.sqrt(variance_hat) + ADAM_EPSILON) + decay_rate * master
    )
    return (moment, variance, updated)


def local(
    code_tokens,
    segments,
    layout,
    durations,
    overflow,
    upper_context,
    embed_table,
    condition_weight,
    attention_weight,
    feedforward_weight,
    output_table,
    norm_gains,
    embed_master,
    condition_master,
    attention_master,
    feedforward_master,
    output_master,
    norms_master,
    embed_first,
    condition_first,
    attention_first,
    feedforward_first,
    output_first,
    norms_first,
    embed_second,
    condition_second,
    attention_second,
    feedforward_second,
    output_second,
    norms_second,
):
    spot = Spot()
    core, yh = spot.c, spot.yh
    settled = core == yh
    length = code_tokens.shape[0]

    keep_native = 1.0 - overflow[0].astype(jnp.float32)
    local_seconds = keep_native * jnp.sum(durations.astype(jnp.float32)) / SAMPLE_RATE
    native_ints = jnp.concatenate([code_tokens, segments, jnp.broadcast_to(overflow, (128,))])
    window_ints = jnp.where(settled, native_ints, swap_core(native_ints))
    window_tokens = window_ints[:length]
    window_segments = window_ints[length : 2 * length]
    keep_flag = 1.0 - window_ints[2 * length].astype(jnp.float32)

    def crossed(value):
        return send(value, lambda z, x, y, c: (z, x, 3 - y, c))

    block = spot.z * 4 + spot.x
    barrier = lax.optimization_barrier
    pieces = crossed(
        pieces_of(attention_weight, feedforward_weight, jnp.stack([block, core]).astype(jnp.int32))
    )
    quarter = attention_weight.shape[2] // 2

    embedded = jnp.take(embed_table, code_tokens, axis=0).astype(F32)
    half_width = embed_table.shape[1]
    embed_part = contract(upper_context, condition_weight, 1, 1)
    embed_part = jnp.concatenate(
        [
            embed_part[:, :half_width] + jnp.where(yh == 0, embedded, 0.0),
            embed_part[:, half_width:] + jnp.where(yh == 1, embedded, 0.0),
        ],
        axis=1,
    )
    width = half_width // 2
    context_own = own_quarter(upper_context, core).astype(F32)
    context_arrived = swap_core(own_quarter(upper_context, 1 - core).astype(F32))
    embed_part, pieces, context_arrived = barrier((embed_part, pieces, context_arrived))
    context_near = jnp.where(settled, context_own, context_arrived)
    from_other = send(
        embed_part,
        lambda z, x, y, c: (z, x, y ^ 2, c) if c != y // 2 else None,
    )
    first, second = [pieces[:, : 5 * quarter]], [pieces[:, 5 * quarter :]]
    for _ in range(3):
        first.append(send(first[-1], ring("x")))
        second.append(send(second[-1], ring("z")))
    window_sum = embed_part + from_other
    residual = jnp.where(settled, window_sum, swap_core(window_sum))

    def half_rows(native):
        halves = own_quarter(native, core).reshape(2, native.shape[0] // 2, -1)
        return lax.dynamic_index_in_dim(halves, 1 - spot.yl, 0, False).astype(F32)

    def turned(pieces, start, stop, axis, *earlier):
        columns = jnp.stack([piece[:, start * quarter : stop * quarter] for piece in pieces])
        return around(after(columns, *earlier), axis)

    up_buffers = turned(second, 2, 6, "x")
    project_buffers = [jnp.stack([piece[:, : 3 * quarter] for piece in first])]
    mix_near = crossed(after(half_rows(attention_weight[3]), from_other))
    project_buffers.append(send(project_buffers[-1], ring("z")))
    project_buffers[1], mix_near = barrier((project_buffers[1], mix_near))
    mix_far = send(mix_near, flipped("y", 1))
    output_near = crossed(after(half_rows(output_table), mix_near))
    project_buffers.append(send(project_buffers[-1], ring("z")))
    project_buffers.append(send(project_buffers[-1], ring("z")))
    project_buffers[3], mix_far = barrier((project_buffers[3], mix_far))
    down_low = turned(first, 3, 5, "z", project_buffers[3])
    down_high = turned(second, 0, 2, "x", up_buffers[3])
    output_far = send(
        after(output_near, project_buffers[3], up_buffers[3]), flipped("y", 1)
    )

    scalars = jnp.stack([spot.z, spot.x, spot.sign, core, spot.yl]).astype(jnp.int32)
    project_full = place(attention_weight, 0, 3, ("z",), project_buffers, scalars)
    mix_full = place_halves(attention_weight[3], mix_near, mix_far, scalars)
    up_full = place(feedforward_weight, 0, 1, ("x",), up_buffers, scalars)[0]

    def down_placed(activated):
        low, high, _ = barrier((down_low[3], down_high[3], activated))
        buffers = [*down_low[:3], low, *down_high[:3], high]
        return place(feedforward_weight, 1, 1, ("z", "x"), buffers, scalars)[0]

    output_full = place_halves(output_table, output_near, output_far, scalars)

    context_far = send(
        after(jnp.where(settled, context_arrived, context_own), output_far), by("y", 2)
    )

    allowed = allowed_mask(window_segments, layout).astype(F32)
    after_block, normed_three, lefts, saved_state = layer_forward(
        residual,
        project_full,
        mix_full,
        up_full,
        down_placed,
        norm_gains,
        allowed,
        (
            (mix_full,),
            (down_low[1], down_high[1], output_near),
            (up_full, down_low[2], down_high[2]),
            (output_far,),
        ),
    )
    heads, totals, mixed_low, after_attention, pre_act, activated, down_full = saved_state
    left_one, left_two, left_three = lefts
    loss_local, grad_logits = head_loss(
        normed_three, output_full, window_tokens, window_segments, keep_flag, spot
    )

    part = contract(grad_logits, output_full, 1, 1)
    other = swap_core(part)
    output_ring = ring_y(
        spot, 512, (left_three, grad_logits, (length, 512), lambda j, half: (0, half), 1)
    )
    grad_block, block_low, left_block, norm_three = norm_backward(
        4, norm_gains, after_block, part, after(other, output_ring.total)
    )
    down_grad = chunk_product(
        [(left_block[None, None], activated, (length, 512), lambda j, s: (0, j), 4)],
        (1, 1, *left_block.shape),
        512,
        jnp.zeros((1,), jnp.int32),
        None,
        pltpu.HBM,
    )
    down_z = scatter_z(down_grad)
    block_low, output_one = barrier((after(block_low, down_grad), output_ring.arrive()))
    output_ring.add(output_one)
    block_low = after(block_low, output_ring.total)

    grad_pre, part = feedforward_backward(block_low, down_full, pre_act, up_full)
    part, output_two = barrier((part, output_ring.arrive()))
    other = swap_core(part)
    up_ring = ring_x(spot, left_two, grad_pre, 512)
    output_ring.add(output_two)
    grad_attention, attention_low, left_attention, norm_two = norm_backward(
        2,
        norm_gains,
        after_attention,
        part,
        after(other, up_ring.total, output_ring.total),
        grad_block,
    )
    grad_mixed = jnp.dot(attention_low, mix_full, preferred_element_type=F32).astype(BF16)
    grad_projected = attention_backward(heads, allowed, totals, grad_mixed)
    grad_projected, up_one, output_three, context_far = barrier(
        (grad_projected, up_ring.arrive(), output_ring.arrive(), context_far)
    )
    up_ring.add(up_one)
    output_ring.add(output_three)
    output_y = output_ring.total
    grad_projected = after(grad_projected, up_ring.total)
    part = jnp.einsum("ste,sde->td", grad_projected, project_full, preferred_element_type=F32)
    other = swap_core(part)
    project_ring = ring_y(
        spot,
        256,
        (left_one, grad_projected, (1, length, 256), lambda j, half: (j, 0, half), 3),
        (left_attention, mixed_low, (length, 256), lambda j, half: (0, half), 1),
    )
    grad_residual, _, left_residual, norm_one = norm_backward(
        0, norm_gains, residual, part, after(other, project_ring.total), grad_attention
    )

    context_far = context_far + 0.0 * local_seconds
    context = jnp.concatenate([context_near, context_far], axis=1).astype(BF16)

    def columns_of(half):
        side = jnp.where(half == 0, grad_residual[:, : 2 * width], grad_residual[:, 2 * width :])
        return own_quarter(side, core)

    own_grad = jnp.concatenate([columns_of(yh), columns_of(1 - yh)], axis=1)
    own_high = own_grad.astype(BF16)
    own_low = (own_grad - own_high.astype(F32)).astype(BF16)
    hot = (jnp.arange(embed_table.shape[0])[:, None] == window_tokens[None, :]).astype(BF16)
    embed_grad = jnp.dot(hot, own_high, preferred_element_type=F32) + jnp.dot(
        hot, own_low, preferred_element_type=F32
    )
    embed_z = scatter_z(embed_grad)
    condition_ring = ring_x(spot, left_residual, context, 512)
    norms_grad = jnp.concatenate([norm_one, norm_two, norm_three])

    token = condition_ring.total

    def step(ring_here):
        nonlocal token
        arrived, _ = barrier((ring_here.arrive(), token))
        ring_here.add(arrived)
        token = ring_here.total
        return token

    norms_at = [("x", 1), ("x", 2), ("y", 1), ("y", 2), ("z", 1), ("z", 2)]
    norms_out = []

    def norms_send():
        axis, bit = norms_at.pop(0)
        norms_out.append(send(norms_grad, flipped(axis, bit)))

    def norms_step():
        nonlocal norms_grad, token
        arrived, _ = barrier((norms_out.pop(), token))
        norms_grad = norms_grad + arrived
        token = norms_grad
        if norms_at:
            norms_send()

    step(up_ring)
    step(condition_ring)
    step(project_ring)
    up_x = step(up_ring)
    step(condition_ring)
    down_ring = ring_of(spot, "x", after(down_z, token))
    step(project_ring)
    condition_x = step(condition_ring)
    up_zring = ring_of(spot, "z", jnp.concatenate([up_x, condition_x], axis=1))
    norms_send()
    step(down_ring)
    step(up_zring)
    norms_step()
    step(down_ring)
    project_y = step(project_ring)
    project_zring = ring_of(spot, "z", jnp.concatenate([output_y, project_y], axis=1))
    step(up_zring)
    step(down_ring)
    embed_ring = ring_of(spot, "x", after(embed_z, token))
    norms_step()
    step(project_zring)
    step(up_zring)
    up_z, down_x = up_zring.total, down_ring.total
    last = direct_y(
        spot,
        jnp.concatenate(
            [
                up_z[:, :1024],
                down_x[:, :1024],
                up_z[:, 2048:2304],
                up_z[:, 1024:2048],
                down_x[:, 1024:],
                up_z[:, 2304:],
            ],
            axis=1,
        ),
        32,
    )
    step(embed_ring)
    norms_step()
    step(project_zring)
    step(embed_ring)
    norms_step()
    step(embed_ring)
    embed_sum = direct_y(spot, embed_ring.total, 64)
    norms_step()
    step(project_zring)
    last_y = direct_sum("x", spot.x, project_zring.total)
    norms_step()
    rings = (output_ring, up_ring, condition_ring, project_ring, down_ring, up_zring, project_zring, embed_ring)
    assert all(r.step == 4 for r in rings) and not norms_at and not norms_out
    output_sum, project_sum, mix_sum = last_y[:, :512], last_y[:, 512:1280], last_y[:, 1280:]
    up_sum, down_sum, condition_sum = last[:, :1024], last[:, 1024:2048], last[:, 2048:]
    dp_rank = ((spot.z * 4 + spot.x) * 2 + spot.yl) * 2 + core
    norms_share = lax.dynamic_slice_in_dim(norms_grad, dp_rank * 16, 16, 1)

    sums = [output_sum, down_sum, up_sum, mix_sum, project_sum, condition_sum, embed_sum]
    squares = 0.5 * jnp.sum((norms_share * SQUARE_SCALE) ** 2)
    for piece in sums:
        squares = squares + jnp.sum((piece * SQUARE_SCALE) ** 2)
    scalars = jnp.stack([0.5 * loss_local, squares, 0.5 * local_seconds])
    flat = [piece.reshape(2, 16, -1) for piece in sums[:-1]] + [sums[-1].reshape(2, 16, 512)]
    flat = jnp.concatenate(flat, axis=2)
    mine = lax.dynamic_index_in_dim(flat, core, 0, False)
    theirs = swap_core(lax.dynamic_index_in_dim(flat, 1 - core, 0, False))
    scalars = pair_sum(jnp.broadcast_to(scalars[:, None], (3, 128)))
    scalars = sum_of_four(scalars, "x", spot.x)
    scalars = sum_of_four(after(scalars, theirs), "z", spot.z)
    scalars = sum_of_four(scalars, "y", spot.y)
    loss_total, seconds_total = scalars[0, 0], scalars[2, 0]
    inverse = 1.0 / seconds_total
    gradient_norm = jnp.sqrt(scalars[1, 0]) * (inverse / SQUARE_SCALE)
    clip_factor = CLIP_NORM / jnp.maximum(gradient_norm, CLIP_NORM)

    low_side = jnp.where(core == 0, mine, theirs)
    high_side = jnp.where(core == 0, theirs, mine)

    def share(start, stop):
        return low_side[:, start:stop], high_side[:, start:stop]

    output_share = jnp.concatenate(share(0, 512), axis=1)
    feedforward_share = jnp.stack(
        [jnp.concatenate(share(1536, 2560), axis=1), jnp.concatenate(share(512, 1536), axis=1)]
    )
    mix_low, mix_high = share(2560, 2816)
    project_low, project_high = share(2816, 3584)
    attention_share = jnp.stack(
        [
            jnp.concatenate(
                [project_low[:, 256 * k : 256 * k + 256], project_high[:, 256 * k : 256 * k + 256]],
                axis=1,
            )
            for k in range(3)
        ]
        + [jnp.concatenate([mix_low, mix_high], axis=1)]
    )
    condition_share = jnp.concatenate(share(3584, 3840), axis=1)
    embed_share = jnp.concatenate([part.reshape(32, 256) for part in share(3840, 4352)], axis=1)

    shares = (
        embed_share,
        condition_share,
        attention_share,
        feedforward_share,
        output_share,
        norms_share,
    )
    masters = (
        embed_master,
        condition_master,
        attention_master,
        feedforward_master,
        output_master,
        norms_master,
    )
    firsts = (
        embed_first,
        condition_first,
        attention_first,
        feedforward_first,
        output_first,
        norms_first,
    )
    seconds_old = (
        embed_second,
        condition_second,
        attention_second,
        feedforward_second,
        output_second,
        norms_second,
    )
    rates = (RATE_TABLE, RATE_MATRIX, RATE_MATRIX, RATE_MATRIX, RATE_MATRIX, RATE_NORMS)
    decays = (WEIGHT_DECAY, WEIGHT_DECAY, WEIGHT_DECAY, WEIGHT_DECAY, WEIGHT_DECAY, 0.0)
    outputs = [loss_total, seconds_total, gradient_norm]
    for slot in range(6):
        outputs += adam_step(
            shares[slot] * inverse * clip_factor,
            masters[slot],
            firsts[slot],
            seconds_old[slot],
            rates[slot],
            decays[slot],
        )
    return tuple(outputs)


def solution(mesh):
    torus = Mesh(mesh.devices.reshape(SIZES), AXES)
    table, slotted = P(DP, "yh"), P(None, DP, "yh")
    state = (table, table, slotted, slotted, table, P(None, DP))
    results = tuple(spec for spec in state for _ in range(3))
    return jax.shard_map(
        local,
        mesh=torus,
        in_specs=(
            P(DP),
            P(DP),
            P(),
            P(DP),
            P(DP),
            table,
            P(None, "yh"),
            P(None, "yh"),
            P(None, None, "yh"),
            P(None, None, "yh"),
            P(None, "yh"),
            P(),
        )
        + state * 3,
        out_specs=(P(), P(), P()) + results,
        check_vma=False,
    )
```

```python
import functools

import jax
import jax.numpy as jnp
import numpy as np
from jax import lax
from jax.experimental import pallas as pl
from jax.experimental.pallas import tpu as pltpu
from jax.sharding import Mesh
from jax.sharding import PartitionSpec as P

HEAD_DIM = 64
BLK = 64
CLIPS_DEV = 4
STEP = 10


LAYER_EPS = 1e-05
SAMPLE_RATE = 44100.0
LOG_TWO_NATS = 0.6931471805599453
CLIP_NORM = 1.0
BETA_FIRST = 0.9
BETA_SECOND = 0.95
ADAM_EPSILON = 1e-08
WEIGHT_DECAY = 0.01
RATE_MATRIX = 0.1
RATE_TABLE = 1.0
RATE_NORMS = 1.0
SQUARE_SCALE = 2.0**-9

AXES = ("z", "x", "yl", "c", "yh")
SIZES = (4, 4, 2, 2, 2)
DP = ("z", "x", "yl", "c")
MIB = 1024 * 1024
QUERY_ROWS = 256
BF16 = jnp.bfloat16
F32 = jnp.float32


def send(value, move):
    pairs = []
    for index in range(int(np.prod(SIZES))):
        z, x, yl, c, yh = (int(i) for i in np.unravel_index(index, SIZES))
        target = move(z, x, yh * 2 + yl, c)
        if target is not None:
            z, x, y, c = target
            y %= 4
            at = (z % 4, x % 4, y % 2, c, y // 2)
            pairs.append((index, int(np.ravel_multi_index(at, SIZES))))
    return lax.ppermute(value, AXES, pairs)


def swap_core(value):
    return send(value, lambda z, x, y, c: (z, x, y, 1 - c))


def pair_sum(value):
    return value + swap_core(value)


def ring(axis):
    def move(z, x, y, c):
        step = 1 - 2 * c
        return {"z": (z + step, x, y, c), "x": (z, x + step, y, c), "y": (z, x, y + step, c)}[axis]

    return move


def by(axis, count):
    def move(z, x, y, c):
        return {"z": (z + count, x, y, c), "x": (z, x + count, y, c), "y": (z, x, y + count, c)}[axis]

    return move


def flipped(axis, bit):
    def move(z, x, y, c):
        return {"z": (z ^ bit, x, y, c), "x": (z, x ^ bit, y, c), "y": (z, x, y ^ bit, c)}[axis]

    return move


def after(value, *earlier):
    return lax.optimization_barrier((value, *earlier))[0]


def pieces_kernel(s_ref, *refs):
    width = 0
    for ref in refs[:-1]:
        refs[-1][:, width : width + ref.shape[-1]] = ref[0].astype(F32)
        width += ref.shape[-1]


def pieces_of(attention_weight, feedforward_weight, index):
    narrow, wide = attention_weight.shape[2] // 2, feedforward_weight.shape[2] // 2
    specs = [pl.BlockSpec((1, 64, narrow), lambda g, s, k=k: (k, s[0], s[1])) for k in range(3)]
    specs += [pl.BlockSpec((1, 64, wide), lambda g, s, k=k: (k, s[0], s[1])) for k in (1, 0)]
    width = 3 * narrow + 2 * wide
    return pl.pallas_call(
        pieces_kernel,
        grid_spec=pltpu.PrefetchScalarGridSpec(
            num_scalar_prefetch=1,
            grid=(1,),
            in_specs=specs,
            out_specs=pl.BlockSpec((64, width), lambda g, s: (0, 0)),
        ),
        out_shape=jax.ShapeDtypeStruct((64, width), F32),
        compiler_params=pltpu.CompilerParams(vmem_limit_bytes=8 * MIB),
        cost_estimate=estimate(1, 1),
    )(index, *in_hbm(*[attention_weight] * 3, *[feedforward_weight] * 2))


def own_quarter(half, core):
    width = half.shape[-1] // 2
    return jnp.where(core == 0, half[..., :width], half[..., width:])


def place_kernel(rings, s_ref, native_ref, *rest):
    out_ref = rest[-1]
    width = native_ref.shape[-1]
    part = width // len(rings)
    out_ref[0, :, :width] = native_ref[0]
    z, x, sign = s_ref[0], s_ref[1], s_ref[2]
    for r, axis in enumerate(rings):
        lanes = slice(width + r * part, width + (r + 1) * part)
        for j in range(4):
            for i in range(4):
                z_at = lax.rem(z - sign * (j if axis == "z" else i) + 8, 4)
                x_at = lax.rem(x - sign * (j if axis == "x" else i) + 8, 4)
                rows = pl.ds(pl.multiple_of(z_at * 256 + x_at * 64, 64), 64)
                out_ref[0, rows, lanes] = rest[4 * r + j][i].astype(BF16)


def place(native, first_slot, slots, rings, buffers, scalars):
    rows, width = native.shape[1], native.shape[2] // 2
    block = pl.BlockSpec((4, 64, width // len(rings)), lambda k, s: (0, 0, k))
    return pl.pallas_call(
        functools.partial(place_kernel, rings),
        grid_spec=pltpu.PrefetchScalarGridSpec(
            num_scalar_prefetch=1,
            grid=(slots,),
            in_specs=[pl.BlockSpec((1, rows, width), lambda k, s: (first_slot + k, 0, s[3]))]
            + [block] * len(buffers),
            out_specs=pl.BlockSpec((1, rows, 2 * width), lambda k, s: (k, 0, 0)),
        ),
        out_shape=jax.ShapeDtypeStruct((slots, rows, 2 * width), BF16),
        compiler_params=pltpu.CompilerParams(vmem_limit_bytes=24 * MIB),
        cost_estimate=estimate(1, 1),
    )(scalars, *in_hbm(native), *buffers)


def place_halves_kernel(s_ref, native_ref, near_ref, far_ref, out_ref):
    half, width = near_ref.shape
    out_ref[:, :width] = native_ref[...]
    near = s_ref[4]
    out_ref[pl.ds(pl.multiple_of(near * half, 64), half), width:] = near_ref[...].astype(BF16)
    out_ref[pl.ds(pl.multiple_of((1 - near) * half, 64), half), width:] = far_ref[...].astype(BF16)


def place_halves(native, near, far, scalars):
    rows, width = native.shape[0], native.shape[1] // 2
    whole = pl.BlockSpec((rows // 2, width), lambda k, s: (0, 0))
    return pl.pallas_call(
        place_halves_kernel,
        grid_spec=pltpu.PrefetchScalarGridSpec(
            num_scalar_prefetch=1,
            grid=(1,),
            in_specs=[pl.BlockSpec((rows, width), lambda k, s: (0, s[3])), whole, whole],
            out_specs=pl.BlockSpec((rows, 2 * width), lambda k, s: (0, 0)),
        ),
        out_shape=jax.ShapeDtypeStruct((rows, 2 * width), BF16),
        compiler_params=pltpu.CompilerParams(vmem_limit_bytes=12 * MIB),
        cost_estimate=pl.CostEstimate(
            flops=0, bytes_accessed=rows * width * 10, transcendentals=0
        ),
    )(scalars, *in_hbm(native), near, far)


def direct(value, axis):
    return jnp.stack([value] + [send(value, by(axis, k)) for k in (1, 2, 3)])


def around(buffer, axis):
    buffers = [buffer]
    for _ in range(3):
        buffers.append(send(buffers[-1], ring(axis)))
    return buffers


class Ring:
    def __init__(self, axis, place_at, sign, part):
        self.axis, self.place_at, self.sign, self.part = axis, place_at, sign, part
        self.step = 1
        self.total = part(lax.rem(place_at - sign + 8, 4))

    def arrive(self):
        return send(self.total, ring(self.axis))

    def add(self, arrived):
        self.step += 1
        own = lax.rem(self.place_at - self.step * self.sign + 8, 4)
        self.total = self.part(own, arrived)


def ring_of(spot, axis, grad):
    view = grad.reshape(1, 4, -1, grad.shape[1])

    def part(k, arrived=None):
        return chunk_added(view, k.astype(jnp.int32)[None], arrived)

    return Ring(axis, spot.z if axis == "z" else spot.x, spot.sign, part)


def added(product, arrived):
    return product if arrived is None else product + arrived


def ring_x(spot, left, right, tile):
    left = left.reshape(4, 4, -1, left.shape[-1])
    segment = (left, right, (right.shape[0], tile), lambda j, s: (0, j), right.shape[1] // tile)

    def part(k, arrived=None):
        index = k.astype(jnp.int32)[None]
        return chunk_product([segment], (4, 1, *left.shape[2:]), tile, index, arrived)

    return Ring("x", spot.x, spot.sign, part)


def ring_y(spot, tile, *segments):
    tokens = segments[0][0].shape[-1]
    rest = segments[0][0].shape[0] // 32

    def part(k, arrived=None):
        half = jnp.where(lax.div(k, 2) == spot.yh, 0, 1)
        index = jnp.stack([lax.rem(k, 2), half]).astype(jnp.int32)
        turned = [
            (left.reshape(16, 2, rest, tokens), right, block, lambda j, s, at=at: at(j, s[1]), tiles)
            for left, right, block, at, tiles in segments
        ]
        return chunk_product(turned, (16, 1, rest, tokens), tile, index, arrived)

    return Ring("y", spot.y, spot.sign, part)


def whole_product(left, right):
    segment = (left[None, None], right, (right.shape[0], 512), lambda j, s: (0, j), right.shape[1] // 512)
    none = jnp.zeros((1,), jnp.int32)
    return chunk_product([segment], (1, 1, *left.shape), 512, none, None, pltpu.HBM)


def scatter_z(grad):
    return lax.psum_scatter(grad, "z", scatter_dimension=0, tiled=True)


def direct_y(spot, grad, rows):
    width = grad.shape[1] // 2
    view = grad.reshape(-1, 2, rows, 2 * width)
    same = lax.dynamic_index_in_dim(view, spot.yl, 1, False)
    other = lax.dynamic_index_in_dim(view, 1 - spot.yl, 1, False)
    near = send(other[..., :width], flipped("y", 1))
    far = send(other[..., width:], flipped("y", 3))
    across = send(same[..., width:], flipped("y", 2))
    return ((same[..., :width] + near) + (far + across)).reshape(-1, width)


def direct_sum(axis, place_at, grad, outer=1):
    view = grad.reshape(outer, 4, grad.shape[0] // (4 * outer), grad.shape[1])
    parts = [
        send(lax.dynamic_index_in_dim(view, lax.rem(place_at + k, 4), 1, False), by(axis, k))
        for k in (1, 2, 3)
    ]
    own = lax.dynamic_index_in_dim(view, place_at, 1, False)
    return ((own + parts[0]) + (parts[1] + parts[2])).reshape(-1, grad.shape[1])


def turned(value):
    return lax.optimization_barrier(value.T)


class Spot:
    def __init__(self):
        self.z, self.x, self.yl, self.c, self.yh = (lax.axis_index(a) for a in AXES)
        self.y = self.yh * 2 + self.yl
        self.sign = 1 - 2 * self.c


def sum_of_four(value, axis, place_at):
    pieces = [value] + [send(value, by(axis, k)) for k in (1, 2, 3)]
    total = None
    for at in range(4):
        back = lax.rem(place_at - at + 4, 4)
        part = pieces[3]
        for k in (2, 1, 0):
            part = jnp.where(back == k, pieces[k], part)
        total = part if total is None else total + part
    return total


def contract(left_side, right_side, left_dim, right_dim):
    return lax.dot_general(
        left_side,
        right_side,
        (((left_dim,), (right_dim,)), ((), ())),
        preferred_element_type=jnp.float32,
    )


def attention_forward_kernel(heads_ref, mask_ref, out_ref, total_ref):
    length = heads_ref.shape[1]
    for half in range(2):
        lanes = slice(half * HEAD_DIM, (half + 1) * HEAD_DIM)
        keys, values = heads_ref[1, :, lanes], heads_ref[2, :, lanes]
        scaled = heads_ref[0, :, lanes] * jnp.asarray(HEAD_DIM ** (-0.5), BF16)
        for start in range(0, length, QUERY_ROWS):
            stop = start + QUERY_ROWS
            scores = contract(scaled[start:stop], keys[:stop], 1, 1)
            scores = jnp.where(mask_ref[start:stop, :stop] > 0, scores, -1e30)
            top = jnp.max(scores, axis=-1, keepdims=True)
            weights = jnp.exp(scores - top)
            sums = jnp.sum(weights, axis=-1, keepdims=True)
            weights = (weights * (1.0 / sums)).astype(BF16)
            out_ref[start:stop, lanes] = contract(weights, values[:stop], 1, 0).astype(BF16)
            total_ref[0, start:stop, half : half + 1] = top + jnp.log(sums)


def attention_backward_kernel(heads_ref, mask_ref, total_ref, grad_ref, out_ref, keys_acc, values_acc):
    length = heads_ref.shape[1]
    for half in range(2):
        lanes = slice(half * HEAD_DIM, (half + 1) * HEAD_DIM)
        keys, values = heads_ref[1, :, lanes], heads_ref[2, :, lanes]
        scaled = heads_ref[0, :, lanes] * jnp.asarray(HEAD_DIM ** (-0.5), BF16)
        for start in range(length - QUERY_ROWS, -1, -QUERY_ROWS):
            stop = start + QUERY_ROWS
            queries, grad = scaled[start:stop], grad_ref[start:stop, lanes]
            scores = contract(queries, keys[:stop], 1, 1)
            scores = jnp.where(mask_ref[start:stop, :stop] > 0, scores, -1e30)
            weights = jnp.exp(scores - total_ref[0, start:stop, half : half + 1])
            grad_values = contract(weights.astype(BF16), grad, 0, 0)
            grad_weights = contract(grad, values[:stop], 1, 1)
            total = jnp.sum(weights * grad_weights, axis=-1, keepdims=True)
            grad_scores = (weights * (grad_weights - total)).astype(BF16)
            grad_queries = contract(grad_scores, keys[:stop], 1, 0) * HEAD_DIM ** (-0.5)
            out_ref[0, start:stop, lanes] = grad_queries.astype(BF16)
            grad_keys = contract(grad_scores, queries, 0, 0)
            if stop == length:
                keys_acc[...] = grad_keys
                values_acc[...] = grad_values
            else:
                keys_acc[:stop] += grad_keys
                values_acc[:stop] += grad_values
        out_ref[1, :, lanes] = keys_acc[...].astype(BF16)
        out_ref[2, :, lanes] = values_acc[...].astype(BF16)


def estimate(flops, moved):
    return pl.CostEstimate(flops=flops, bytes_accessed=moved, transcendentals=0)


def in_hbm(*values):
    return [pltpu.with_memory_space_constraint(value, pltpu.HBM) for value in values]


def norm_forward_kernel(row, parts, base_ref, *rest):
    ins, outs = rest[: parts + 1], rest[parts + 1 :]
    gains_ref = ins[-1]
    values = base_ref[...]
    if parts:
        values = values + (ins[0][...] + ins[1][...])
        outs[2][...] = values
    centred = values - jnp.mean(values, axis=-1, keepdims=True)
    variance = jnp.mean(centred * centred, axis=-1, keepdims=True)
    normed = centred * lax.rsqrt(variance + LAYER_EPS) * gains_ref[row : row + 1] + gains_ref[row + 1 : row + 2]
    outs[0][...] = normed.astype(BF16)
    outs[1][...] = normed.T.astype(BF16)


def norm_forward(row, gains, base, parts=()):
    length, width = base.shape
    rows = 128
    block = pl.BlockSpec((rows, width), lambda g: (g, 0))
    turned = pl.BlockSpec((width, rows), lambda g: (0, g))
    shapes = [jax.ShapeDtypeStruct((length, width), BF16), jax.ShapeDtypeStruct((width, length), BF16)]
    if parts:
        shapes.append(jax.ShapeDtypeStruct((length, width), F32))
    return pl.pallas_call(
        functools.partial(norm_forward_kernel, row, len(parts)),
        grid=(length // rows,),
        in_specs=[block] * (1 + len(parts)) + [pl.BlockSpec(gains.shape, lambda g: (0, 0))],
        out_specs=[block, turned, block][: len(shapes)],
        out_shape=shapes,
        compiler_params=pltpu.CompilerParams(vmem_limit_bytes=14 * MIB),
        cost_estimate=estimate(1, 1),
    )(base, *parts, gains)


def norm_backward_kernel(row, has_base, values_ref, part_ref, other_ref, gains_ref, *rest):
    if has_base:
        base_ref, rest = rest[0], rest[1:]
    out_ref, low_ref, turned_ref, sums_ref = rest
    values = values_ref[...]
    grad = part_ref[...] + other_ref[...]
    centred = values - jnp.mean(values, axis=-1, keepdims=True)
    scale = lax.rsqrt(jnp.mean(centred * centred, axis=-1, keepdims=True) + LAYER_EPS)
    normed = centred * scale
    gained = grad * gains_ref[row : row + 1]
    inner = gained - jnp.mean(gained, axis=-1, keepdims=True)
    inner = scale * (inner - normed * jnp.mean(gained * normed, axis=-1, keepdims=True))
    if has_base:
        inner = base_ref[...] + inner
    out_ref[...] = inner
    low_ref[...] = inner.astype(BF16)
    turned_ref[...] = inner.T.astype(BF16)
    sums = jnp.concatenate(
        [jnp.sum(grad * normed, axis=0, keepdims=True), jnp.sum(grad, axis=0, keepdims=True)], axis=0
    )

    @pl.when(pl.program_id(0) == 0)
    def _():
        sums_ref[...] = sums

    @pl.when(pl.program_id(0) > 0)
    def _():
        sums_ref[...] += sums


def norm_backward(row, gains, values, part, other, base=None):
    length, width = values.shape
    rows = 128
    block = pl.BlockSpec((rows, width), lambda g: (g, 0))
    operands = [values, part, other, gains] + ([] if base is None else [base])
    specs = [block] * 3 + [pl.BlockSpec(gains.shape, lambda g: (0, 0))] + ([] if base is None else [block])
    return pl.pallas_call(
        functools.partial(norm_backward_kernel, row, base is not None),
        grid=(length // rows,),
        in_specs=specs,
        out_specs=[
            block,
            block,
            pl.BlockSpec((width, rows), lambda g: (0, g)),
            pl.BlockSpec((2, width), lambda g: (0, 0)),
        ],
        out_shape=[
            jax.ShapeDtypeStruct((length, width), F32),
            jax.ShapeDtypeStruct((length, width), BF16),
            jax.ShapeDtypeStruct((width, length), BF16),
            jax.ShapeDtypeStruct((2, width), F32),
        ],
        compiler_params=pltpu.CompilerParams(vmem_limit_bytes=16 * MIB),
        cost_estimate=estimate(1, 1),
    )(*operands)


def chunk_kernel(bounds, plain, has_recv, s_ref, *rest):
    out_ref = rest[-1]
    for n, (start, stop) in enumerate(bounds):
        left_ref, right_ref = rest[2 * n], rest[2 * n + 1]

        @pl.when((pl.program_id(0) >= start) & (pl.program_id(0) < stop))
        def _(left_ref=left_ref, right_ref=right_ref):
            if plain[n]:
                total = left_ref[...].reshape(out_ref.shape[0], left_ref.shape[-1])
                total = jnp.concatenate([total, total], axis=1)
            else:
                left = left_ref[...].reshape(out_ref.shape[0], left_ref.shape[-1])
                right = right_ref[...].reshape(right_ref.shape[-2:])
                total = jnp.dot(left, right, preferred_element_type=F32)
            if has_recv:
                total += rest[2 * len(bounds)][...]
            out_ref[...] = total


def chunk_product(segments, left_block, tile, index, arrived, place_for=jax.ShapeDtypeStruct):
    rows = int(np.prod(left_block[:-1]))
    out_spec = pl.BlockSpec((rows, tile), lambda j, s: (0, j))
    operands, specs, bounds, start = [], [], [], 0
    for left, right, right_block, right_at, tiles in segments:

        def at(j, s, start=start, tiles=tiles, right_at=right_at):
            return right_at(jnp.clip(j - start, 0, tiles - 1), s)

        operands += [left, index if right is None else right]
        specs += [
            pl.BlockSpec((*left_block[:-1], left.shape[-1]), lambda j, s: (0, s[0], 0, 0)),
            pl.BlockSpec(memory_space=pltpu.SMEM) if right is None else pl.BlockSpec(right_block, at),
        ]
        bounds.append((start, start + tiles))
        start += tiles
    extra = [] if arrived is None else [arrived]
    return pl.pallas_call(
        functools.partial(
            chunk_kernel, tuple(bounds), [seg[1] is None for seg in segments], arrived is not None
        ),
        grid_spec=pltpu.PrefetchScalarGridSpec(
            num_scalar_prefetch=1,
            grid=(start,),
            in_specs=specs + [out_spec] * len(extra),
            out_specs=out_spec,
        ),
        out_shape=place_for((rows, tile * start), F32),
        compiler_params=pltpu.CompilerParams(vmem_limit_bytes=16 * MIB),
        cost_estimate=estimate(1, 1),
    )(index, *operands, *extra)


def add_kernel(s_ref, own_ref, *rest):
    out_ref = rest[-1]
    total = own_ref[0, 0]
    for arrived_ref in rest[:-1]:
        total = total + arrived_ref[...]
    out_ref[...] = total


def chunk_added(view, index, arrived):
    rows, width = view.shape[2:]
    tile = width // 2
    out_spec = pl.BlockSpec((rows, tile), lambda j, s: (0, j))
    extra = [] if arrived is None else [arrived]
    return pl.pallas_call(
        add_kernel,
        grid_spec=pltpu.PrefetchScalarGridSpec(
            num_scalar_prefetch=1,
            grid=(2,),
            in_specs=[pl.BlockSpec((1, 1, rows, tile), lambda j, s: (0, s[0], 0, j))]
            + [out_spec] * len(extra),
            out_specs=out_spec,
        ),
        out_shape=jax.ShapeDtypeStruct((rows, width), F32),
        compiler_params=pltpu.CompilerParams(vmem_limit_bytes=8 * MIB),
        cost_estimate=estimate(1, 1),
    )(index, view, *extra)


def attention_forward(heads, mask):
    length, width = heads.shape[1:]
    return pl.pallas_call(
        attention_forward_kernel,
        grid=(width // 128,),
        in_specs=[
            pl.BlockSpec((3, length, 128), lambda g: (0, 0, g)),
            pl.BlockSpec((length, length), lambda g: (0, 0)),
        ],
        out_specs=[
            pl.BlockSpec((length, 128), lambda g: (0, g)),
            pl.BlockSpec((1, length, 2), lambda g: (g, 0, 0)),
        ],
        out_shape=[
            jax.ShapeDtypeStruct((length, width), BF16),
            jax.ShapeDtypeStruct((width // 128, length, 2), F32),
        ],
        compiler_params=pltpu.CompilerParams(vmem_limit_bytes=16 * MIB),
        cost_estimate=estimate(1, 1),
    )(heads, mask)


def attention_backward(heads, mask, totals, grad_mixed):
    length, width = heads.shape[1:]
    return pl.pallas_call(
        attention_backward_kernel,
        grid=(width // 128,),
        in_specs=[
            pl.BlockSpec((3, length, 128), lambda g: (0, 0, g)),
            pl.BlockSpec((length, length), lambda g: (0, 0)),
            pl.BlockSpec((1, length, 2), lambda g: (g, 0, 0)),
            pl.BlockSpec((length, 128), lambda g: (0, g)),
        ],
        out_specs=pl.BlockSpec((3, length, 128), lambda g: (0, 0, g)),
        out_shape=jax.ShapeDtypeStruct((3, length, width), BF16),
        scratch_shapes=[pltpu.VMEM((length, HEAD_DIM), F32), pltpu.VMEM((length, HEAD_DIM), F32)],
        compiler_params=pltpu.CompilerParams(vmem_limit_bytes=16 * MIB),
        cost_estimate=estimate(1, 1),
    )(heads, mask, totals, grad_mixed)


def feedforward_backward_kernel(block_ref, down_ref, pre_ref, up_ref, grad_pre_ref, normed_ref):
    grad_activated = jnp.dot(block_ref[...], down_ref[...], preferred_element_type=F32)
    pre = pre_ref[...]
    slope = 0.7978845608028654
    bent = jnp.tanh(slope * (pre + 0.044715 * pre * pre * pre))
    inner = slope * (1.0 + 3.0 * 0.044715 * pre * pre)
    factor = 0.5 * (1.0 + bent) + 0.5 * pre * (1.0 - bent * bent) * inner
    grad_pre = (grad_activated * factor).astype(BF16)
    grad_pre_ref[...] = grad_pre
    part = contract(grad_pre, up_ref[...], 1, 1)

    @pl.when(pl.program_id(0) == 0)
    def _():
        normed_ref[...] = part

    @pl.when(pl.program_id(0) > 0)
    def _():
        normed_ref[...] += part


def feedforward_backward(block_low, down_full, pre_act, up_full):
    length, hidden = pre_act.shape
    width, tile = block_low.shape[1], 512
    return pl.pallas_call(
        feedforward_backward_kernel,
        grid=(hidden // tile,),
        in_specs=[
            pl.BlockSpec((length, width), lambda g: (0, 0)),
            pl.BlockSpec((width, tile), lambda g: (0, g)),
            pl.BlockSpec((length, tile), lambda g: (0, g)),
            pl.BlockSpec((width, tile), lambda g: (0, g)),
        ],
        out_specs=[
            pl.BlockSpec((length, tile), lambda g: (0, g)),
            pl.BlockSpec((length, width), lambda g: (0, 0)),
        ],
        out_shape=[
            jax.ShapeDtypeStruct((length, hidden), BF16),
            jax.ShapeDtypeStruct((length, width), F32),
        ],
        compiler_params=pltpu.CompilerParams(vmem_limit_bytes=22 * MIB),
        cost_estimate=estimate(1, 1),
    )(*in_hbm(block_low, down_full, pre_act, up_full))


def allowed_mask(segments, layout):
    length = segments.shape[0]
    position = jnp.arange(length)
    blocks = layout.shape[0]
    block_open = (
        jnp.broadcast_to(layout[:, None, :, None], (blocks, BLK, blocks, BLK)).reshape(
            length, length
        )
        > 0
    )
    causal = position[None, :] <= position[:, None]
    return causal & (segments[:, None] == segments[None, :]) & block_open


def layer_forward(residual, project_weight, mix_weight, up_weight, down_weight, norm_gains, mask, early):
    normed_one, left_one = norm_forward(0, norm_gains, residual)
    heads = jnp.einsum(
        "td,sde->ste", normed_one, project_weight, preferred_element_type=jnp.float32
    ).astype(jnp.bfloat16)
    heads = after(heads, *early[0])
    mixed_low, totals = attention_forward(heads, mask)
    mixed_low = after(mixed_low, *early[1])
    part = contract(mixed_low, mix_weight, 1, 1)
    other = after(swap_core(part), *early[2])
    normed_two, left_two, after_attention = norm_forward(2, norm_gains, residual, (part, other))
    pre_act = jnp.dot(normed_two, up_weight, preferred_element_type=jnp.float32)
    activated = jax.nn.gelu(pre_act).astype(jnp.bfloat16)
    activated = after(activated, *early[3])
    down_full = down_weight(activated)
    part = contract(activated, down_full, 1, 1)
    normed_three, left_three, after_block = norm_forward(
        4, norm_gains, after_attention, (part, swap_core(part))
    )
    saved_state = (heads, totals, mixed_low, after_attention, pre_act, activated, down_full)
    return (after_block, normed_three, (left_one, left_two, left_three), saved_state)


def head_loss(normed_three, output_table, code_tokens, segments, keep_flag, spot):
    logits = jnp.dot(normed_three, output_table, preferred_element_type=jnp.float32)
    width = output_table.shape[1]
    quarter = width // 2
    targets = jnp.concatenate([code_tokens[1:], code_tokens[-1:]])
    column = jnp.arange(width)
    code = jnp.where(
        column < quarter,
        spot.yh * width + spot.c * quarter + column,
        (1 - spot.yh) * width + spot.c * quarter + column - quarter,
    )
    target_hit = code[None, :] == targets[:, None]
    row_top = jnp.max(logits, axis=1)
    row_sums = jnp.sum(jnp.exp(logits - row_top[:, None]), axis=1)
    picked = jnp.sum(jnp.where(target_hit, logits, 0.0), axis=1)
    other = swap_core(jnp.stack([row_top, row_sums, picked]))
    both_top = jnp.maximum(row_top, other[0])
    both_sums = row_sums * jnp.exp(row_top - both_top) + other[1] * jnp.exp(other[0] - both_top)
    log_norm = both_top + jnp.log(both_sums)
    next_segment = jnp.concatenate([segments[1:], jnp.full((1,), -1, jnp.int32)])
    counted = ((segments == next_segment) & (segments < CLIPS_DEV)).astype(jnp.float32) * keep_flag
    loss_local = jnp.sum(counted * (log_norm - (picked + other[2]))) / LOG_TWO_NATS
    grad_logits = (counted / LOG_TWO_NATS)[:, None] * (
        jnp.exp(logits - log_norm[:, None]) - target_hit.astype(jnp.float32)
    )
    grad_low = grad_logits.astype(jnp.bfloat16)
    return (loss_local, grad_low)


def adam_step(gradient, master, first_old, second_old, step_rate, decay_rate):
    moment = BETA_FIRST * first_old + (1.0 - BETA_FIRST) * gradient
    variance = BETA_SECOND * second_old + (1.0 - BETA_SECOND) * gradient * gradient
    moment_hat = moment / (1.0 - BETA_FIRST**STEP)
    variance_hat = variance / (1.0 - BETA_SECOND**STEP)
    updated = master - step_rate * (
        moment_hat / (jnp.sqrt(variance_hat) + ADAM_EPSILON) + decay_rate * master
    )
    return (moment, variance, updated)


def local(
    code_tokens,
    segments,
    layout,
    durations,
    overflow,
    upper_context,
    embed_table,
    condition_weight,
    attention_weight,
    feedforward_weight,
    output_table,
    norm_gains,
    embed_master,
    condition_master,
    attention_master,
    feedforward_master,
    output_master,
    norms_master,
    embed_first,
    condition_first,
    attention_first,
    feedforward_first,
    output_first,
    norms_first,
    embed_second,
    condition_second,
    attention_second,
    feedforward_second,
    output_second,
    norms_second,
):
    spot = Spot()
    core, yh = spot.c, spot.yh
    settled = core == yh
    length = code_tokens.shape[0]

    keep_native = 1.0 - overflow[0].astype(jnp.float32)
    local_seconds = keep_native * jnp.sum(durations.astype(jnp.float32)) / SAMPLE_RATE
    native_ints = jnp.concatenate([code_tokens, segments, jnp.broadcast_to(overflow, (128,))])
    window_ints = jnp.where(settled, native_ints, swap_core(native_ints))
    window_tokens = window_ints[:length]
    window_segments = window_ints[length : 2 * length]
    keep_flag = 1.0 - window_ints[2 * length].astype(jnp.float32)

    def crossed(value):
        return send(value, lambda z, x, y, c: (z, x, 3 - y, c))

    block = spot.z * 4 + spot.x
    barrier = lax.optimization_barrier
    pieces = crossed(
        pieces_of(attention_weight, feedforward_weight, jnp.stack([block, core]).astype(jnp.int32))
    )
    quarter = attention_weight.shape[2] // 2

    embedded = jnp.take(embed_table, code_tokens, axis=0).astype(F32)
    half_width = embed_table.shape[1]
    embed_part = contract(upper_context, condition_weight, 1, 1)
    embed_part = jnp.concatenate(
        [
            embed_part[:, :half_width] + jnp.where(yh == 0, embedded, 0.0),
            embed_part[:, half_width:] + jnp.where(yh == 1, embedded, 0.0),
        ],
        axis=1,
    )
    width = half_width // 2
    context_own = own_quarter(upper_context, core).astype(F32)
    context_arrived = swap_core(own_quarter(upper_context, 1 - core).astype(F32))
    embed_part, pieces, context_arrived = barrier((embed_part, pieces, context_arrived))
    context_near = jnp.where(settled, context_own, context_arrived)
    from_other = send(
        embed_part,
        lambda z, x, y, c: (z, x, y ^ 2, c) if c != y // 2 else None,
    )
    first, second = [pieces[:, : 5 * quarter]], [pieces[:, 5 * quarter :]]
    for _ in range(3):
        first.append(send(first[-1], ring("x")))
        second.append(send(second[-1], ring("z")))
    window_sum = embed_part + from_other
    residual = jnp.where(settled, window_sum, swap_core(window_sum))

    def half_rows(native):
        halves = own_quarter(native, core).reshape(2, native.shape[0] // 2, -1)
        return lax.dynamic_index_in_dim(halves, 1 - spot.yl, 0, False).astype(F32)

    def turned(pieces, start, stop, axis, *earlier):
        columns = jnp.stack([piece[:, start * quarter : stop * quarter] for piece in pieces])
        return around(after(columns, *earlier), axis)

    up_buffers = turned(second, 2, 6, "x")
    project_buffers = [jnp.stack([piece[:, : 3 * quarter] for piece in first])]
    mix_near = crossed(after(half_rows(attention_weight[3]), from_other))
    project_buffers.append(send(project_buffers[-1], ring("z")))
    project_buffers[1], mix_near = barrier((project_buffers[1], mix_near))
    mix_far = send(mix_near, flipped("y", 1))
    output_near = crossed(after(half_rows(output_table), mix_near))
    project_buffers.append(send(project_buffers[-1], ring("z")))
    project_buffers.append(send(project_buffers[-1], ring("z")))
    project_buffers[3], mix_far = barrier((project_buffers[3], mix_far))
    down_low = turned(first, 3, 5, "z", project_buffers[3])
    down_high = turned(second, 0, 2, "x", up_buffers[3])
    output_far = send(
        after(output_near, project_buffers[3], up_buffers[3]), flipped("y", 1)
    )

    scalars = jnp.stack([spot.z, spot.x, spot.sign, core, spot.yl]).astype(jnp.int32)
    project_full = place(attention_weight, 0, 3, ("z",), project_buffers, scalars)
    mix_full = place_halves(attention_weight[3], mix_near, mix_far, scalars)
    up_full = place(feedforward_weight, 0, 1, ("x",), up_buffers, scalars)[0]

    def down_placed(activated):
        low, high, _ = barrier((down_low[3], down_high[3], activated))
        buffers = [*down_low[:3], low, *down_high[:3], high]
        return place(feedforward_weight, 1, 1, ("z", "x"), buffers, scalars)[0]

    output_full = place_halves(output_table, output_near, output_far, scalars)

    context_far = send(
        after(jnp.where(settled, context_arrived, context_own), output_far), by("y", 2)
    )

    allowed = allowed_mask(window_segments, layout).astype(F32)
    after_block, normed_three, lefts, saved_state = layer_forward(
        residual,
        project_full,
        mix_full,
        up_full,
        down_placed,
        norm_gains,
        allowed,
        (
            (mix_full,),
            (down_low[1], down_high[1], output_near),
            (up_full, down_low[2], down_high[2]),
            (output_far,),
        ),
    )
    heads, totals, mixed_low, after_attention, pre_act, activated, down_full = saved_state
    left_one, left_two, left_three = lefts
    loss_local, grad_logits = head_loss(
        normed_three, output_full, window_tokens, window_segments, keep_flag, spot
    )

    part = contract(grad_logits, output_full, 1, 1)
    other = swap_core(part)
    output_grad = whole_product(left_three, grad_logits)
    output_z = scatter_z(output_grad)
    grad_block, block_low, left_block, norm_three = norm_backward(
        4, norm_gains, after_block, part, after(other, output_grad)
    )
    down_grad = whole_product(left_block, activated)
    down_z = scatter_z(down_grad)
    block_low = after(block_low, down_grad)

    grad_pre, part = feedforward_backward(block_low, down_full, pre_act, up_full)
    other = swap_core(part)
    up_ring = ring_x(spot, left_two, grad_pre, 512)
    grad_attention, attention_low, left_attention, norm_two = norm_backward(
        2,
        norm_gains,
        after_attention,
        part,
        after(other, up_ring.total),
        grad_block,
    )
    grad_mixed = jnp.dot(attention_low, mix_full, preferred_element_type=F32).astype(BF16)
    grad_projected = attention_backward(heads, allowed, totals, grad_mixed)
    grad_projected, up_one, context_far = barrier((grad_projected, up_ring.arrive(), context_far))
    up_ring.add(up_one)
    grad_projected = after(grad_projected, up_ring.total)
    part = jnp.einsum("ste,sde->td", grad_projected, project_full, preferred_element_type=F32)
    other = swap_core(part)
    project_ring = ring_y(
        spot,
        256,
        (left_one, grad_projected, (1, length, 256), lambda j, half: (j, 0, half), 3),
        (left_attention, mixed_low, (length, 256), lambda j, half: (0, half), 1),
    )
    grad_residual, _, left_residual, norm_one = norm_backward(
        0, norm_gains, residual, part, after(other, project_ring.total), grad_attention
    )

    context_far = context_far + 0.0 * local_seconds
    context = jnp.concatenate([context_near, context_far], axis=1).astype(BF16)

    def columns_of(half):
        side = jnp.where(half == 0, grad_residual[:, : 2 * width], grad_residual[:, 2 * width :])
        return own_quarter(side, core)

    own_grad = jnp.concatenate([columns_of(yh), columns_of(1 - yh)], axis=1)
    own_high = own_grad.astype(BF16)
    own_low = (own_grad - own_high.astype(F32)).astype(BF16)
    hot = (jnp.arange(embed_table.shape[0])[:, None] == window_tokens[None, :]).astype(BF16)
    embed_grad = jnp.dot(hot, own_high, preferred_element_type=F32) + jnp.dot(
        hot, own_low, preferred_element_type=F32
    )
    norms_grad = jnp.concatenate([norm_one, norm_two, norm_three])
    norms_rows = jnp.pad(norms_grad.T, ((0, 0), (0, 122))).reshape(4, 4, 64, 128)

    def condition_part(k, arrived=None):
        left = left_residual.reshape(4, 4, 64, length)
        segments = [
            (left, context, (length, 256), lambda j, s: (0, j), 2),
            (norms_rows, None, None, lambda j, s: (0, 0), 1),
        ]
        return chunk_product(segments, (4, 1, 64, length), 256, k.astype(jnp.int32)[None], arrived)

    condition_ring = Ring("x", spot.x, spot.sign, condition_part)
    condition_ring.total, embed_grad = barrier((condition_ring.total, embed_grad))
    embed_zring = ring_of(spot, "z", embed_grad)
    condition_ring.total, embed_zring.total = barrier((condition_ring.total, embed_zring.total))

    token = condition_ring.total

    def step(ring_here):
        nonlocal token
        arrived, _ = barrier((ring_here.arrive(), token))
        ring_here.add(arrived)
        token = ring_here.total
        return token

    step(up_ring)
    step(condition_ring)
    step(project_ring)
    step(embed_zring)
    up_x = step(up_ring)
    step(condition_ring)
    step(embed_zring)
    down_ring = ring_of(spot, "x", after(jnp.concatenate([down_z, output_z], axis=1), token))
    step(project_ring)
    condition_x = step(condition_ring)
    up_z = scatter_z(jnp.concatenate([up_x, condition_x], axis=1))
    step(down_ring)
    project_y = step(project_ring)
    project_z = scatter_z(project_y)
    embed_z = step(embed_zring)
    step(down_ring)
    embed_ring = ring_of(spot, "x", after(embed_z, token))
    step(down_ring)
    step(embed_ring)
    step(embed_ring)
    step(embed_ring)
    embed_sum = direct_y(spot, embed_ring.total, 64)
    down_x = down_ring.total
    last = direct_y(
        spot,
        jnp.concatenate(
            [
                up_z[:, :1024],
                down_x[:, :1024],
                up_z[:, 2048:2304],
                down_x[:, 2048:2560],
                up_z[:, 2560:2688],
                up_z[:, 1024:2048],
                down_x[:, 1024:2048],
                up_z[:, 2304:2560],
                down_x[:, 2560:],
                up_z[:, 2688:],
            ],
            axis=1,
        ),
        32,
    )
    last_y = direct_sum("x", spot.x, project_z)
    rings = (up_ring, condition_ring, project_ring, down_ring, embed_ring, embed_zring)
    assert all(r.step == 4 for r in rings)
    project_sum, mix_sum = last_y[:, :768], last_y[:, 768:]
    up_sum, down_sum = last[:, :1024], last[:, 1024:2048]
    condition_sum, output_sum = last[:, 2048:2304], last[:, 2304:2816]
    norms_both = last[:, 2816:].reshape(2, 16, 128)
    norms_share = lax.dynamic_index_in_dim(norms_both, core, 0, False)[:, :6].T

    sums = [output_sum, down_sum, up_sum, mix_sum, project_sum, condition_sum, embed_sum]
    squares = 0.5 * jnp.sum((norms_share * SQUARE_SCALE) ** 2)
    for piece in sums:
        squares = squares + jnp.sum((piece * SQUARE_SCALE) ** 2)
    scalars = jnp.stack([0.5 * loss_local, squares, 0.5 * local_seconds])
    flat = [piece.reshape(2, 16, -1) for piece in sums[:-1]] + [sums[-1].reshape(2, 16, 512)]
    flat = jnp.concatenate(flat, axis=2)
    mine = lax.dynamic_index_in_dim(flat, core, 0, False)
    theirs = swap_core(lax.dynamic_index_in_dim(flat, 1 - core, 0, False))
    scalars = pair_sum(jnp.broadcast_to(scalars[:, None], (3, 128)))
    scalars = sum_of_four(scalars, "x", spot.x)
    scalars = sum_of_four(after(scalars, theirs), "z", spot.z)
    scalars = sum_of_four(scalars, "y", spot.y)
    loss_total, seconds_total = scalars[0, 0], scalars[2, 0]
    inverse = 1.0 / seconds_total
    gradient_norm = jnp.sqrt(scalars[1, 0]) * (inverse / SQUARE_SCALE)
    clip_factor = CLIP_NORM / jnp.maximum(gradient_norm, CLIP_NORM)

    low_side = jnp.where(core == 0, mine, theirs)
    high_side = jnp.where(core == 0, theirs, mine)

    def share(start, stop):
        return low_side[:, start:stop], high_side[:, start:stop]

    output_share = jnp.concatenate(share(0, 512), axis=1)
    feedforward_share = jnp.stack(
        [jnp.concatenate(share(1536, 2560), axis=1), jnp.concatenate(share(512, 1536), axis=1)]
    )
    mix_low, mix_high = share(2560, 2816)
    project_low, project_high = share(2816, 3584)
    attention_share = jnp.stack(
        [
            jnp.concatenate(
                [project_low[:, 256 * k : 256 * k + 256], project_high[:, 256 * k : 256 * k + 256]],
                axis=1,
            )
            for k in range(3)
        ]
        + [jnp.concatenate([mix_low, mix_high], axis=1)]
    )
    condition_share = jnp.concatenate(share(3584, 3840), axis=1)
    embed_share = jnp.concatenate([part.reshape(32, 256) for part in share(3840, 4352)], axis=1)

    shares = (
        embed_share,
        condition_share,
        attention_share,
        feedforward_share,
        output_share,
        norms_share,
    )
    masters = (
        embed_master,
        condition_master,
        attention_master,
        feedforward_master,
        output_master,
        norms_master,
    )
    firsts = (
        embed_first,
        condition_first,
        attention_first,
        feedforward_first,
        output_first,
        norms_first,
    )
    seconds_old = (
        embed_second,
        condition_second,
        attention_second,
        feedforward_second,
        output_second,
        norms_second,
    )
    rates = (RATE_TABLE, RATE_MATRIX, RATE_MATRIX, RATE_MATRIX, RATE_MATRIX, RATE_NORMS)
    decays = (WEIGHT_DECAY, WEIGHT_DECAY, WEIGHT_DECAY, WEIGHT_DECAY, WEIGHT_DECAY, 0.0)
    outputs = [loss_total, seconds_total, gradient_norm]
    for slot in range(6):
        outputs += adam_step(
            shares[slot] * inverse * clip_factor,
            masters[slot],
            firsts[slot],
            seconds_old[slot],
            rates[slot],
            decays[slot],
        )
    return tuple(outputs)


def solution(mesh):
    torus = Mesh(mesh.devices.reshape(SIZES), AXES)
    table, slotted = P(DP, "yh"), P(None, DP, "yh")
    state = (table, table, slotted, slotted, table, P(None, DP))
    results = tuple(spec for spec in state for _ in range(3))
    return jax.shard_map(
        local,
        mesh=torus,
        in_specs=(
            P(DP),
            P(DP),
            P(),
            P(DP),
            P(DP),
            table,
            P(None, "yh"),
            P(None, "yh"),
            P(None, None, "yh"),
            P(None, None, "yh"),
            P(None, "yh"),
            P(),
        )
        + state * 3,
        out_specs=(P(), P(), P()) + results,
        check_vma=False,
    )
```

```python
import functools

import jax
import jax.numpy as jnp
import numpy as np
from jax import lax
from jax.experimental import pallas as pl
from jax.experimental.pallas import tpu as pltpu
from jax.sharding import Mesh
from jax.sharding import PartitionSpec as P

HEAD_DIM = 64
BLK = 64
CLIPS_DEV = 4
STEP = 10


LAYER_EPS = 1e-05
SAMPLE_RATE = 44100.0
LOG_TWO_NATS = 0.6931471805599453
CLIP_NORM = 1.0
BETA_FIRST = 0.9
BETA_SECOND = 0.95
ADAM_EPSILON = 1e-08
WEIGHT_DECAY = 0.01
RATE_MATRIX = 0.1
RATE_TABLE = 1.0
RATE_NORMS = 1.0
SQUARE_SCALE = 2.0**-9

AXES = ("z", "x", "yl", "c", "yh")
SIZES = (4, 4, 2, 2, 2)
DP = ("z", "x", "yl", "c")
MIB = 1024 * 1024
QUERY_ROWS = 256
BF16 = jnp.bfloat16
F32 = jnp.float32


def send(value, move):
    pairs = []
    for index in range(int(np.prod(SIZES))):
        z, x, yl, c, yh = (int(i) for i in np.unravel_index(index, SIZES))
        target = move(z, x, yh * 2 + yl, c)
        if target is not None:
            z, x, y, c = target
            y %= 4
            at = (z % 4, x % 4, y % 2, c, y // 2)
            pairs.append((index, int(np.ravel_multi_index(at, SIZES))))
    return lax.ppermute(value, AXES, pairs)


def swap_core(value):
    return send(value, lambda z, x, y, c: (z, x, y, 1 - c))


def pair_sum(value):
    return value + swap_core(value)


def ring(axis):
    def move(z, x, y, c):
        step = 1 - 2 * c
        return {"z": (z + step, x, y, c), "x": (z, x + step, y, c), "y": (z, x, y + step, c)}[axis]

    return move


def by(axis, count):
    def move(z, x, y, c):
        return {"z": (z + count, x, y, c), "x": (z, x + count, y, c), "y": (z, x, y + count, c)}[axis]

    return move


def flipped(axis, bit):
    def move(z, x, y, c):
        return {"z": (z ^ bit, x, y, c), "x": (z, x ^ bit, y, c), "y": (z, x, y ^ bit, c)}[axis]

    return move


def after(value, *earlier):
    return lax.optimization_barrier((value, *earlier))[0]


def pieces_kernel(s_ref, *refs):
    width = 0
    for ref in refs[:-1]:
        refs[-1][:, width : width + ref.shape[-1]] = ref[0].astype(F32)
        width += ref.shape[-1]


def pieces_of(attention_weight, feedforward_weight, index):
    narrow, wide = attention_weight.shape[2] // 2, feedforward_weight.shape[2] // 2
    specs = [pl.BlockSpec((1, 64, narrow), lambda g, s, k=k: (k, s[0], s[1])) for k in range(3)]
    specs += [pl.BlockSpec((1, 64, wide), lambda g, s, k=k: (k, s[0], s[1])) for k in (1, 0)]
    width = 3 * narrow + 2 * wide
    return pl.pallas_call(
        pieces_kernel,
        grid_spec=pltpu.PrefetchScalarGridSpec(
            num_scalar_prefetch=1,
            grid=(1,),
            in_specs=specs,
            out_specs=pl.BlockSpec((64, width), lambda g, s: (0, 0)),
        ),
        out_shape=jax.ShapeDtypeStruct((64, width), F32),
        compiler_params=pltpu.CompilerParams(vmem_limit_bytes=8 * MIB),
        cost_estimate=estimate(1, 1),
    )(index, *in_hbm(*[attention_weight] * 3, *[feedforward_weight] * 2))


def own_quarter(half, core):
    width = half.shape[-1] // 2
    return jnp.where(core == 0, half[..., :width], half[..., width:])


def place_kernel(rings, s_ref, native_ref, *rest):
    out_ref = rest[-1]
    width = native_ref.shape[-1]
    part = width // len(rings)
    out_ref[0, :, :width] = native_ref[0]
    z, x, sign = s_ref[0], s_ref[1], s_ref[2]
    for r, axis in enumerate(rings):
        lanes = slice(width + r * part, width + (r + 1) * part)
        for j in range(4):
            for i in range(4):
                z_at = lax.rem(z - sign * (j if axis == "z" else i) + 8, 4)
                x_at = lax.rem(x - sign * (j if axis == "x" else i) + 8, 4)
                rows = pl.ds(pl.multiple_of(z_at * 256 + x_at * 64, 64), 64)
                out_ref[0, rows, lanes] = rest[4 * r + j][i].astype(BF16)


def place(native, first_slot, slots, rings, buffers, scalars):
    rows, width = native.shape[1], native.shape[2] // 2
    block = pl.BlockSpec((4, 64, width // len(rings)), lambda k, s: (0, 0, k))
    return pl.pallas_call(
        functools.partial(place_kernel, rings),
        grid_spec=pltpu.PrefetchScalarGridSpec(
            num_scalar_prefetch=1,
            grid=(slots,),
            in_specs=[pl.BlockSpec((1, rows, width), lambda k, s: (first_slot + k, 0, s[3]))]
            + [block] * len(buffers),
            out_specs=pl.BlockSpec((1, rows, 2 * width), lambda k, s: (k, 0, 0)),
        ),
        out_shape=jax.ShapeDtypeStruct((slots, rows, 2 * width), BF16),
        compiler_params=pltpu.CompilerParams(vmem_limit_bytes=24 * MIB),
        cost_estimate=estimate(1, 1),
    )(scalars, *in_hbm(native), *buffers)


def place_halves_kernel(s_ref, native_ref, near_ref, far_ref, out_ref):
    half, width = near_ref.shape
    out_ref[:, :width] = native_ref[...]
    near = s_ref[4]
    out_ref[pl.ds(pl.multiple_of(near * half, 64), half), width:] = near_ref[...].astype(BF16)
    out_ref[pl.ds(pl.multiple_of((1 - near) * half, 64), half), width:] = far_ref[...].astype(BF16)


def place_halves(native, near, far, scalars):
    rows, width = native.shape[0], native.shape[1] // 2
    whole = pl.BlockSpec((rows // 2, width), lambda k, s: (0, 0))
    return pl.pallas_call(
        place_halves_kernel,
        grid_spec=pltpu.PrefetchScalarGridSpec(
            num_scalar_prefetch=1,
            grid=(1,),
            in_specs=[pl.BlockSpec((rows, width), lambda k, s: (0, s[3])), whole, whole],
            out_specs=pl.BlockSpec((rows, 2 * width), lambda k, s: (0, 0)),
        ),
        out_shape=jax.ShapeDtypeStruct((rows, 2 * width), BF16),
        compiler_params=pltpu.CompilerParams(vmem_limit_bytes=12 * MIB),
        cost_estimate=pl.CostEstimate(
            flops=0, bytes_accessed=rows * width * 10, transcendentals=0
        ),
    )(scalars, *in_hbm(native), near, far)


def direct(value, axis):
    return jnp.stack([value] + [send(value, by(axis, k)) for k in (1, 2, 3)])


def around(buffer, axis):
    buffers = [buffer]
    for _ in range(3):
        buffers.append(send(buffers[-1], ring(axis)))
    return buffers


class Ring:
    def __init__(self, axis, place_at, sign, part):
        self.axis, self.place_at, self.sign, self.part = axis, place_at, sign, part
        self.step = 1
        self.total = part(lax.rem(place_at - sign + 8, 4))

    def arrive(self):
        return send(self.total, ring(self.axis))

    def add(self, arrived):
        self.step += 1
        own = lax.rem(self.place_at - self.step * self.sign + 8, 4)
        self.total = self.part(own, arrived)


def ring_of(spot, axis, grad):
    view = grad.reshape(1, 4, -1, grad.shape[1])

    def part(k, arrived=None):
        return chunk_added(view, k.astype(jnp.int32)[None], arrived)

    return Ring(axis, spot.z if axis == "z" else spot.x, spot.sign, part)


def added(product, arrived):
    return product if arrived is None else product + arrived


def ring_x(spot, left, right, tile):
    left = left.reshape(4, 4, -1, left.shape[-1])
    segment = (left, right, (right.shape[0], tile), lambda j, s: (0, j), right.shape[1] // tile)

    def part(k, arrived=None):
        index = k.astype(jnp.int32)[None]
        return chunk_product([segment], (4, 1, *left.shape[2:]), tile, index, arrived)

    return Ring("x", spot.x, spot.sign, part)


def ring_y(spot, tile, *segments):
    tokens = segments[0][0].shape[-1]
    rest = segments[0][0].shape[0] // 32

    def part(k, arrived=None):
        half = jnp.where(lax.div(k, 2) == spot.yh, 0, 1)
        index = jnp.stack([lax.rem(k, 2), half]).astype(jnp.int32)
        turned = [
            (left.reshape(16, 2, rest, tokens), right, block, lambda j, s, at=at: at(j, s[1]), tiles)
            for left, right, block, at, tiles in segments
        ]
        return chunk_product(turned, (16, 1, rest, tokens), tile, index, arrived)

    return Ring("y", spot.y, spot.sign, part)


def whole_product(left, right):
    segment = (left[None, None], right, (right.shape[0], 512), lambda j, s: (0, j), right.shape[1] // 512)
    none = jnp.zeros((1,), jnp.int32)
    return chunk_product([segment], (1, 1, *left.shape), 512, none, None, pltpu.HBM)


def scatter_z(grad):
    return lax.psum_scatter(grad, "z", scatter_dimension=0, tiled=True)


def direct_y(spot, grad, rows):
    width = grad.shape[1] // 2
    view = grad.reshape(-1, 2, rows, 2 * width)
    same = lax.dynamic_index_in_dim(view, spot.yl, 1, False)
    other = lax.dynamic_index_in_dim(view, 1 - spot.yl, 1, False)
    near = send(other[..., :width], flipped("y", 1))
    far = send(other[..., width:], flipped("y", 3))
    across = send(same[..., width:], flipped("y", 2))
    return ((same[..., :width] + near) + (far + across)).reshape(-1, width)


def direct_sum(axis, place_at, grad, outer=1):
    view = grad.reshape(outer, 4, grad.shape[0] // (4 * outer), grad.shape[1])
    parts = [
        send(lax.dynamic_index_in_dim(view, lax.rem(place_at + k, 4), 1, False), by(axis, k))
        for k in (1, 2, 3)
    ]
    own = lax.dynamic_index_in_dim(view, place_at, 1, False)
    return ((own + parts[0]) + (parts[1] + parts[2])).reshape(-1, grad.shape[1])


def turned(value):
    return lax.optimization_barrier(value.T)


class Spot:
    def __init__(self):
        self.z, self.x, self.yl, self.c, self.yh = (lax.axis_index(a) for a in AXES)
        self.y = self.yh * 2 + self.yl
        self.sign = 1 - 2 * self.c


def sum_of_four(value, axis, place_at):
    pieces = [value] + [send(value, by(axis, k)) for k in (1, 2, 3)]
    total = None
    for at in range(4):
        back = lax.rem(place_at - at + 4, 4)
        part = pieces[3]
        for k in (2, 1, 0):
            part = jnp.where(back == k, pieces[k], part)
        total = part if total is None else total + part
    return total


def contract(left_side, right_side, left_dim, right_dim):
    return lax.dot_general(
        left_side,
        right_side,
        (((left_dim,), (right_dim,)), ((), ())),
        preferred_element_type=jnp.float32,
    )


def attention_forward_kernel(heads_ref, mask_ref, out_ref, total_ref):
    length = heads_ref.shape[1]
    for half in range(2):
        lanes = slice(half * HEAD_DIM, (half + 1) * HEAD_DIM)
        keys, values = heads_ref[1, :, lanes], heads_ref[2, :, lanes]
        scaled = heads_ref[0, :, lanes] * jnp.asarray(HEAD_DIM ** (-0.5), BF16)
        for start in range(0, length, QUERY_ROWS):
            stop = start + QUERY_ROWS
            scores = contract(scaled[start:stop], keys[:stop], 1, 1)
            scores = jnp.where(mask_ref[start:stop, :stop] > 0, scores, -1e30)
            top = jnp.max(scores, axis=-1, keepdims=True)
            weights = jnp.exp(scores - top)
            sums = jnp.sum(weights, axis=-1, keepdims=True)
            weights = (weights * (1.0 / sums)).astype(BF16)
            out_ref[start:stop, lanes] = contract(weights, values[:stop], 1, 0).astype(BF16)
            total_ref[0, start:stop, half : half + 1] = top + jnp.log(sums)


def attention_backward_kernel(heads_ref, mask_ref, total_ref, grad_ref, out_ref, keys_acc, values_acc):
    length = heads_ref.shape[1]
    for half in range(2):
        lanes = slice(half * HEAD_DIM, (half + 1) * HEAD_DIM)
        keys, values = heads_ref[1, :, lanes], heads_ref[2, :, lanes]
        scaled = heads_ref[0, :, lanes] * jnp.asarray(HEAD_DIM ** (-0.5), BF16)
        for start in range(length - QUERY_ROWS, -1, -QUERY_ROWS):
            stop = start + QUERY_ROWS
            queries, grad = scaled[start:stop], grad_ref[start:stop, lanes]
            scores = contract(queries, keys[:stop], 1, 1)
            scores = jnp.where(mask_ref[start:stop, :stop] > 0, scores, -1e30)
            weights = jnp.exp(scores - total_ref[0, start:stop, half : half + 1])
            grad_values = contract(weights.astype(BF16), grad, 0, 0)
            grad_weights = contract(grad, values[:stop], 1, 1)
            total = jnp.sum(weights * grad_weights, axis=-1, keepdims=True)
            grad_scores = (weights * (grad_weights - total)).astype(BF16)
            grad_queries = contract(grad_scores, keys[:stop], 1, 0) * HEAD_DIM ** (-0.5)
            out_ref[0, start:stop, lanes] = grad_queries.astype(BF16)
            grad_keys = contract(grad_scores, queries, 0, 0)
            if stop == length:
                keys_acc[...] = grad_keys
                values_acc[...] = grad_values
            else:
                keys_acc[:stop] += grad_keys
                values_acc[:stop] += grad_values
        out_ref[1, :, lanes] = keys_acc[...].astype(BF16)
        out_ref[2, :, lanes] = values_acc[...].astype(BF16)


def estimate(flops, moved):
    return pl.CostEstimate(flops=flops, bytes_accessed=moved, transcendentals=0)


def in_hbm(*values):
    return [pltpu.with_memory_space_constraint(value, pltpu.HBM) for value in values]


def norm_forward_kernel(row, parts, base_ref, *rest):
    ins, outs = rest[: parts + 1], rest[parts + 1 :]
    gains_ref = ins[-1]
    values = base_ref[...]
    if parts:
        values = values + (ins[0][...] + ins[1][...])
        outs[2][...] = values
    centred = values - jnp.mean(values, axis=-1, keepdims=True)
    variance = jnp.mean(centred * centred, axis=-1, keepdims=True)
    normed = centred * lax.rsqrt(variance + LAYER_EPS) * gains_ref[row : row + 1] + gains_ref[row + 1 : row + 2]
    outs[0][...] = normed.astype(BF16)
    outs[1][...] = normed.T.astype(BF16)


def norm_forward(row, gains, base, parts=()):
    length, width = base.shape
    rows = 256
    block = pl.BlockSpec((rows, width), lambda g: (g, 0))
    turned = pl.BlockSpec((width, rows), lambda g: (0, g))
    shapes = [jax.ShapeDtypeStruct((length, width), BF16), jax.ShapeDtypeStruct((width, length), BF16)]
    if parts:
        shapes.append(jax.ShapeDtypeStruct((length, width), F32))
    return pl.pallas_call(
        functools.partial(norm_forward_kernel, row, len(parts)),
        grid=(length // rows,),
        in_specs=[block] * (1 + len(parts)) + [pl.BlockSpec(gains.shape, lambda g: (0, 0))],
        out_specs=[block, turned, block][: len(shapes)],
        out_shape=shapes,
        compiler_params=pltpu.CompilerParams(vmem_limit_bytes=22 * MIB),
        cost_estimate=estimate(1, 1),
    )(base, *parts, gains)


def norm_backward_kernel(row, has_base, values_ref, part_ref, other_ref, gains_ref, *rest):
    if has_base:
        base_ref, rest = rest[0], rest[1:]
    out_ref, low_ref, turned_ref, sums_ref = rest
    values = values_ref[...]
    grad = part_ref[...] + other_ref[...]
    centred = values - jnp.mean(values, axis=-1, keepdims=True)
    scale = lax.rsqrt(jnp.mean(centred * centred, axis=-1, keepdims=True) + LAYER_EPS)
    normed = centred * scale
    gained = grad * gains_ref[row : row + 1]
    inner = gained - jnp.mean(gained, axis=-1, keepdims=True)
    inner = scale * (inner - normed * jnp.mean(gained * normed, axis=-1, keepdims=True))
    if has_base:
        inner = base_ref[...] + inner
    out_ref[...] = inner
    low_ref[...] = inner.astype(BF16)
    turned_ref[...] = inner.T.astype(BF16)
    sums = jnp.concatenate(
        [jnp.sum(grad * normed, axis=0, keepdims=True), jnp.sum(grad, axis=0, keepdims=True)], axis=0
    )

    @pl.when(pl.program_id(0) == 0)
    def _():
        sums_ref[...] = sums

    @pl.when(pl.program_id(0) > 0)
    def _():
        sums_ref[...] += sums


def norm_backward(row, gains, values, part, other, base=None):
    length, width = values.shape
    rows = 256
    block = pl.BlockSpec((rows, width), lambda g: (g, 0))
    operands = [values, part, other, gains] + ([] if base is None else [base])
    specs = [block] * 3 + [pl.BlockSpec(gains.shape, lambda g: (0, 0))] + ([] if base is None else [block])
    return pl.pallas_call(
        functools.partial(norm_backward_kernel, row, base is not None),
        grid=(length // rows,),
        in_specs=specs,
        out_specs=[
            block,
            block,
            pl.BlockSpec((width, rows), lambda g: (0, g)),
            pl.BlockSpec((2, width), lambda g: (0, 0)),
        ],
        out_shape=[
            jax.ShapeDtypeStruct((length, width), F32),
            jax.ShapeDtypeStruct((length, width), BF16),
            jax.ShapeDtypeStruct((width, length), BF16),
            jax.ShapeDtypeStruct((2, width), F32),
        ],
        compiler_params=pltpu.CompilerParams(vmem_limit_bytes=26 * MIB),
        cost_estimate=estimate(1, 1),
    )(*operands)


def chunk_kernel(bounds, plain, has_recv, s_ref, *rest):
    out_ref = rest[-1]
    for n, (start, stop) in enumerate(bounds):
        left_ref, right_ref = rest[2 * n], rest[2 * n + 1]

        @pl.when((pl.program_id(0) >= start) & (pl.program_id(0) < stop))
        def _(left_ref=left_ref, right_ref=right_ref):
            if plain[n]:
                total = left_ref[...].reshape(out_ref.shape[0], left_ref.shape[-1])
                total = jnp.concatenate([total, total], axis=1)
            else:
                left = left_ref[...].reshape(out_ref.shape[0], left_ref.shape[-1])
                right = right_ref[...].reshape(right_ref.shape[-2:])
                total = jnp.dot(left, right, preferred_element_type=F32)
            if has_recv:
                total += rest[2 * len(bounds)][...]
            out_ref[...] = total


def chunk_product(segments, left_block, tile, index, arrived, place_for=jax.ShapeDtypeStruct):
    rows = int(np.prod(left_block[:-1]))
    out_spec = pl.BlockSpec((rows, tile), lambda j, s: (0, j))
    operands, specs, bounds, start = [], [], [], 0
    for left, right, right_block, right_at, tiles in segments:

        def at(j, s, start=start, tiles=tiles, right_at=right_at):
            return right_at(jnp.clip(j - start, 0, tiles - 1), s)

        operands += [left, index if right is None else right]
        specs += [
            pl.BlockSpec((*left_block[:-1], left.shape[-1]), lambda j, s: (0, s[0], 0, 0)),
            pl.BlockSpec(memory_space=pltpu.SMEM) if right is None else pl.BlockSpec(right_block, at),
        ]
        bounds.append((start, start + tiles))
        start += tiles
    extra = [] if arrived is None else [arrived]
    return pl.pallas_call(
        functools.partial(
            chunk_kernel, tuple(bounds), [seg[1] is None for seg in segments], arrived is not None
        ),
        grid_spec=pltpu.PrefetchScalarGridSpec(
            num_scalar_prefetch=1,
            grid=(start,),
            in_specs=specs + [out_spec] * len(extra),
            out_specs=out_spec,
        ),
        out_shape=place_for((rows, tile * start), F32),
        compiler_params=pltpu.CompilerParams(vmem_limit_bytes=16 * MIB),
        cost_estimate=estimate(1, 1),
    )(index, *operands, *extra)


def add_kernel(s_ref, own_ref, *rest):
    out_ref = rest[-1]
    total = own_ref[0, 0]
    for arrived_ref in rest[:-1]:
        total = total + arrived_ref[...]
    out_ref[...] = total


def chunk_added(view, index, arrived):
    rows, width = view.shape[2:]
    tile = width // 2
    out_spec = pl.BlockSpec((rows, tile), lambda j, s: (0, j))
    extra = [] if arrived is None else [arrived]
    return pl.pallas_call(
        add_kernel,
        grid_spec=pltpu.PrefetchScalarGridSpec(
            num_scalar_prefetch=1,
            grid=(2,),
            in_specs=[pl.BlockSpec((1, 1, rows, tile), lambda j, s: (0, s[0], 0, j))]
            + [out_spec] * len(extra),
            out_specs=out_spec,
        ),
        out_shape=jax.ShapeDtypeStruct((rows, width), F32),
        compiler_params=pltpu.CompilerParams(vmem_limit_bytes=8 * MIB),
        cost_estimate=estimate(1, 1),
    )(index, view, *extra)


def attention_forward(heads, mask):
    length, width = heads.shape[1:]
    return pl.pallas_call(
        attention_forward_kernel,
        grid=(width // 128,),
        in_specs=[
            pl.BlockSpec((3, length, 128), lambda g: (0, 0, g)),
            pl.BlockSpec((length, length), lambda g: (0, 0)),
        ],
        out_specs=[
            pl.BlockSpec((length, 128), lambda g: (0, g)),
            pl.BlockSpec((1, length, 2), lambda g: (g, 0, 0)),
        ],
        out_shape=[
            jax.ShapeDtypeStruct((length, width), BF16),
            jax.ShapeDtypeStruct((width // 128, length, 2), F32),
        ],
        compiler_params=pltpu.CompilerParams(vmem_limit_bytes=16 * MIB),
        cost_estimate=estimate(1, 1),
    )(heads, mask)


def attention_backward(heads, mask, totals, grad_mixed):
    length, width = heads.shape[1:]
    return pl.pallas_call(
        attention_backward_kernel,
        grid=(width // 128,),
        in_specs=[
            pl.BlockSpec((3, length, 128), lambda g: (0, 0, g)),
            pl.BlockSpec((length, length), lambda g: (0, 0)),
            pl.BlockSpec((1, length, 2), lambda g: (g, 0, 0)),
            pl.BlockSpec((length, 128), lambda g: (0, g)),
        ],
        out_specs=pl.BlockSpec((3, length, 128), lambda g: (0, 0, g)),
        out_shape=jax.ShapeDtypeStruct((3, length, width), BF16),
        scratch_shapes=[pltpu.VMEM((length, HEAD_DIM), F32), pltpu.VMEM((length, HEAD_DIM), F32)],
        compiler_params=pltpu.CompilerParams(vmem_limit_bytes=16 * MIB),
        cost_estimate=estimate(1, 1),
    )(heads, mask, totals, grad_mixed)


def feedforward_backward_kernel(block_ref, down_ref, pre_ref, up_ref, grad_pre_ref, normed_ref):
    grad_activated = jnp.dot(block_ref[...], down_ref[...], preferred_element_type=F32)
    pre = pre_ref[...]
    slope = 0.7978845608028654
    square = pre * pre
    bent = jnp.tanh(pre * (slope + (slope * 0.044715) * square))
    inner = pre * (0.5 * slope + (1.5 * slope * 0.044715) * square)
    factor = (0.5 + 0.5 * bent) + inner * (1.0 - bent * bent)
    grad_pre = (grad_activated * factor).astype(BF16)
    grad_pre_ref[...] = grad_pre
    part = contract(grad_pre, up_ref[...], 1, 1)

    @pl.when(pl.program_id(0) == 0)
    def _():
        normed_ref[...] = part

    @pl.when(pl.program_id(0) > 0)
    def _():
        normed_ref[...] += part


def feedforward_backward(block_low, down_full, pre_act, up_full):
    length, hidden = pre_act.shape
    width, tile = block_low.shape[1], 512
    return pl.pallas_call(
        feedforward_backward_kernel,
        grid=(hidden // tile,),
        in_specs=[
            pl.BlockSpec((length, width), lambda g: (0, 0)),
            pl.BlockSpec((width, tile), lambda g: (0, g)),
            pl.BlockSpec((length, tile), lambda g: (0, g)),
            pl.BlockSpec((width, tile), lambda g: (0, g)),
        ],
        out_specs=[
            pl.BlockSpec((length, tile), lambda g: (0, g)),
            pl.BlockSpec((length, width), lambda g: (0, 0)),
        ],
        out_shape=[
            jax.ShapeDtypeStruct((length, hidden), BF16),
            jax.ShapeDtypeStruct((length, width), F32),
        ],
        compiler_params=pltpu.CompilerParams(vmem_limit_bytes=22 * MIB),
        cost_estimate=estimate(1, 1),
    )(*in_hbm(block_low, down_full, pre_act, up_full))


def allowed_mask(segments, layout):
    length = segments.shape[0]
    position = jnp.arange(length)
    blocks = layout.shape[0]
    block_open = (
        jnp.broadcast_to(layout[:, None, :, None], (blocks, BLK, blocks, BLK)).reshape(
            length, length
        )
        > 0
    )
    causal = position[None, :] <= position[:, None]
    return causal & (segments[:, None] == segments[None, :]) & block_open


def layer_forward(residual, project_weight, mix_weight, up_weight, down_weight, norm_gains, mask, early):
    normed_one, left_one = norm_forward(0, norm_gains, residual)
    heads = jnp.einsum(
        "td,sde->ste", normed_one, project_weight, preferred_element_type=jnp.float32
    ).astype(jnp.bfloat16)
    heads = after(heads, *early[0])
    mixed_low, totals = attention_forward(heads, mask)
    mixed_low = after(mixed_low, *early[1])
    part = contract(mixed_low, mix_weight, 1, 1)
    other = after(swap_core(part), *early[2])
    normed_two, left_two, after_attention = norm_forward(2, norm_gains, residual, (part, other))
    pre_act = jnp.dot(normed_two, up_weight, preferred_element_type=jnp.float32)
    activated = jax.nn.gelu(pre_act).astype(jnp.bfloat16)
    activated = after(activated, *early[3])
    down_full = down_weight(activated)
    part = contract(activated, down_full, 1, 1)
    normed_three, left_three, after_block = norm_forward(
        4, norm_gains, after_attention, (part, swap_core(part))
    )
    saved_state = (heads, totals, mixed_low, after_attention, pre_act, activated, down_full)
    return (after_block, normed_three, (left_one, left_two, left_three), saved_state)


def head_loss(normed_three, output_table, code_tokens, segments, keep_flag, spot):
    logits = jnp.dot(normed_three, output_table, preferred_element_type=jnp.float32)
    width = output_table.shape[1]
    quarter = width // 2
    targets = jnp.concatenate([code_tokens[1:], code_tokens[-1:]])
    column = jnp.arange(width)
    code = jnp.where(
        column < quarter,
        spot.yh * width + spot.c * quarter + column,
        (1 - spot.yh) * width + spot.c * quarter + column - quarter,
    )
    target_hit = code[None, :] == targets[:, None]
    row_top = jnp.max(logits, axis=1)
    row_sums = jnp.sum(jnp.exp(logits - row_top[:, None]), axis=1)
    picked = jnp.sum(jnp.where(target_hit, logits, 0.0), axis=1)
    other = swap_core(jnp.stack([row_top, row_sums, picked]))
    both_top = jnp.maximum(row_top, other[0])
    both_sums = row_sums * jnp.exp(row_top - both_top) + other[1] * jnp.exp(other[0] - both_top)
    log_norm = both_top + jnp.log(both_sums)
    next_segment = jnp.concatenate([segments[1:], jnp.full((1,), -1, jnp.int32)])
    counted = ((segments == next_segment) & (segments < CLIPS_DEV)).astype(jnp.float32) * keep_flag
    loss_local = jnp.sum(counted * (log_norm - (picked + other[2]))) / LOG_TWO_NATS
    grad_logits = (counted / LOG_TWO_NATS)[:, None] * (
        jnp.exp(logits - log_norm[:, None]) - target_hit.astype(jnp.float32)
    )
    grad_low = grad_logits.astype(jnp.bfloat16)
    return (loss_local, grad_low)


def adam_step(gradient, master, first_old, second_old, step_rate, decay_rate):
    moment = BETA_FIRST * first_old + (1.0 - BETA_FIRST) * gradient
    variance = BETA_SECOND * second_old + (1.0 - BETA_SECOND) * gradient * gradient
    moment_hat = moment / (1.0 - BETA_FIRST**STEP)
    variance_hat = variance / (1.0 - BETA_SECOND**STEP)
    updated = master - step_rate * (
        moment_hat / (jnp.sqrt(variance_hat) + ADAM_EPSILON) + decay_rate * master
    )
    return (moment, variance, updated)


def local(
    code_tokens,
    segments,
    layout,
    durations,
    overflow,
    upper_context,
    embed_table,
    condition_weight,
    attention_weight,
    feedforward_weight,
    output_table,
    norm_gains,
    embed_master,
    condition_master,
    attention_master,
    feedforward_master,
    output_master,
    norms_master,
    embed_first,
    condition_first,
    attention_first,
    feedforward_first,
    output_first,
    norms_first,
    embed_second,
    condition_second,
    attention_second,
    feedforward_second,
    output_second,
    norms_second,
):
    spot = Spot()
    core, yh = spot.c, spot.yh
    settled = core == yh
    length = code_tokens.shape[0]

    keep_native = 1.0 - overflow[0].astype(jnp.float32)
    local_seconds = keep_native * jnp.sum(durations.astype(jnp.float32)) / SAMPLE_RATE
    native_ints = jnp.concatenate([code_tokens, segments, jnp.broadcast_to(overflow, (128,))])
    window_ints = jnp.where(settled, native_ints, swap_core(native_ints))
    window_tokens = window_ints[:length]
    window_segments = window_ints[length : 2 * length]
    keep_flag = 1.0 - window_ints[2 * length].astype(jnp.float32)

    barrier = lax.optimization_barrier

    def crossed(value):
        return send(value, lambda z, x, y, c: (z, x, 3 - y, c))

    block = spot.z * 4 + spot.x
    own_pieces = pieces_of(
        attention_weight, feedforward_weight, jnp.stack([block, core]).astype(jnp.int32)
    )
    own_pieces, upper_context = barrier((own_pieces, upper_context))
    pieces = crossed(own_pieces)
    quarter = attention_weight.shape[2] // 2

    embedded = jnp.take(embed_table, code_tokens, axis=0).astype(F32)
    half_width = embed_table.shape[1]
    embed_part = contract(upper_context, condition_weight, 1, 1)
    embed_part = jnp.concatenate(
        [
            embed_part[:, :half_width] + jnp.where(yh == 0, embedded, 0.0),
            embed_part[:, half_width:] + jnp.where(yh == 1, embedded, 0.0),
        ],
        axis=1,
    )
    width = half_width // 2
    context_own = own_quarter(upper_context, core).astype(F32)
    context_arrived = swap_core(own_quarter(upper_context, 1 - core).astype(F32))
    embed_part, pieces, context_arrived = barrier((embed_part, pieces, context_arrived))
    context_near = jnp.where(settled, context_own, context_arrived)
    from_other = send(
        embed_part,
        lambda z, x, y, c: (z, x, y ^ 2, c) if c != y // 2 else None,
    )
    first, second = [pieces[:, : 5 * quarter]], [pieces[:, 5 * quarter :]]
    for _ in range(3):
        first.append(send(first[-1], ring("x")))
        second.append(send(second[-1], ring("z")))
    window_sum = embed_part + from_other
    residual = jnp.where(settled, window_sum, swap_core(window_sum))

    def half_rows(native):
        halves = own_quarter(native, core).reshape(2, native.shape[0] // 2, -1)
        return lax.dynamic_index_in_dim(halves, 1 - spot.yl, 0, False).astype(F32)

    def turned(pieces, start, stop, axis, *earlier):
        columns = jnp.stack([piece[:, start * quarter : stop * quarter] for piece in pieces])
        return around(after(columns, *earlier), axis)

    up_buffers = turned(second, 2, 6, "x")
    project_buffers = [jnp.stack([piece[:, : 3 * quarter] for piece in first])]
    mix_near = crossed(after(half_rows(attention_weight[3]), from_other))
    project_buffers.append(send(project_buffers[-1], ring("z")))
    project_buffers[1], mix_near = barrier((project_buffers[1], mix_near))
    mix_far = send(mix_near, flipped("y", 1))
    output_near = crossed(after(half_rows(output_table), mix_near))
    project_buffers.append(send(project_buffers[-1], ring("z")))
    project_buffers.append(send(project_buffers[-1], ring("z")))
    project_buffers[3], mix_far = barrier((project_buffers[3], mix_far))
    down_low = turned(first, 3, 5, "z", project_buffers[3])
    down_high = turned(second, 0, 2, "x", up_buffers[3])
    output_far = send(
        after(output_near, project_buffers[3], up_buffers[3]), flipped("y", 1)
    )

    scalars = jnp.stack([spot.z, spot.x, spot.sign, core, spot.yl]).astype(jnp.int32)
    project_full = place(attention_weight, 0, 3, ("z",), project_buffers, scalars)
    mix_full = place_halves(attention_weight[3], mix_near, mix_far, scalars)
    up_full = place(feedforward_weight, 0, 1, ("x",), up_buffers, scalars)[0]

    def down_placed(activated):
        low, high, _ = barrier((down_low[3], down_high[3], activated))
        buffers = [*down_low[:3], low, *down_high[:3], high]
        return place(feedforward_weight, 1, 1, ("z", "x"), buffers, scalars)[0]

    output_full = place_halves(output_table, output_near, output_far, scalars)

    context_far = send(
        after(jnp.where(settled, context_arrived, context_own), output_far), by("y", 2)
    )

    allowed = allowed_mask(window_segments, layout).astype(F32)
    after_block, normed_three, lefts, saved_state = layer_forward(
        residual,
        project_full,
        mix_full,
        up_full,
        down_placed,
        norm_gains,
        allowed,
        (
            (mix_full,),
            (down_low[1], down_high[1], output_near),
            (up_full, down_low[2], down_high[2]),
            (output_far,),
        ),
    )
    heads, totals, mixed_low, after_attention, pre_act, activated, down_full = saved_state
    left_one, left_two, left_three = lefts
    loss_local, grad_logits = head_loss(
        normed_three, output_full, window_tokens, window_segments, keep_flag, spot
    )

    part = contract(grad_logits, output_full, 1, 1)
    other = swap_core(part)
    output_grad = whole_product(left_three, grad_logits)
    output_z = scatter_z(output_grad)
    grad_block, block_low, left_block, norm_three = norm_backward(
        4, norm_gains, after_block, part, after(other, output_grad)
    )
    down_grad = whole_product(left_block, activated)
    down_z = scatter_z(down_grad)
    block_low = after(block_low, down_grad)

    grad_pre, part = feedforward_backward(block_low, down_full, pre_act, up_full)
    other = swap_core(part)
    up_ring = ring_x(spot, left_two, grad_pre, 1024)
    grad_attention, attention_low, left_attention, norm_two = norm_backward(
        2,
        norm_gains,
        after_attention,
        part,
        after(other, up_ring.total),
        grad_block,
    )
    grad_mixed = jnp.dot(attention_low, mix_full, preferred_element_type=F32).astype(BF16)
    grad_projected = attention_backward(heads, allowed, totals, grad_mixed)
    grad_projected, up_one, context_far = barrier((grad_projected, up_ring.arrive(), context_far))
    up_ring.add(up_one)
    grad_projected = after(grad_projected, up_ring.total)
    part = jnp.einsum("ste,sde->td", grad_projected, project_full, preferred_element_type=F32)
    other = swap_core(part)
    project_ring = ring_y(
        spot,
        256,
        (left_one, grad_projected, (1, length, 256), lambda j, half: (j, 0, half), 3),
        (left_attention, mixed_low, (length, 256), lambda j, half: (0, half), 1),
    )
    grad_residual, _, left_residual, norm_one = norm_backward(
        0, norm_gains, residual, part, after(other, project_ring.total), grad_attention
    )

    context_far = context_far + 0.0 * local_seconds
    context = jnp.concatenate([context_near, context_far], axis=1).astype(BF16)

    def columns_of(half):
        side = jnp.where(half == 0, grad_residual[:, : 2 * width], grad_residual[:, 2 * width :])
        return own_quarter(side, core)

    own_grad = jnp.concatenate([columns_of(yh), columns_of(1 - yh)], axis=1)
    own_high = own_grad.astype(BF16)
    own_low = (own_grad - own_high.astype(F32)).astype(BF16)
    hot = (jnp.arange(embed_table.shape[0])[:, None] == window_tokens[None, :]).astype(BF16)
    embed_grad = jnp.dot(hot, own_high, preferred_element_type=F32) + jnp.dot(
        hot, own_low, preferred_element_type=F32
    )
    norms_grad = jnp.concatenate([norm_one, norm_two, norm_three])
    norms_rows = jnp.pad(norms_grad.T, ((0, 0), (0, 122))).reshape(4, 4, 64, 128)

    def condition_part(k, arrived=None):
        left = left_residual.reshape(4, 4, 64, length)
        segments = [
            (left, context, (length, 256), lambda j, s: (0, j), 2),
            (norms_rows, None, None, lambda j, s: (0, 0), 1),
        ]
        return chunk_product(segments, (4, 1, 64, length), 256, k.astype(jnp.int32)[None], arrived)

    condition_ring = Ring("x", spot.x, spot.sign, condition_part)
    condition_ring.total, embed_grad = barrier((condition_ring.total, embed_grad))
    embed_zring = ring_of(spot, "z", embed_grad)
    condition_ring.total, embed_zring.total = barrier((condition_ring.total, embed_zring.total))

    token = condition_ring.total

    def step(ring_here):
        nonlocal token
        arrived, _ = barrier((ring_here.arrive(), token))
        ring_here.add(arrived)
        token = ring_here.total
        return token

    step(up_ring)
    step(condition_ring)
    step(project_ring)
    step(embed_zring)
    up_x = step(up_ring)
    step(condition_ring)
    step(embed_zring)
    down_ring = ring_of(spot, "x", after(jnp.concatenate([down_z, output_z], axis=1), token))
    step(project_ring)
    condition_x = step(condition_ring)
    up_z = scatter_z(jnp.concatenate([up_x, condition_x], axis=1))
    step(down_ring)
    project_y = step(project_ring)
    project_z = scatter_z(project_y)
    embed_z = step(embed_zring)
    step(down_ring)
    embed_ring = ring_of(spot, "x", after(embed_z, token))
    step(down_ring)
    step(embed_ring)
    step(embed_ring)
    step(embed_ring)
    embed_sum = direct_y(spot, embed_ring.total, 64)
    down_x = down_ring.total
    last = direct_y(
        spot,
        jnp.concatenate(
            [
                up_z[:, :1024],
                down_x[:, :1024],
                up_z[:, 2048:2304],
                down_x[:, 2048:2560],
                up_z[:, 2560:2688],
                up_z[:, 1024:2048],
                down_x[:, 1024:2048],
                up_z[:, 2304:2560],
                down_x[:, 2560:],
                up_z[:, 2688:],
            ],
            axis=1,
        ),
        32,
    )
    last_y = direct_sum("x", spot.x, project_z)
    rings = (up_ring, condition_ring, project_ring, down_ring, embed_ring, embed_zring)
    assert all(r.step == 4 for r in rings)
    project_sum, mix_sum = last_y[:, :768], last_y[:, 768:]
    up_sum, down_sum = last[:, :1024], last[:, 1024:2048]
    condition_sum, output_sum = last[:, 2048:2304], last[:, 2304:2816]
    norms_both = last[:, 2816:].reshape(2, 16, 128)
    norms_share = lax.dynamic_index_in_dim(norms_both, core, 0, False)[:, :6].T

    sums = [output_sum, down_sum, up_sum, mix_sum, project_sum, condition_sum, embed_sum]
    squares = 0.5 * jnp.sum((norms_share * SQUARE_SCALE) ** 2)
    for piece in sums:
        squares = squares + jnp.sum((piece * SQUARE_SCALE) ** 2)
    scalars = jnp.stack([0.5 * loss_local, squares, 0.5 * local_seconds])
    flat = [piece.reshape(2, 16, -1) for piece in sums[:-1]] + [sums[-1].reshape(2, 16, 512)]
    flat = jnp.concatenate(flat, axis=2)
    mine = lax.dynamic_index_in_dim(flat, core, 0, False)
    theirs = swap_core(lax.dynamic_index_in_dim(flat, 1 - core, 0, False))
    scalars = pair_sum(jnp.broadcast_to(scalars[:, None], (3, 128)))
    scalars = sum_of_four(scalars, "x", spot.x)
    scalars = sum_of_four(after(scalars, theirs), "z", spot.z)
    scalars = sum_of_four(scalars, "y", spot.y)
    loss_total, seconds_total = scalars[0, 0], scalars[2, 0]
    inverse = 1.0 / seconds_total
    gradient_norm = jnp.sqrt(scalars[1, 0]) * (inverse / SQUARE_SCALE)
    clip_factor = CLIP_NORM / jnp.maximum(gradient_norm, CLIP_NORM)

    low_side = jnp.where(core == 0, mine, theirs)
    high_side = jnp.where(core == 0, theirs, mine)

    def share(start, stop):
        return low_side[:, start:stop], high_side[:, start:stop]

    output_share = jnp.concatenate(share(0, 512), axis=1)
    feedforward_share = jnp.stack(
        [jnp.concatenate(share(1536, 2560), axis=1), jnp.concatenate(share(512, 1536), axis=1)]
    )
    mix_low, mix_high = share(2560, 2816)
    project_low, project_high = share(2816, 3584)
    attention_share = jnp.stack(
        [
            jnp.concatenate(
                [project_low[:, 256 * k : 256 * k + 256], project_high[:, 256 * k : 256 * k + 256]],
                axis=1,
            )
            for k in range(3)
        ]
        + [jnp.concatenate([mix_low, mix_high], axis=1)]
    )
    condition_share = jnp.concatenate(share(3584, 3840), axis=1)
    embed_share = jnp.concatenate([part.reshape(32, 256) for part in share(3840, 4352)], axis=1)

    shares = (
        embed_share,
        condition_share,
        attention_share,
        feedforward_share,
        output_share,
        norms_share,
    )
    masters = (
        embed_master,
        condition_master,
        attention_master,
        feedforward_master,
        output_master,
        norms_master,
    )
    firsts = (
        embed_first,
        condition_first,
        attention_first,
        feedforward_first,
        output_first,
        norms_first,
    )
    seconds_old = (
        embed_second,
        condition_second,
        attention_second,
        feedforward_second,
        output_second,
        norms_second,
    )
    rates = (RATE_TABLE, RATE_MATRIX, RATE_MATRIX, RATE_MATRIX, RATE_MATRIX, RATE_NORMS)
    decays = (WEIGHT_DECAY, WEIGHT_DECAY, WEIGHT_DECAY, WEIGHT_DECAY, WEIGHT_DECAY, 0.0)
    outputs = [loss_total, seconds_total, gradient_norm]
    for slot in range(6):
        outputs += adam_step(
            shares[slot] * inverse * clip_factor,
            masters[slot],
            firsts[slot],
            seconds_old[slot],
            rates[slot],
            decays[slot],
        )
    return tuple(outputs)


def solution(mesh):
    torus = Mesh(mesh.devices.reshape(SIZES), AXES)
    table, slotted = P(DP, "yh"), P(None, DP, "yh")
    state = (table, table, slotted, slotted, table, P(None, DP))
    results = tuple(spec for spec in state for _ in range(3))
    return jax.shard_map(
        local,
        mesh=torus,
        in_specs=(
            P(DP),
            P(DP),
            P(),
            P(DP),
            P(DP),
            table,
            P(None, "yh"),
            P(None, "yh"),
            P(None, None, "yh"),
            P(None, None, "yh"),
            P(None, "yh"),
            P(),
        )
        + state * 3,
        out_specs=(P(), P(), P()) + results,
        check_vma=False,
    )
```

```python
import functools

import jax
import jax.numpy as jnp
import numpy as np
from jax import lax
from jax.experimental import pallas as pl
from jax.experimental.pallas import tpu as pltpu
from jax.sharding import Mesh
from jax.sharding import PartitionSpec as P

HEAD_DIM = 64
BLK = 64
CLIPS_DEV = 4
STEP = 10


LAYER_EPS = 1e-05
SAMPLE_RATE = 44100.0
LOG_TWO_NATS = 0.6931471805599453
CLIP_NORM = 1.0
BETA_FIRST = 0.9
BETA_SECOND = 0.95
ADAM_EPSILON = 1e-08
WEIGHT_DECAY = 0.01
RATE_MATRIX = 0.1
RATE_TABLE = 1.0
RATE_NORMS = 1.0
SQUARE_SCALE = 2.0**-9

AXES = ("z", "x", "yl", "c", "yh")
SIZES = (4, 4, 2, 2, 2)
DP = ("z", "x", "yl", "c")
MIB = 1024 * 1024
QUERY_ROWS = 256
BF16 = jnp.bfloat16
F32 = jnp.float32


def send(value, move):
    pairs = []
    for index in range(int(np.prod(SIZES))):
        z, x, yl, c, yh = (int(i) for i in np.unravel_index(index, SIZES))
        target = move(z, x, yh * 2 + yl, c)
        if target is not None:
            z, x, y, c = target
            y %= 4
            at = (z % 4, x % 4, y % 2, c, y // 2)
            pairs.append((index, int(np.ravel_multi_index(at, SIZES))))
    return lax.ppermute(value, AXES, pairs)


def swap_core(value):
    return send(value, lambda z, x, y, c: (z, x, y, 1 - c))


def pair_sum(value):
    return value + swap_core(value)


def ring(axis):
    def move(z, x, y, c):
        step = 1 - 2 * c
        return {"z": (z + step, x, y, c), "x": (z, x + step, y, c), "y": (z, x, y + step, c)}[axis]

    return move


def by(axis, count):
    def move(z, x, y, c):
        return {"z": (z + count, x, y, c), "x": (z, x + count, y, c), "y": (z, x, y + count, c)}[axis]

    return move


def flipped(axis, bit):
    def move(z, x, y, c):
        return {"z": (z ^ bit, x, y, c), "x": (z, x ^ bit, y, c), "y": (z, x, y ^ bit, c)}[axis]

    return move


def after(value, *earlier):
    return lax.optimization_barrier((value, *earlier))[0]


def pieces_kernel(s_ref, *refs):
    width = 0
    for ref in refs[:-1]:
        refs[-1][:, width : width + ref.shape[-1]] = ref[0].astype(F32)
        width += ref.shape[-1]


def pieces_of(attention_weight, feedforward_weight, index):
    narrow, wide = attention_weight.shape[2] // 2, feedforward_weight.shape[2] // 2
    specs = [pl.BlockSpec((1, 64, narrow), lambda g, s, k=k: (k, s[0], s[1])) for k in range(3)]
    specs += [pl.BlockSpec((1, 64, wide), lambda g, s, k=k: (k, s[0], s[1])) for k in (1, 0)]
    width = 3 * narrow + 2 * wide
    return pl.pallas_call(
        pieces_kernel,
        grid_spec=pltpu.PrefetchScalarGridSpec(
            num_scalar_prefetch=1,
            grid=(1,),
            in_specs=specs,
            out_specs=pl.BlockSpec((64, width), lambda g, s: (0, 0)),
        ),
        out_shape=jax.ShapeDtypeStruct((64, width), F32),
        compiler_params=pltpu.CompilerParams(vmem_limit_bytes=8 * MIB),
        cost_estimate=estimate(1, 1),
    )(index, *in_hbm(*[attention_weight] * 3, *[feedforward_weight] * 2))


def own_quarter(half, core):
    width = half.shape[-1] // 2
    return jnp.where(core == 0, half[..., :width], half[..., width:])


def place_kernel(rings, s_ref, native_ref, *rest):
    out_ref = rest[-1]
    width = native_ref.shape[-1]
    part = width // len(rings)
    out_ref[0, :, :width] = native_ref[0]
    z, x, sign = s_ref[0], s_ref[1], s_ref[2]
    for r, axis in enumerate(rings):
        lanes = slice(width + r * part, width + (r + 1) * part)
        for j in range(4):
            for i in range(4):
                z_at = lax.rem(z - sign * (j if axis == "z" else i) + 8, 4)
                x_at = lax.rem(x - sign * (j if axis == "x" else i) + 8, 4)
                rows = pl.ds(pl.multiple_of(z_at * 256 + x_at * 64, 64), 64)
                out_ref[0, rows, lanes] = rest[4 * r + j][i].astype(BF16)


def place(native, first_slot, slots, rings, buffers, scalars):
    rows, width = native.shape[1], native.shape[2] // 2
    block = pl.BlockSpec((4, 64, width // len(rings)), lambda k, s: (0, 0, k))
    return pl.pallas_call(
        functools.partial(place_kernel, rings),
        grid_spec=pltpu.PrefetchScalarGridSpec(
            num_scalar_prefetch=1,
            grid=(slots,),
            in_specs=[pl.BlockSpec((1, rows, width), lambda k, s: (first_slot + k, 0, s[3]))]
            + [block] * len(buffers),
            out_specs=pl.BlockSpec((1, rows, 2 * width), lambda k, s: (k, 0, 0)),
        ),
        out_shape=jax.ShapeDtypeStruct((slots, rows, 2 * width), BF16),
        compiler_params=pltpu.CompilerParams(vmem_limit_bytes=24 * MIB),
        cost_estimate=estimate(1, 1),
    )(scalars, *in_hbm(native), *buffers)


def place_halves_kernel(s_ref, native_ref, near_ref, far_ref, out_ref):
    half, width = near_ref.shape
    out_ref[:, :width] = native_ref[...]
    near = s_ref[4]
    out_ref[pl.ds(pl.multiple_of(near * half, 64), half), width:] = near_ref[...].astype(BF16)
    out_ref[pl.ds(pl.multiple_of((1 - near) * half, 64), half), width:] = far_ref[...].astype(BF16)


def place_halves(native, near, far, scalars):
    rows, width = native.shape[0], native.shape[1] // 2
    whole = pl.BlockSpec((rows // 2, width), lambda k, s: (0, 0))
    return pl.pallas_call(
        place_halves_kernel,
        grid_spec=pltpu.PrefetchScalarGridSpec(
            num_scalar_prefetch=1,
            grid=(1,),
            in_specs=[pl.BlockSpec((rows, width), lambda k, s: (0, s[3])), whole, whole],
            out_specs=pl.BlockSpec((rows, 2 * width), lambda k, s: (0, 0)),
        ),
        out_shape=jax.ShapeDtypeStruct((rows, 2 * width), BF16),
        compiler_params=pltpu.CompilerParams(vmem_limit_bytes=12 * MIB),
        cost_estimate=pl.CostEstimate(
            flops=0, bytes_accessed=rows * width * 10, transcendentals=0
        ),
    )(scalars, *in_hbm(native), near, far)


def direct(value, axis):
    return jnp.stack([value] + [send(value, by(axis, k)) for k in (1, 2, 3)])


def around(buffer, axis):
    buffers = [buffer]
    for _ in range(3):
        buffers.append(send(buffers[-1], ring(axis)))
    return buffers


class Ring:
    def __init__(self, axis, place_at, sign, part):
        self.axis, self.place_at, self.sign, self.part = axis, place_at, sign, part
        self.step = 1
        self.total = part(lax.rem(place_at - sign + 8, 4))

    def arrive(self):
        return send(self.total, ring(self.axis))

    def add(self, arrived):
        self.step += 1
        own = lax.rem(self.place_at - self.step * self.sign + 8, 4)
        self.total = self.part(own, arrived)


def ring_of(spot, axis, grad):
    view = grad.reshape(1, 4, -1, grad.shape[1])

    def part(k, arrived=None):
        return chunk_added(view, k.astype(jnp.int32)[None], arrived)

    return Ring(axis, spot.z if axis == "z" else spot.x, spot.sign, part)


def added(product, arrived):
    return product if arrived is None else product + arrived


def ring_x(spot, left, right, tile):
    left = left.reshape(4, 4, -1, left.shape[-1])
    segment = (left, right, (right.shape[0], tile), lambda j, s: (0, j), right.shape[1] // tile)

    def part(k, arrived=None):
        index = k.astype(jnp.int32)[None]
        return chunk_product([segment], (4, 1, *left.shape[2:]), tile, index, arrived)

    return Ring("x", spot.x, spot.sign, part)


def ring_y(spot, tile, *segments):
    tokens = segments[0][0].shape[-1]
    rest = segments[0][0].shape[0] // 32

    def part(k, arrived=None):
        half = jnp.where(lax.div(k, 2) == spot.yh, 0, 1)
        index = jnp.stack([lax.rem(k, 2), half]).astype(jnp.int32)
        turned = [
            (left.reshape(16, 2, rest, tokens), right, block, lambda j, s, at=at: at(j, s[1]), tiles)
            for left, right, block, at, tiles in segments
        ]
        return chunk_product(turned, (16, 1, rest, tokens), tile, index, arrived)

    return Ring("y", spot.y, spot.sign, part)


def whole_product(left, right):
    segment = (left[None, None], right, (right.shape[0], 512), lambda j, s: (0, j), right.shape[1] // 512)
    none = jnp.zeros((1,), jnp.int32)
    return chunk_product([segment], (1, 1, *left.shape), 512, none, None, pltpu.HBM)


def scatter_z(grad):
    return lax.psum_scatter(grad, "z", scatter_dimension=0, tiled=True)


def direct_y(spot, grad, rows):
    width = grad.shape[1] // 2
    view = grad.reshape(-1, 2, rows, 2 * width)
    same = lax.dynamic_index_in_dim(view, spot.yl, 1, False)
    other = lax.dynamic_index_in_dim(view, 1 - spot.yl, 1, False)
    near = send(other[..., :width], flipped("y", 1))
    far = send(other[..., width:], flipped("y", 3))
    across = send(same[..., width:], flipped("y", 2))
    return ((same[..., :width] + near) + (far + across)).reshape(-1, width)


def direct_sum(axis, place_at, grad, outer=1):
    view = grad.reshape(outer, 4, grad.shape[0] // (4 * outer), grad.shape[1])
    parts = [
        send(lax.dynamic_index_in_dim(view, lax.rem(place_at + k, 4), 1, False), by(axis, k))
        for k in (1, 2, 3)
    ]
    own = lax.dynamic_index_in_dim(view, place_at, 1, False)
    return ((own + parts[0]) + (parts[1] + parts[2])).reshape(-1, grad.shape[1])


def turned(value):
    return lax.optimization_barrier(value.T)


class Spot:
    def __init__(self):
        self.z, self.x, self.yl, self.c, self.yh = (lax.axis_index(a) for a in AXES)
        self.y = self.yh * 2 + self.yl
        self.sign = 1 - 2 * self.c


def sum_of_four(value, axis, place_at):
    pieces = [value] + [send(value, by(axis, k)) for k in (1, 2, 3)]
    total = None
    for at in range(4):
        back = lax.rem(place_at - at + 4, 4)
        part = pieces[3]
        for k in (2, 1, 0):
            part = jnp.where(back == k, pieces[k], part)
        total = part if total is None else total + part
    return total


def contract(left_side, right_side, left_dim, right_dim):
    return lax.dot_general(
        left_side,
        right_side,
        (((left_dim,), (right_dim,)), ((), ())),
        preferred_element_type=jnp.float32,
    )


def attention_forward_kernel(heads_ref, mask_ref, out_ref, total_ref):
    length = heads_ref.shape[1]
    for half in range(2):
        lanes = slice(half * HEAD_DIM, (half + 1) * HEAD_DIM)
        keys, values = heads_ref[1, :, lanes], heads_ref[2, :, lanes]
        scaled = heads_ref[0, :, lanes] * jnp.asarray(HEAD_DIM ** (-0.5), BF16)
        for start in range(0, length, QUERY_ROWS):
            stop = start + QUERY_ROWS
            scores = contract(scaled[start:stop], keys[:stop], 1, 1)
            scores = jnp.where(mask_ref[start:stop, :stop] > 0, scores, -1e30)
            top = jnp.max(scores, axis=-1, keepdims=True)
            weights = jnp.exp(scores - top)
            sums = jnp.sum(weights, axis=-1, keepdims=True)
            weights = (weights * (1.0 / sums)).astype(BF16)
            out_ref[start:stop, lanes] = contract(weights, values[:stop], 1, 0).astype(BF16)
            total_ref[0, start:stop, half : half + 1] = top + jnp.log(sums)


def attention_backward_kernel(heads_ref, mask_ref, total_ref, grad_ref, out_ref, keys_acc, values_acc):
    length = heads_ref.shape[1]
    for half in range(2):
        lanes = slice(half * HEAD_DIM, (half + 1) * HEAD_DIM)
        keys, values = heads_ref[1, :, lanes], heads_ref[2, :, lanes]
        scaled = heads_ref[0, :, lanes] * jnp.asarray(HEAD_DIM ** (-0.5), BF16)
        for start in range(length - QUERY_ROWS, -1, -QUERY_ROWS):
            stop = start + QUERY_ROWS
            queries, grad = scaled[start:stop], grad_ref[start:stop, lanes]
            scores = contract(queries, keys[:stop], 1, 1)
            scores = jnp.where(mask_ref[start:stop, :stop] > 0, scores, -1e30)
            weights = jnp.exp(scores - total_ref[0, start:stop, half : half + 1])
            grad_values = contract(weights.astype(BF16), grad, 0, 0)
            grad_weights = contract(grad, values[:stop], 1, 1)
            total = jnp.sum(weights * grad_weights, axis=-1, keepdims=True)
            grad_scores = (weights * (grad_weights - total)).astype(BF16)
            grad_queries = contract(grad_scores, keys[:stop], 1, 0) * HEAD_DIM ** (-0.5)
            out_ref[0, start:stop, lanes] = grad_queries.astype(BF16)
            grad_keys = contract(grad_scores, queries, 0, 0)
            if stop == length:
                keys_acc[...] = grad_keys
                values_acc[...] = grad_values
            else:
                keys_acc[:stop] += grad_keys
                values_acc[:stop] += grad_values
        out_ref[1, :, lanes] = keys_acc[...].astype(BF16)
        out_ref[2, :, lanes] = values_acc[...].astype(BF16)


def estimate(flops, moved):
    return pl.CostEstimate(flops=flops, bytes_accessed=moved, transcendentals=0)


def in_hbm(*values):
    return [pltpu.with_memory_space_constraint(value, pltpu.HBM) for value in values]


def norm_forward_kernel(row, parts, base_ref, *rest):
    ins, outs = rest[: parts + 1], rest[parts + 1 :]
    gains_ref = ins[-1]
    values = base_ref[...]
    if parts:
        values = values + (ins[0][...] + ins[1][...])
        outs[2][...] = values
    centred = values - jnp.mean(values, axis=-1, keepdims=True)
    variance = jnp.mean(centred * centred, axis=-1, keepdims=True)
    normed = centred * lax.rsqrt(variance + LAYER_EPS) * gains_ref[row : row + 1] + gains_ref[row + 1 : row + 2]
    outs[0][...] = normed.astype(BF16)
    outs[1][...] = normed.T.astype(BF16)


def norm_forward(row, gains, base, parts=()):
    length, width = base.shape
    rows = 256
    block = pl.BlockSpec((rows, width), lambda g: (g, 0))
    turned = pl.BlockSpec((width, rows), lambda g: (0, g))
    shapes = [jax.ShapeDtypeStruct((length, width), BF16), jax.ShapeDtypeStruct((width, length), BF16)]
    if parts:
        shapes.append(jax.ShapeDtypeStruct((length, width), F32))
    return pl.pallas_call(
        functools.partial(norm_forward_kernel, row, len(parts)),
        grid=(length // rows,),
        in_specs=[block] * (1 + len(parts)) + [pl.BlockSpec(gains.shape, lambda g: (0, 0))],
        out_specs=[block, turned, block][: len(shapes)],
        out_shape=shapes,
        compiler_params=pltpu.CompilerParams(vmem_limit_bytes=22 * MIB),
        cost_estimate=estimate(1, 1),
    )(base, *parts, gains)


def norm_backward_kernel(row, has_base, values_ref, part_ref, other_ref, gains_ref, *rest):
    if has_base:
        base_ref, rest = rest[0], rest[1:]
    out_ref, low_ref, turned_ref, sums_ref = rest
    values = values_ref[...]
    grad = part_ref[...] + other_ref[...]
    centred = values - jnp.mean(values, axis=-1, keepdims=True)
    scale = lax.rsqrt(jnp.mean(centred * centred, axis=-1, keepdims=True) + LAYER_EPS)
    normed = centred * scale
    gained = grad * gains_ref[row : row + 1]
    inner = gained - jnp.mean(gained, axis=-1, keepdims=True)
    inner = scale * (inner - normed * jnp.mean(gained * normed, axis=-1, keepdims=True))
    if has_base:
        inner = base_ref[...] + inner
    out_ref[...] = inner
    low_ref[...] = inner.astype(BF16)
    turned_ref[...] = inner.T.astype(BF16)
    sums = jnp.concatenate(
        [jnp.sum(grad * normed, axis=0, keepdims=True), jnp.sum(grad, axis=0, keepdims=True)], axis=0
    )

    @pl.when(pl.program_id(0) == 0)
    def _():
        sums_ref[...] = sums

    @pl.when(pl.program_id(0) > 0)
    def _():
        sums_ref[...] += sums


def norm_backward(row, gains, values, part, other, base=None):
    length, width = values.shape
    rows = 256
    block = pl.BlockSpec((rows, width), lambda g: (g, 0))
    operands = [values, part, other, gains] + ([] if base is None else [base])
    specs = [block] * 3 + [pl.BlockSpec(gains.shape, lambda g: (0, 0))] + ([] if base is None else [block])
    return pl.pallas_call(
        functools.partial(norm_backward_kernel, row, base is not None),
        grid=(length // rows,),
        in_specs=specs,
        out_specs=[
            block,
            block,
            pl.BlockSpec((width, rows), lambda g: (0, g)),
            pl.BlockSpec((2, width), lambda g: (0, 0)),
        ],
        out_shape=[
            jax.ShapeDtypeStruct((length, width), F32),
            jax.ShapeDtypeStruct((length, width), BF16),
            jax.ShapeDtypeStruct((width, length), BF16),
            jax.ShapeDtypeStruct((2, width), F32),
        ],
        compiler_params=pltpu.CompilerParams(vmem_limit_bytes=26 * MIB),
        cost_estimate=estimate(1, 1),
    )(*operands)


def chunk_kernel(bounds, plain, has_recv, s_ref, *rest):
    out_ref = rest[-1]
    for n, (start, stop) in enumerate(bounds):
        left_ref, right_ref = rest[2 * n], rest[2 * n + 1]

        @pl.when((pl.program_id(0) >= start) & (pl.program_id(0) < stop))
        def _(left_ref=left_ref, right_ref=right_ref):
            if plain[n]:
                total = left_ref[...].reshape(out_ref.shape[0], left_ref.shape[-1])
                total = jnp.concatenate([total, total], axis=1)
            else:
                left = left_ref[...].reshape(out_ref.shape[0], left_ref.shape[-1])
                right = right_ref[...].reshape(right_ref.shape[-2:])
                total = jnp.dot(left, right, preferred_element_type=F32)
            if has_recv:
                total += rest[2 * len(bounds)][...]
            out_ref[...] = total


def chunk_product(segments, left_block, tile, index, arrived, place_for=jax.ShapeDtypeStruct):
    rows = int(np.prod(left_block[:-1]))
    out_spec = pl.BlockSpec((rows, tile), lambda j, s: (0, j))
    operands, specs, bounds, start = [], [], [], 0
    for left, right, right_block, right_at, tiles in segments:

        def at(j, s, start=start, tiles=tiles, right_at=right_at):
            return right_at(jnp.clip(j - start, 0, tiles - 1), s)

        operands += [left, index if right is None else right]
        specs += [
            pl.BlockSpec((*left_block[:-1], left.shape[-1]), lambda j, s: (0, s[0], 0, 0)),
            pl.BlockSpec(memory_space=pltpu.SMEM) if right is None else pl.BlockSpec(right_block, at),
        ]
        bounds.append((start, start + tiles))
        start += tiles
    extra = [] if arrived is None else [arrived]
    return pl.pallas_call(
        functools.partial(
            chunk_kernel, tuple(bounds), [seg[1] is None for seg in segments], arrived is not None
        ),
        grid_spec=pltpu.PrefetchScalarGridSpec(
            num_scalar_prefetch=1,
            grid=(start,),
            in_specs=specs + [out_spec] * len(extra),
            out_specs=out_spec,
        ),
        out_shape=place_for((rows, tile * start), F32),
        compiler_params=pltpu.CompilerParams(vmem_limit_bytes=16 * MIB),
        cost_estimate=estimate(1, 1),
    )(index, *operands, *extra)


def add_kernel(s_ref, own_ref, *rest):
    out_ref = rest[-1]
    total = own_ref[0, 0]
    for arrived_ref in rest[:-1]:
        total = total + arrived_ref[...]
    out_ref[...] = total


def chunk_added(view, index, arrived):
    rows, width = view.shape[2:]
    tile = width // 2
    out_spec = pl.BlockSpec((rows, tile), lambda j, s: (0, j))
    extra = [] if arrived is None else [arrived]
    return pl.pallas_call(
        add_kernel,
        grid_spec=pltpu.PrefetchScalarGridSpec(
            num_scalar_prefetch=1,
            grid=(2,),
            in_specs=[pl.BlockSpec((1, 1, rows, tile), lambda j, s: (0, s[0], 0, j))]
            + [out_spec] * len(extra),
            out_specs=out_spec,
        ),
        out_shape=jax.ShapeDtypeStruct((rows, width), F32),
        compiler_params=pltpu.CompilerParams(vmem_limit_bytes=8 * MIB),
        cost_estimate=estimate(1, 1),
    )(index, view, *extra)


def attention_forward(heads, mask):
    length, width = heads.shape[1:]
    return pl.pallas_call(
        attention_forward_kernel,
        grid=(width // 128,),
        in_specs=[
            pl.BlockSpec((3, length, 128), lambda g: (0, 0, g)),
            pl.BlockSpec((length, length), lambda g: (0, 0)),
        ],
        out_specs=[
            pl.BlockSpec((length, 128), lambda g: (0, g)),
            pl.BlockSpec((1, length, 2), lambda g: (g, 0, 0)),
        ],
        out_shape=[
            jax.ShapeDtypeStruct((length, width), BF16),
            jax.ShapeDtypeStruct((width // 128, length, 2), F32),
        ],
        compiler_params=pltpu.CompilerParams(vmem_limit_bytes=16 * MIB),
        cost_estimate=estimate(1, 1),
    )(heads, mask)


def attention_backward(heads, mask, totals, grad_mixed):
    length, width = heads.shape[1:]
    return pl.pallas_call(
        attention_backward_kernel,
        grid=(width // 128,),
        in_specs=[
            pl.BlockSpec((3, length, 128), lambda g: (0, 0, g)),
            pl.BlockSpec((length, length), lambda g: (0, 0)),
            pl.BlockSpec((1, length, 2), lambda g: (g, 0, 0)),
            pl.BlockSpec((length, 128), lambda g: (0, g)),
        ],
        out_specs=pl.BlockSpec((3, length, 128), lambda g: (0, 0, g)),
        out_shape=jax.ShapeDtypeStruct((3, length, width), BF16),
        scratch_shapes=[pltpu.VMEM((length, HEAD_DIM), F32), pltpu.VMEM((length, HEAD_DIM), F32)],
        compiler_params=pltpu.CompilerParams(vmem_limit_bytes=16 * MIB),
        cost_estimate=estimate(1, 1),
    )(heads, mask, totals, grad_mixed)


def feedforward_backward_kernel(block_ref, down_ref, pre_ref, up_ref, grad_pre_ref, normed_ref):
    grad_activated = jnp.dot(block_ref[...], down_ref[...], preferred_element_type=F32)
    pre = pre_ref[...]
    slope = 0.7978845608028654
    square = pre * pre
    bent = jnp.tanh(pre * (slope + (slope * 0.044715) * square))
    inner = pre * (0.5 * slope + (1.5 * slope * 0.044715) * square)
    factor = (0.5 + 0.5 * bent) + inner * (1.0 - bent * bent)
    grad_pre = (grad_activated * factor).astype(BF16)
    grad_pre_ref[...] = grad_pre
    part = contract(grad_pre, up_ref[...], 1, 1)

    @pl.when(pl.program_id(0) == 0)
    def _():
        normed_ref[...] = part

    @pl.when(pl.program_id(0) > 0)
    def _():
        normed_ref[...] += part


def feedforward_backward(block_low, down_full, pre_act, up_full):
    length, hidden = pre_act.shape
    width, tile = block_low.shape[1], 1024
    return pl.pallas_call(
        feedforward_backward_kernel,
        grid=(hidden // tile,),
        in_specs=[
            pl.BlockSpec((length, width), lambda g: (0, 0)),
            pl.BlockSpec((width, tile), lambda g: (0, g)),
            pl.BlockSpec((length, tile), lambda g: (0, g)),
            pl.BlockSpec((width, tile), lambda g: (0, g)),
        ],
        out_specs=[
            pl.BlockSpec((length, tile), lambda g: (0, g)),
            pl.BlockSpec((length, width), lambda g: (0, 0)),
        ],
        out_shape=[
            jax.ShapeDtypeStruct((length, hidden), BF16),
            jax.ShapeDtypeStruct((length, width), F32),
        ],
        compiler_params=pltpu.CompilerParams(vmem_limit_bytes=36 * MIB),
        cost_estimate=estimate(1, 1),
    )(*in_hbm(block_low, down_full, pre_act, up_full))


def allowed_mask(segments, layout):
    length = segments.shape[0]
    position = jnp.arange(length)
    blocks = layout.shape[0]
    block_open = (
        jnp.broadcast_to(layout[:, None, :, None], (blocks, BLK, blocks, BLK)).reshape(
            length, length
        )
        > 0
    )
    causal = position[None, :] <= position[:, None]
    return causal & (segments[:, None] == segments[None, :]) & block_open


def layer_forward(residual, project_weight, mix_weight, up_weight, down_weight, norm_gains, mask, early):
    normed_one, left_one = norm_forward(0, norm_gains, residual)
    heads = jnp.einsum(
        "td,sde->ste", normed_one, project_weight, preferred_element_type=jnp.float32
    ).astype(jnp.bfloat16)
    heads = after(heads, *early[0])
    mixed_low, totals = attention_forward(heads, mask)
    mixed_low = after(mixed_low, *early[1])
    part = contract(mixed_low, mix_weight, 1, 1)
    other = after(swap_core(part), *early[2])
    normed_two, left_two, after_attention = norm_forward(2, norm_gains, residual, (part, other))
    pre_act = jnp.dot(normed_two, up_weight, preferred_element_type=jnp.float32)
    activated = jax.nn.gelu(pre_act).astype(jnp.bfloat16)
    activated = after(activated, *early[3])
    down_full = down_weight(activated)
    part = contract(activated, down_full, 1, 1)
    normed_three, left_three, after_block = norm_forward(
        4, norm_gains, after_attention, (part, swap_core(part))
    )
    saved_state = (heads, totals, mixed_low, after_attention, pre_act, activated, down_full)
    return (after_block, normed_three, (left_one, left_two, left_three), saved_state)


def head_loss(normed_three, output_table, code_tokens, segments, keep_flag, spot):
    logits = jnp.dot(normed_three, output_table, preferred_element_type=jnp.float32)
    width = output_table.shape[1]
    quarter = width // 2
    targets = jnp.concatenate([code_tokens[1:], code_tokens[-1:]])
    column = jnp.arange(width)
    code = jnp.where(
        column < quarter,
        spot.yh * width + spot.c * quarter + column,
        (1 - spot.yh) * width + spot.c * quarter + column - quarter,
    )
    target_hit = code[None, :] == targets[:, None]
    row_top = jnp.max(logits, axis=1)
    row_sums = jnp.sum(jnp.exp(logits - row_top[:, None]), axis=1)
    picked = jnp.sum(jnp.where(target_hit, logits, 0.0), axis=1)
    other = swap_core(jnp.stack([row_top, row_sums, picked]))
    both_top = jnp.maximum(row_top, other[0])
    both_sums = row_sums * jnp.exp(row_top - both_top) + other[1] * jnp.exp(other[0] - both_top)
    log_norm = both_top + jnp.log(both_sums)
    next_segment = jnp.concatenate([segments[1:], jnp.full((1,), -1, jnp.int32)])
    counted = ((segments == next_segment) & (segments < CLIPS_DEV)).astype(jnp.float32) * keep_flag
    loss_local = jnp.sum(counted * (log_norm - (picked + other[2]))) / LOG_TWO_NATS
    grad_logits = (counted / LOG_TWO_NATS)[:, None] * (
        jnp.exp(logits - log_norm[:, None]) - target_hit.astype(jnp.float32)
    )
    grad_low = grad_logits.astype(jnp.bfloat16)
    return (loss_local, grad_low)


def adam_step(gradient, master, first_old, second_old, step_rate, decay_rate):
    moment = BETA_FIRST * first_old + (1.0 - BETA_FIRST) * gradient
    variance = BETA_SECOND * second_old + (1.0 - BETA_SECOND) * gradient * gradient
    moment_hat = moment / (1.0 - BETA_FIRST**STEP)
    variance_hat = variance / (1.0 - BETA_SECOND**STEP)
    updated = master - step_rate * (
        moment_hat / (jnp.sqrt(variance_hat) + ADAM_EPSILON) + decay_rate * master
    )
    return (moment, variance, updated)


def local(
    code_tokens,
    segments,
    layout,
    durations,
    overflow,
    upper_context,
    embed_table,
    condition_weight,
    attention_weight,
    feedforward_weight,
    output_table,
    norm_gains,
    embed_master,
    condition_master,
    attention_master,
    feedforward_master,
    output_master,
    norms_master,
    embed_first,
    condition_first,
    attention_first,
    feedforward_first,
    output_first,
    norms_first,
    embed_second,
    condition_second,
    attention_second,
    feedforward_second,
    output_second,
    norms_second,
):
    spot = Spot()
    core, yh = spot.c, spot.yh
    settled = core == yh
    length = code_tokens.shape[0]

    keep_native = 1.0 - overflow[0].astype(jnp.float32)
    local_seconds = keep_native * jnp.sum(durations.astype(jnp.float32)) / SAMPLE_RATE
    native_ints = jnp.concatenate([code_tokens, segments, jnp.broadcast_to(overflow, (128,))])
    window_ints = jnp.where(settled, native_ints, swap_core(native_ints))
    window_tokens = window_ints[:length]
    window_segments = window_ints[length : 2 * length]
    keep_flag = 1.0 - window_ints[2 * length].astype(jnp.float32)

    barrier = lax.optimization_barrier

    def crossed(value):
        return send(value, lambda z, x, y, c: (z, x, 3 - y, c))

    block = spot.z * 4 + spot.x
    own_pieces = pieces_of(
        attention_weight, feedforward_weight, jnp.stack([block, core]).astype(jnp.int32)
    )
    own_pieces, upper_context = barrier((own_pieces, upper_context))
    pieces = crossed(own_pieces)
    quarter = attention_weight.shape[2] // 2

    embedded = jnp.take(embed_table, code_tokens, axis=0).astype(F32)
    half_width = embed_table.shape[1]
    embed_part = contract(upper_context, condition_weight, 1, 1)
    embed_part = jnp.concatenate(
        [
            embed_part[:, :half_width] + jnp.where(yh == 0, embedded, 0.0),
            embed_part[:, half_width:] + jnp.where(yh == 1, embedded, 0.0),
        ],
        axis=1,
    )
    width = half_width // 2
    context_own = own_quarter(upper_context, core).astype(F32)
    context_arrived = swap_core(own_quarter(upper_context, 1 - core).astype(F32))
    embed_part, pieces, context_arrived = barrier((embed_part, pieces, context_arrived))
    context_near = jnp.where(settled, context_own, context_arrived)
    from_other = send(
        embed_part,
        lambda z, x, y, c: (z, x, y ^ 2, c) if c != y // 2 else None,
    )
    first, second = [pieces[:, : 5 * quarter]], [pieces[:, 5 * quarter :]]
    for _ in range(3):
        first.append(send(first[-1], ring("x")))
        second.append(send(second[-1], ring("z")))
    window_sum = embed_part + from_other
    residual = jnp.where(settled, window_sum, swap_core(window_sum))

    def half_rows(native):
        halves = own_quarter(native, core).reshape(2, native.shape[0] // 2, -1)
        return lax.dynamic_index_in_dim(halves, 1 - spot.yl, 0, False).astype(F32)

    def turned(pieces, start, stop, axis, *earlier):
        columns = jnp.stack([piece[:, start * quarter : stop * quarter] for piece in pieces])
        return around(after(columns, *earlier), axis)

    up_buffers = turned(second, 2, 6, "x")
    project_buffers = [jnp.stack([piece[:, : 3 * quarter] for piece in first])]
    mix_near = crossed(after(half_rows(attention_weight[3]), from_other))
    project_buffers.append(send(project_buffers[-1], ring("z")))
    project_buffers[1], mix_near = barrier((project_buffers[1], mix_near))
    mix_far = send(mix_near, flipped("y", 1))
    output_near = crossed(after(half_rows(output_table), mix_near))
    project_buffers.append(send(project_buffers[-1], ring("z")))
    project_buffers.append(send(project_buffers[-1], ring("z")))
    project_buffers[3], mix_far = barrier((project_buffers[3], mix_far))
    down_low = turned(first, 3, 5, "z", project_buffers[3])
    down_high = turned(second, 0, 2, "x", up_buffers[3])
    output_far = send(
        after(output_near, project_buffers[3], up_buffers[3]), flipped("y", 1)
    )

    scalars = jnp.stack([spot.z, spot.x, spot.sign, core, spot.yl]).astype(jnp.int32)
    project_full = place(attention_weight, 0, 3, ("z",), project_buffers, scalars)
    mix_full = place_halves(attention_weight[3], mix_near, mix_far, scalars)
    up_full = place(feedforward_weight, 0, 1, ("x",), up_buffers, scalars)[0]

    def down_placed(activated):
        low, high, _ = barrier((down_low[3], down_high[3], activated))
        buffers = [*down_low[:3], low, *down_high[:3], high]
        return place(feedforward_weight, 1, 1, ("z", "x"), buffers, scalars)[0]

    output_full = place_halves(output_table, output_near, output_far, scalars)

    context_far = send(
        after(jnp.where(settled, context_arrived, context_own), output_far), by("y", 2)
    )

    allowed = allowed_mask(window_segments, layout).astype(F32)
    after_block, normed_three, lefts, saved_state = layer_forward(
        residual,
        project_full,
        mix_full,
        up_full,
        down_placed,
        norm_gains,
        allowed,
        (
            (mix_full,),
            (down_low[1], down_high[1], output_near),
            (up_full, down_low[2], down_high[2]),
            (output_far,),
        ),
    )
    heads, totals, mixed_low, after_attention, pre_act, activated, down_full = saved_state
    left_one, left_two, left_three = lefts
    loss_local, grad_logits = head_loss(
        normed_three, output_full, window_tokens, window_segments, keep_flag, spot
    )

    part = contract(grad_logits, output_full, 1, 1)
    other = swap_core(part)
    output_grad = whole_product(left_three, grad_logits)
    output_z = scatter_z(output_grad)
    grad_block, block_low, left_block, norm_three = norm_backward(
        4, norm_gains, after_block, part, after(other, output_grad)
    )
    down_grad = whole_product(left_block, activated)
    down_z = scatter_z(down_grad)
    block_low = after(block_low, down_grad)

    grad_pre, part = feedforward_backward(block_low, down_full, pre_act, up_full)
    other = swap_core(part)
    up_ring = ring_x(spot, left_two, grad_pre, 1024)
    grad_attention, attention_low, left_attention, norm_two = norm_backward(
        2,
        norm_gains,
        after_attention,
        part,
        after(other, up_ring.total),
        grad_block,
    )
    grad_mixed = jnp.dot(attention_low, mix_full, preferred_element_type=F32).astype(BF16)
    grad_projected = attention_backward(heads, allowed, totals, grad_mixed)
    grad_projected, up_one, context_far = barrier((grad_projected, up_ring.arrive(), context_far))
    up_ring.add(up_one)
    grad_projected = after(grad_projected, up_ring.total)
    part = jnp.einsum("ste,sde->td", grad_projected, project_full, preferred_element_type=F32)
    other = swap_core(part)
    project_ring = ring_y(
        spot,
        256,
        (left_one, grad_projected, (1, length, 256), lambda j, half: (j, 0, half), 3),
        (left_attention, mixed_low, (length, 256), lambda j, half: (0, half), 1),
    )
    grad_residual, _, left_residual, norm_one = norm_backward(
        0, norm_gains, residual, part, after(other, project_ring.total), grad_attention
    )

    context_far = context_far + 0.0 * local_seconds
    context = jnp.concatenate([context_near, context_far], axis=1).astype(BF16)

    def columns_of(half):
        side = jnp.where(half == 0, grad_residual[:, : 2 * width], grad_residual[:, 2 * width :])
        return own_quarter(side, core)

    own_grad = jnp.concatenate([columns_of(yh), columns_of(1 - yh)], axis=1)
    own_high = own_grad.astype(BF16)
    own_low = (own_grad - own_high.astype(F32)).astype(BF16)
    hot = (jnp.arange(embed_table.shape[0])[:, None] == window_tokens[None, :]).astype(BF16)
    embed_grad = jnp.dot(hot, own_high, preferred_element_type=F32) + jnp.dot(
        hot, own_low, preferred_element_type=F32
    )
    norms_grad = jnp.concatenate([norm_one, norm_two, norm_three])
    norms_rows = jnp.pad(norms_grad.T, ((0, 0), (0, 122))).reshape(4, 4, 64, 128)

    def condition_part(k, arrived=None):
        left = left_residual.reshape(4, 4, 64, length)
        segments = [
            (left, context, (length, 256), lambda j, s: (0, j), 2),
            (norms_rows, None, None, lambda j, s: (0, 0), 1),
        ]
        return chunk_product(segments, (4, 1, 64, length), 256, k.astype(jnp.int32)[None], arrived)

    condition_ring = Ring("x", spot.x, spot.sign, condition_part)
    condition_ring.total, embed_grad = barrier((condition_ring.total, embed_grad))
    embed_zring = ring_of(spot, "z", embed_grad)
    condition_ring.total, embed_zring.total = barrier((condition_ring.total, embed_zring.total))

    token = condition_ring.total

    def step(ring_here):
        nonlocal token
        arrived, _ = barrier((ring_here.arrive(), token))
        ring_here.add(arrived)
        token = ring_here.total
        return token

    step(up_ring)
    step(condition_ring)
    step(project_ring)
    step(embed_zring)
    up_x = step(up_ring)
    step(condition_ring)
    step(embed_zring)
    down_ring = ring_of(spot, "x", after(jnp.concatenate([down_z, output_z], axis=1), token))
    step(project_ring)
    condition_x = step(condition_ring)
    up_z = scatter_z(jnp.concatenate([up_x, condition_x], axis=1))
    step(down_ring)
    project_y = step(project_ring)
    project_z = scatter_z(project_y)
    embed_z = step(embed_zring)
    step(down_ring)
    embed_ring = ring_of(spot, "x", after(embed_z, token))
    step(down_ring)
    step(embed_ring)
    step(embed_ring)
    step(embed_ring)
    embed_sum = direct_y(spot, embed_ring.total, 64)
    down_x = down_ring.total
    last = direct_y(
        spot,
        jnp.concatenate(
            [
                up_z[:, :1024],
                down_x[:, :1024],
                up_z[:, 2048:2304],
                down_x[:, 2048:2560],
                up_z[:, 2560:2688],
                up_z[:, 1024:2048],
                down_x[:, 1024:2048],
                up_z[:, 2304:2560],
                down_x[:, 2560:],
                up_z[:, 2688:],
            ],
            axis=1,
        ),
        32,
    )
    last_y = direct_sum("x", spot.x, project_z)
    rings = (up_ring, condition_ring, project_ring, down_ring, embed_ring, embed_zring)
    assert all(r.step == 4 for r in rings)
    project_sum, mix_sum = last_y[:, :768], last_y[:, 768:]
    up_sum, down_sum = last[:, :1024], last[:, 1024:2048]
    condition_sum, output_sum = last[:, 2048:2304], last[:, 2304:2816]
    norms_both = last[:, 2816:].reshape(2, 16, 128)
    norms_share = lax.dynamic_index_in_dim(norms_both, core, 0, False)[:, :6].T

    sums = [output_sum, down_sum, up_sum, mix_sum, project_sum, condition_sum, embed_sum]
    squares = 0.5 * jnp.sum((norms_share * SQUARE_SCALE) ** 2)
    for piece in sums:
        squares = squares + jnp.sum((piece * SQUARE_SCALE) ** 2)
    scalars = jnp.stack([0.5 * loss_local, squares, 0.5 * local_seconds])
    flat = [piece.reshape(2, 16, -1) for piece in sums[:-1]] + [sums[-1].reshape(2, 16, 512)]
    flat = jnp.concatenate(flat, axis=2)
    mine = lax.dynamic_index_in_dim(flat, core, 0, False)
    theirs = swap_core(lax.dynamic_index_in_dim(flat, 1 - core, 0, False))
    scalars = pair_sum(jnp.broadcast_to(scalars[:, None], (3, 128)))
    scalars = sum_of_four(scalars, "x", spot.x)
    scalars = sum_of_four(after(scalars, theirs), "z", spot.z)
    scalars = sum_of_four(scalars, "y", spot.y)
    loss_total, seconds_total = scalars[0, 0], scalars[2, 0]
    inverse = 1.0 / seconds_total
    gradient_norm = jnp.sqrt(scalars[1, 0]) * (inverse / SQUARE_SCALE)
    clip_factor = CLIP_NORM / jnp.maximum(gradient_norm, CLIP_NORM)

    low_side = jnp.where(core == 0, mine, theirs)
    high_side = jnp.where(core == 0, theirs, mine)

    def share(start, stop):
        return low_side[:, start:stop], high_side[:, start:stop]

    output_share = jnp.concatenate(share(0, 512), axis=1)
    feedforward_share = jnp.stack(
        [jnp.concatenate(share(1536, 2560), axis=1), jnp.concatenate(share(512, 1536), axis=1)]
    )
    mix_low, mix_high = share(2560, 2816)
    project_low, project_high = share(2816, 3584)
    attention_share = jnp.stack(
        [
            jnp.concatenate(
                [project_low[:, 256 * k : 256 * k + 256], project_high[:, 256 * k : 256 * k + 256]],
                axis=1,
            )
            for k in range(3)
        ]
        + [jnp.concatenate([mix_low, mix_high], axis=1)]
    )
    condition_share = jnp.concatenate(share(3584, 3840), axis=1)
    embed_share = jnp.concatenate([part.reshape(32, 256) for part in share(3840, 4352)], axis=1)

    shares = (
        embed_share,
        condition_share,
        attention_share,
        feedforward_share,
        output_share,
        norms_share,
    )
    masters = (
        embed_master,
        condition_master,
        attention_master,
        feedforward_master,
        output_master,
        norms_master,
    )
    firsts = (
        embed_first,
        condition_first,
        attention_first,
        feedforward_first,
        output_first,
        norms_first,
    )
    seconds_old = (
        embed_second,
        condition_second,
        attention_second,
        feedforward_second,
        output_second,
        norms_second,
    )
    rates = (RATE_TABLE, RATE_MATRIX, RATE_MATRIX, RATE_MATRIX, RATE_MATRIX, RATE_NORMS)
    decays = (WEIGHT_DECAY, WEIGHT_DECAY, WEIGHT_DECAY, WEIGHT_DECAY, WEIGHT_DECAY, 0.0)
    outputs = [loss_total, seconds_total, gradient_norm]
    for slot in range(6):
        outputs += adam_step(
            shares[slot] * inverse * clip_factor,
            masters[slot],
            firsts[slot],
            seconds_old[slot],
            rates[slot],
            decays[slot],
        )
    return tuple(outputs)


def solution(mesh):
    torus = Mesh(mesh.devices.reshape(SIZES), AXES)
    table, slotted = P(DP, "yh"), P(None, DP, "yh")
    state = (table, table, slotted, slotted, table, P(None, DP))
    results = tuple(spec for spec in state for _ in range(3))
    return jax.shard_map(
        local,
        mesh=torus,
        in_specs=(
            P(DP),
            P(DP),
            P(),
            P(DP),
            P(DP),
            table,
            P(None, "yh"),
            P(None, "yh"),
            P(None, None, "yh"),
            P(None, None, "yh"),
            P(None, "yh"),
            P(),
        )
        + state * 3,
        out_specs=(P(), P(), P()) + results,
        check_vma=False,
    )
```
